256 devices in a mesh: az: 64 (over z, x, y_hi), ax: 4 (over y_lo, core).
Axes of the slice: x: 4, y: 4 (y_hi: 2, y_lo: 2; y = y_hi * 2 + y_lo), z: 8, core: 2. Of those that a mesh axis runs over, the one named last changes fastest.
Arguments:
- tangent: float32 [256, 64, 2048], P('az', 'ax'), may hold values from -6 to 6
- velocity: float32 [3, 256, 64, 64], P(None, 'az', 'ax'), may hold values from -0.25 to 0.25
- face_frac: float32 [2, 3, 256, 64, 64], P(None, None, 'az', 'ax'), may hold values from 0.05 to 1
- branch: int32 [2, 3, 256, 64, 64], P(None, None, 'az', 'ax'), may hold values from 0 to 2
- basis: bfloat16 [3, 256, 64, 2048], P(None, 'az', 'ax'), may hold values from -0.5 to 0.5
- design: bfloat16 [32, 32], replicated, may hold values from -5 to 5
- exit_film: float32 [256, 64], P('az'), may hold values from 0.15 to 4.5, as said below
Outputs:
- tangent_out: float32 [256, 64, 2048], P('az', 'ax')
- velocity_tangent: bfloat16 [3, 256, 64, 2048], P(None, 'az', 'ax')
- film: float32 [256, 32], P('az', 'ax')
The draws below stay inside these ranges and needn't reach their ends.
Inputs may be any that keep to these rules, and one draw needn't show every extreme that they name: `branch`: 0 upwind, 1 blended, 2 central. `exit_film`: positive film thickness.
All inputs are finite; a program needn't handle non-finite values.
Results may differ from the reference program's by a relative error of at most 0.0034.
Values sent between devices are 32-bit elements; how exact they have to be, the bound alone decides.
No kernel may reach another device: no remote copies, remote signals or barrier semaphores. Data moves between devices by JAX's collectives and lax.ppermute only.
A program may use at most 128 MiB of HBM per device.

```python
import jax
import jax.numpy as jnp
from jax import lax

NR = 64
DIRS = 32
PARAMS = 32
STEPS = 2
NA = 256
NX = 64


def draw_exit_film(key, part):
    key = jax.random.fold_in(key, 7)
    rough = jax.random.uniform(key, (NA, NR), jnp.float32, 0.3, 1.0)
    place = (jnp.arange(NA).astype(jnp.float32) + 0.5) / NA
    rise = 1.0 + 2.0 * place
    return rough * rise[:, None]


def plant(entries, key, low, largest):
    index_at = [jax.random.randint(jax.random.fold_in(key, axis), (), 0, length) for axis, length in enumerate(entries.shape)]
    widest = entries.shape.index(max(entries.shape))
    neighbour = index_at[:widest] + [(index_at[widest] + 1) % entries.shape[widest]] + index_at[widest + 1:]
    return entries.at[tuple(index_at)].set(low).at[tuple(neighbour)].set(largest)


def block_scale(rng, extent, shards, low, largest):
    factor_of, own = 1.0, jax.random.fold_in(rng, 6)
    for position, blocks in shards:
        draws = jnp.exp(jax.random.uniform(jax.random.fold_in(own, position), (blocks,), jnp.float32, low / len(shards), largest / len(shards)))
        factor_of = factor_of * jnp.repeat(draws, extent[position] // blocks).reshape([-1 if axis == position else 1 for axis in range(len(extent))])
    return factor_of


def gaussian(rng, shape, scale, bound, pieces=(), dtype=jnp.bfloat16):
    result = jax.random.normal(rng, shape, jnp.float32) * scale
    if len(pieces) > 0:
        result = block_scale(rng, shape, pieces, -0.22, 0.18) * result
    return jnp.clip(result, min=-bound, max=bound).astype(dtype)


def setup_inputs(seed: int = 0) -> dict:
    streams_of = jax.random.split(jax.random.key(seed), 8)
    return {
        "tangent": gaussian(streams_of[0], (NA, NX, NR * DIRS), 1.0, 6.0, ((0, 64), (1, 4)), jnp.float32),
        "velocity": jnp.clip(jax.random.uniform(streams_of[1], (3, NA, NX, NR), jnp.float32, -0.25, 0.25) * block_scale(streams_of[1], (3, NA, NX, NR), ((1, 64), (2, 4)), -0.4, 0.0), -0.25, 0.25),
        "face_frac": jnp.clip(0.05 + 0.95 * jax.random.uniform(streams_of[2], (STEPS, 3, NA, NX, NR), jnp.float32) ** block_scale(streams_of[2], (STEPS, 3, NA, NX, NR), ((2, 64), (3, 4)), -0.2, 0.2), 0.05, 1.0),
        "branch": plant(jax.random.randint(streams_of[3], (STEPS, 3, NA, NX, NR), 0, 3), jax.random.fold_in(streams_of[3], 1), 0, 2).astype(jnp.int32),
        "basis": gaussian(streams_of[4], (3, NA, NX, NR * PARAMS), (4 * PARAMS) ** -0.5, 0.5, ((1, 64), (2, 4))),
        "design": gaussian(streams_of[5], (PARAMS, DIRS), 1.0, 5.0),
        "exit_film": draw_exit_film(jax.random.fold_in(streams_of[7], 71), 0),
    }


def face_flux(here, there, speed, frac, coef, dspeed):
    upwind = jnp.where(speed > 0, here, there)
    downwind = jnp.where(speed > 0, there, here)
    return dspeed * frac + speed * (upwind + coef * (downwind - upwind))


def spread(values):
    return jnp.repeat(values, DIRS, axis=-1)


def next_along(field, axis, wrap):
    rolled = jnp.roll(field, -1, axis)
    if wrap:
        return rolled
    place = lax.broadcasted_iota(jnp.int32, field.shape, axis)
    return jnp.where(place < field.shape[axis] - 1, rolled, jnp.zeros_like(rolled))


def prev_along(field, axis, wrap):
    rolled = jnp.roll(field, 1, axis)
    if wrap:
        return rolled
    place = lax.broadcasted_iota(jnp.int32, field.shape, axis)
    return jnp.where(place > 0, rolled, jnp.zeros_like(rolled))


def reference(tangent, velocity, face_frac, branch, basis, design, exit_film):
    comps = []
    for comp in range(3):
        block = basis[comp].reshape(NA, NX, NR, PARAMS).astype(jnp.float32)
        prod = jnp.einsum("axrp,pd->axrd", block, design.astype(jnp.float32))
        comps.append(prod.astype(jnp.bfloat16).reshape(NA, NX, NR * DIRS))
    velocity_tangent = jnp.stack(comps, 0)
    wall = spread((jnp.arange(NR) < NR - 1).astype(jnp.float32))
    field = tangent
    exit_sum = jnp.zeros((NA, NR * DIRS), jnp.float32)
    for step in range(STEPS):
        upper = face_flux(field, next_along(field, 0, True), spread(velocity[0]), spread(face_frac[step, 0]),
                          spread(0.25 * branch[step, 0].astype(jnp.float32)), velocity_tangent[0].astype(jnp.float32))
        change = upper - prev_along(upper, 0, True)
        upper = face_flux(field, next_along(field, 1, False), spread(velocity[1]), spread(face_frac[step, 1]),
                          spread(0.25 * branch[step, 1].astype(jnp.float32)), velocity_tangent[1].astype(jnp.float32))
        exit_sum = exit_sum + upper[:, NX - 1, :]
        change = change + (upper - prev_along(upper, 1, False))
        radial_next = jnp.concatenate([field[..., DIRS:], jnp.zeros((NA, NX, DIRS), jnp.float32)], -1)
        upper = face_flux(field, radial_next, spread(velocity[2]), spread(face_frac[step, 2]),
                          spread(0.25 * branch[step, 2].astype(jnp.float32)), velocity_tangent[2].astype(jnp.float32)) * wall
        radial_prev = jnp.concatenate([jnp.zeros((NA, NX, DIRS), jnp.float32), upper[..., :-DIRS]], -1)
        change = change + (upper - radial_prev)
        field = field - change
    weights = (jnp.arange(NR).astype(jnp.float32) + 0.5) / NR
    raw = jnp.sum(exit_sum.reshape(NA, NR, DIRS) * weights[None, :, None], axis=1)
    row_film = jnp.sum(exit_film * weights[None, :], axis=1)
    mean_film = jnp.sum(row_film) / NA
    film = raw * (mean_film / row_film)[:, None]
    return field, velocity_tangent, film
```

```python
import jax
import jax.numpy as jnp
from jax import lax
from jax.experimental import pallas as pl
from jax.experimental.pallas import tpu as pltpu
from jax.sharding import PartitionSpec as P

F32, BF16 = jnp.float32, jnp.bfloat16
CHUNK = 256
RADIAL = 64
CELLS = 4
UNROLL = 8
AT_C1, AT_B2, AT_C2, AT_ROW_A, AT_ROW_B, AT_COEF, AT_FIRST, AT_END = 0, 256, 512, 768, 1024, 1280, 1408, 1664


def mix(speed, branch):
    part = speed * (0.25 * branch.astype(F32))
    rest = speed - part
    ahead = speed > 0
    return jnp.where(ahead, rest, part), jnp.where(ahead, part, rest)


def two_terms(values):
    high = values.astype(BF16)
    low = (values - high.astype(F32)).astype(BF16)
    return jnp.concatenate([high, low], axis=-1)


def spreader(offset, lanes, radial, dirs):
    row = lax.broadcasted_iota(jnp.int32, (2 * radial, lanes), 0)
    lane = lax.broadcasted_iota(jnp.int32, (2 * radial, lanes), 1) + offset
    shift = dirs.bit_length() - 1
    return jnp.where((row & (radial - 1)) == (lane >> shift), 1.0, 0.0).astype(BF16)


def spread_all(packed, outs, radial, dirs):
    lanes = outs[0].shape[1]

    @pl.loop(0, lanes // CHUNK, unroll=UNROLL)
    def _(k):
        at = pl.multiple_of(k * CHUNK, CHUNK)
        ones = spreader(at, CHUNK, radial, dirs)
        row = 0
        for out in outs:
            count = out.shape[0]
            left = packed[pl.ds(row, count), :]
            out[:, pl.ds(at, CHUNK)] = jnp.dot(left, ones, preferred_element_type=F32)
            row += count


def blocks_of(design):
    dirs = design.shape[1]
    row = lax.broadcasted_iota(jnp.int32, (CHUNK, dirs), 0)
    col = lax.broadcasted_iota(jnp.int32, (CHUNK, dirs), 1)
    pick = jnp.where((row & (dirs - 1)) == col, 1.0, 0.0).astype(BF16)
    tiled = jnp.dot(pick, design, preferred_element_type=F32).astype(BF16)
    tiled = lax.dot_general(tiled, pick, (((1,), (1,)), ((), ())), preferred_element_type=F32)
    row = lax.broadcasted_iota(jnp.int32, (CHUNK, CHUNK), 0)
    col = lax.broadcasted_iota(jnp.int32, (CHUNK, CHUNK), 1)
    shift = dirs.bit_length() - 1
    return jnp.where((row >> shift) == (col >> shift), tiled, 0.0).astype(BF16)


def wall(radial):
    lane = lax.broadcasted_iota(jnp.int32, (1, radial), 1)
    return jnp.where(lane < radial - 1, 1.0, 0.0)


def ahead_x(rows, last):
    n = rows.shape[0]
    at = lax.broadcasted_iota(jnp.int32, rows.shape, 0)
    return jnp.where(at == n - 1, last, pltpu.roll(rows, n - 1, 0))


def behind_x(rows, first):
    at = lax.broadcasted_iota(jnp.int32, rows.shape, 0)
    return jnp.where(at == 0, first, pltpu.roll(rows, 1, 0))


def ahead_r(rows, dirs):
    return pltpu.roll(rows, rows.shape[1] - dirs, 1)


def behind_r(rows, dirs):
    return pltpu.roll(rows, dirs, 1)


def even_az():
    return lax.rem(lax.axis_index("az"), 2) == 0


def radial_weights(radial):
    return (lax.broadcasted_iota(jnp.int32, (1, radial), 1).astype(F32) + 0.5) / radial


EDGE = ((0, 0), (0, 2), (0, 3), (1, 0), (1, 3), (2, 0), (2, 3))


def edge_kernel(
    tangent, velocity, frac, branch, basis, design, exit_film,
    msg_e, msg_o, sums,
    field, vel, share, share_2, kind, kind_2, left, mat, film, vel_tan, packed, spread, work, ends, edge, faces, face_a, sems,
):
    cells, rows, lanes = field.shape
    radial = vel.shape[-1]
    dirs = lanes // radial
    last, end = cells - 1, rows - 1
    inner = wall(radial)
    pairs = [
        (exit_film, film), (velocity, vel), (branch.at[0], kind), (frac.at[0], share), (frac.at[1, 0, last], share_2),
        (branch.at[1, 0, last], kind_2), (design, mat), (tangent, field),
    ]
    copies = [pltpu.make_async_copy(src, dst, sems.at[i]) for i, (src, dst) in enumerate(pairs)]
    base = len(copies)
    copies += [
        pltpu.make_async_copy(basis.at[c, a], left.at[pl.ds(i * rows, rows)], sems.at[base + i])
        for i, (c, a) in enumerate(EDGE)
    ]
    for copy in copies:
        copy.start()
    copies[0].wait()
    sums[...] = jnp.full(sums.shape, jnp.sum(film[...] * radial_weights(radial)), F32)
    for copy in copies[1:6]:
        copy.wait()

    at = {}
    row = 0
    for c, a in EDGE:
        low, high = mix(vel[c, a], kind[c, a])
        if (c, a) == (0, last):
            high_a = high
        if c == 1:
            at["high", a] = high
        for name, part in zip("plh", (share[c, a], low, high), strict=True):
            packed[pl.ds(row, rows), :] = two_terms(part * inner if c == 2 else part)
            at[name, c, a] = row
            row += rows
    low_2, high_2 = mix(vel[0, last], kind_2[...])
    for name, part in zip("pl", (share_2[...], low_2), strict=True):
        packed[pl.ds(row, rows), :] = two_terms(part)
        at[name] = row
        row += rows
    spread_all(packed, [spread], radial, dirs)

    for copy in copies[6:]:
        copy.wait()
    weights = blocks_of(mat[...])

    @pl.loop(0, lanes // CHUNK, unroll=UNROLL)
    def _(k):
        lane = pl.ds(pl.multiple_of(k * CHUNK, CHUNK), CHUNK)
        vel_tan[:, lane] = jnp.dot(left[:, lane], weights, preferred_element_type=F32).astype(BF16)

    def sp(*key):
        return spread[pl.ds(at[key], rows), :]

    def speed(c, a):
        return vel_tan[pl.ds(EDGE.index((c, a)) * rows, rows), :].astype(F32)

    def along_az(a):
        f = field[a]
        face = speed(0, a) * sp("p", 0, a) + sp("l", 0, a) * f
        return face if a == last else face + sp("h", 0, a) * field[a + 1]

    faces[0] = along_az(0)
    faces[1] = along_az(last - 1)
    face_a[...] = along_az(last)
    for i, a in enumerate((0, last)):
        f = field[a]
        change = faces[0] if a == 0 else face_a[...] - faces[1]
        face = speed(1, a) * sp("p", 1, a) + sp("l", 1, a) * f + sp("h", 1, a) * ahead_x(f, 0.0)
        ends[pl.ds(i, 1), :] = face[end:, :]
        change = change + (face - behind_x(face, 0.0))
        face = speed(2, a) * sp("p", 2, a) + sp("l", 2, a) * f + sp("h", 2, a) * ahead_r(f, dirs)
        change = change + (face - behind_r(face, dirs))
        edge[i] = f - change
    work[...] = speed(0, last) * spread[pl.ds(at["p"], rows), :] + spread[pl.ds(at["l"], rows), :] * edge[1]

    def small_rows(msg, lane, block):
        for k in range(lanes // CHUNK):
            msg[pl.ds(2 * rows + k, 1), pl.ds(lane, CHUNK)] = block[:, k * CHUNK:(k + 1) * CHUNK]

    def halves(msg, lane, block):
        for k in range(rows // 8):
            msg[pl.ds(2 * rows, 8), pl.ds(lane + 128 * k, radial)] = block[8 * k:8 * k + 8]

    def fill(up_msg, down_msg):
        for msg in (up_msg, down_msg):
            msg[pl.ds(2 * rows, 8), :] = jnp.zeros((8, lanes), F32)
        up_msg[pl.ds(0, rows), :] = face_a[...]
        up_msg[pl.ds(rows, rows), :] = work[...]
        halves(up_msg, AT_C1, high_a)
        halves(up_msg, AT_B2, low_2)
        halves(up_msg, AT_C2, high_2)
        small_rows(up_msg, AT_ROW_A, ends[pl.ds(1, 1), :])
        small_rows(up_msg, AT_ROW_B, field[last, pl.ds(0, 1), :])
        small_rows(up_msg, AT_FIRST, sp("h", 0, last)[0:1])
        small_rows(up_msg, AT_END, sp("h", 0, last)[end:])
        up_msg[pl.ds(2 * rows, 1), pl.ds(AT_COEF, radial)] = at["high", last][end:, :]
        down_msg[pl.ds(0, rows), :] = field[0]
        down_msg[pl.ds(rows, rows), :] = edge[0]
        small_rows(down_msg, AT_ROW_A, ends[pl.ds(0, 1), :])
        down_msg[pl.ds(2 * rows, 1), pl.ds(AT_COEF, radial)] = at["high", 0][end:, :]

    even = even_az()

    @pl.when(even)
    def _():
        fill(msg_e, msg_o)

    @pl.when(jnp.logical_not(even))
    def _():
        fill(msg_o, msg_e)


MIDDLE = dict(
    ends=0, end_fixed=4, low_end=8, first=12, partial_first=16, partial_end=20, front=24, coef_a=26, coefs=28
)


def local_kernel(
    tangent, velocity, frac, branch, basis, design, exit_film,
    vel_tan, coef_2, middle, partial, fixed, edges,
    field, vel, share, kind, left, mat, film, product, packed, spread, mixed, sems,
):
    cells, rows, lanes = field.shape
    radial = vel.shape[-1]
    dirs = lanes // radial
    n = cells * rows
    last, end = cells - 1, rows - 1
    inner = wall(radial)
    pairs = [
        (velocity, vel), (branch, kind), (frac, share), (design, mat), (basis, left), (tangent, field), (exit_film, film),
    ]
    copies = [pltpu.make_async_copy(src, dst, sems.at[i]) for i, (src, dst) in enumerate(pairs)]
    for copy in copies:
        copy.start()
    for copy in copies[:3]:
        copy.wait()

    for step in range(2):
        for c in range(3):
            low, high = mix(vel[c], kind[step, c])
            for k, part in enumerate((share[step, c], low, high)):
                part = part.reshape(n, radial)
                part = two_terms(part * inner if c == 2 else part)
                if step == 0 or k == 0:
                    packed[pl.ds(((step * 3 + k) * 3 + c) * n, n), :] = part
                else:
                    for a in range(cells):
                        row = 12 * n + ((a * 2 + k - 1) * 3 + c) * rows
                        packed[pl.ds(row, rows), :] = part[a * rows:(a + 1) * rows]
            if c == 1:
                segments = [(0, high)] if step == 0 else [(6, low), (10, high)]
                if step == 0:
                    middle[pl.ds(MIDDLE["coefs"], 1), :] = jnp.zeros((1, lanes), F32)
                for start, part in segments:
                    for a in range(cells):
                        middle[pl.ds(MIDDLE["coefs"], 1), pl.ds(128 * (start + a), radial)] = part[a, end:, :]
    spread_all(packed, [spread, mixed], radial, dirs)
    done = [pltpu.make_async_copy(mixed, coef_2, sems.at[len(copies) + 1])]
    done[0].start()
    for copy in copies[3:5]:
        copy.wait()
    weights = blocks_of(mat[...])

    @pl.loop(0, lanes // CHUNK, unroll=UNROLL)
    def _(k):
        lane = pl.ds(pl.multiple_of(k * CHUNK, CHUNK), CHUNK)
        block = jnp.dot(left[:, :, :, lane].reshape(3 * n, CHUNK), weights, preferred_element_type=F32)
        product[:, :, :, lane] = block.astype(BF16).reshape(3, cells, rows, CHUNK)

    done.append(pltpu.make_async_copy(product, vel_tan, sems.at[len(copies)]))
    done[-1].start()
    for copy in copies[5:]:
        copy.wait()

    def sp(k, c, a):
        return spread[pl.ds((k * 3 + c) * n + a * rows, rows), :]

    def speed(c, a):
        return product[c, a].astype(F32)

    def put(name, a, block):
        middle[pl.ds(MIDDLE[name] + a, block.shape[0]), :] = block

    before = before_2 = None
    for a in range(cells):
        f = field[a]
        here = speed(0, a) * sp(0, 0, a) + sp(1, 0, a) * f
        if a < last:
            here = here + sp(2, 0, a) * field[a + 1]
        change = here if before is None else here - before
        before = here
        face = speed(1, a) * sp(0, 1, a) + sp(1, 1, a) * f + sp(2, 1, a) * ahead_x(f, 0.0)
        put("ends", a, face[end:])
        edges[pl.ds(2 * rows + a, 1), :] = face[end:]
        change = change + (face - behind_x(face, 0.0))
        face = speed(2, a) * sp(0, 2, a) + sp(1, 2, a) * f + sp(2, 2, a) * ahead_r(f, dirs)
        change = change + (face - behind_r(face, dirs))
        block = f - change
        partial[a] = block
        put("first", a, f[0:1])
        edges[pl.ds(2 * rows + 4 + a, 1), :] = f[0:1]
        put("partial_first", a, block[0:1])
        put("partial_end", a, block[end:])
        put("low_end", a, mixed[pl.ds((a * 6 + 1) * rows + end, 1), :])
        edges[pl.ds(2 * rows + 8 + a, 1), :] = sp(2, 1, a)[end:]
        here_2 = speed(0, a) * sp(3, 0, a)
        change = here_2 if before_2 is None else here_2 - before_2
        before_2 = here_2
        face = speed(1, a) * sp(3, 1, a)
        put("end_fixed", a, face[end:])
        change = change + (face - behind_x(face, 0.0))
        face = speed(2, a) * sp(3, 2, a)
        fixed[a] = change + (face - behind_r(face, dirs))
    edges[pl.ds(0, rows), :] = before
    edges[pl.ds(2 * rows + 16, rows), :] = field[0]
    edges[pl.ds(rows, rows), :] = sp(2, 0, last)
    for k, x in enumerate((0, end)):
        put("front", k, field[0, pl.ds(x, 1), :])
        put("coef_a", k, sp(2, 0, last)[x:x + 1])
    row_film = jnp.sum(film[...] * radial_weights(radial), axis=1, keepdims=True)
    edges[pl.ds(2 * rows + 12, cells), :] = jnp.broadcast_to(row_film, (cells, lanes))
    for copy in done:
        copy.wait()


def gathered_row(msg, row, lane, lanes):
    return jnp.concatenate([msg[pl.ds(row + k, 1), pl.ds(lane, CHUNK)] for k in range(lanes // CHUNK)], axis=1)


def middle_kernel(
    middle, in_e, in_o, totals,
    msg_e, msg_o, film_msg,
):
    cells, rows, lanes = CELLS, (in_e.shape[0] - 8) // 2, in_e.shape[1]
    radial, dirs = RADIAL, lanes // RADIAL
    last, end = cells - 1, rows - 1

    def take(name, count=CELLS, at=0):
        return middle[pl.ds(MIDDLE[name] + at, count), :]

    even = even_az()

    def work(up, down, out_up, out_down):
        at_a = lax.broadcasted_iota(jnp.int32, (cells, 1), 0)
        partial_x = []
        for k, (x, lane, name) in enumerate(((0, AT_FIRST, "partial_first"), (end, AT_END, "partial_end"))):
            face = up[pl.ds(x, 1), :] + gathered_row(up, 2 * rows, lane, lanes) * take("front", 1, k)
            beyond = take("coef_a", 1, k) * down[pl.ds(x, 1), :]
            partial_x.append(take(name) + jnp.where(at_a == 0, face, 0.0) - jnp.where(at_a == last, beyond, 0.0))
        second = take("end_fixed") + take("low_end") * partial_x[1]

        lane = lax.broadcasted_iota(jnp.int32, (1, lanes), 1)
        weight = ((lane // dirs).astype(F32) + 0.5) / radial
        raw = (take("ends") + second) * weight
        film = raw[:, 0:128]
        for k in range(1, lanes // 128):
            film = film + raw[:, 128 * k:128 * k + 128]
        shift = 64
        while shift >= dirs:
            film = film + pltpu.roll(film, shift, 1)
            shift //= 2
        quarter = jnp.sum(totals[...], axis=0)
        film_msg[...] = jnp.zeros(film_msg.shape, F32)
        film_msg[pl.ds(0, cells), :] = film
        film_msg[pl.ds(cells, 1), :] = quarter

        def finish(up_msg, down_msg):
            for msg in (up_msg, down_msg):
                msg[1, pl.ds(2, 2), :] = jnp.zeros((2, lanes), F32)
                for a in range(cells):
                    msg[1, pl.ds(3, 1), pl.ds(128 * a, 128)] = film[a:a + 1]
                msg[1, pl.ds(3, 1), pl.ds(128 * cells, 128)] = quarter
            up_msg[0] = take("ends")
            up_msg[1, pl.ds(0, 1), :] = gathered_row(up, 2 * rows, AT_ROW_A, lanes)
            up_msg[1, pl.ds(1, 1), :] = gathered_row(down, 2 * rows, AT_ROW_A, lanes)
            up_msg[1, pl.ds(2, 1), :] = take("coefs", 1)
            up_msg[1, pl.ds(2, 1), pl.ds(128 * 4, radial)] = up[pl.ds(2 * rows, 1), pl.ds(AT_COEF, radial)]
            up_msg[1, pl.ds(2, 1), pl.ds(128 * 5, radial)] = down[pl.ds(2 * rows, 1), pl.ds(AT_COEF, radial)]
            up_msg[2] = second
            down_msg[0] = take("first")
            down_msg[1, pl.ds(0, 1), :] = gathered_row(up, 2 * rows, AT_ROW_B, lanes)
            down_msg[1, pl.ds(1, 1), :] = down[pl.ds(0, 1), :]
            down_msg[2] = partial_x[0]

        even_x = lax.rem(lax.axis_index("ax"), 2) == 0

        @pl.when(even_x)
        def _():
            finish(out_up, out_down)

        @pl.when(jnp.logical_not(even_x))
        def _():
            finish(out_down, out_up)

    @pl.when(even)
    def _():
        work(in_o, in_e, msg_e, msg_o)

    @pl.when(jnp.logical_not(even))
    def _():
        work(in_e, in_o, msg_e, msg_o)


def last_kernel(
    coef_2, partial, fixed, edges, in_e, in_o, x_e, x_o, film_own, film_1,
    out, film_out,
    packed, spread, up, down, below, above, now, edge, result, mixed, sems,
):
    cells, rows, lanes = partial.shape
    radial = packed.shape[1] // 2
    dirs = lanes // radial
    n = cells * rows
    last, end = cells - 1, rows - 1
    even = even_az()
    place = lax.axis_index("ax")
    even_x = lax.rem(place, 2) == 0
    final = lax.axis_size("ax") - 1
    layer = 6 * rows
    loads = [
        pltpu.make_async_copy(coef_2.at[pl.ds(a * layer, layer)], mixed.at[pl.ds(a * layer, layer)], sems.at[cells + a])
        for a in range(cells)
    ]
    for copy in loads:
        copy.start()

    @pl.when(even)
    def _():
        up[...] = in_o[...]
        down[...] = in_e[...]

    @pl.when(jnp.logical_not(even))
    def _():
        up[...] = in_e[...]
        down[...] = in_o[...]

    @pl.when(even_x)
    def _():
        below[...] = jnp.where(place == 0, 0.0, x_o[...])
        above[...] = x_e[...]

    @pl.when(jnp.logical_not(even_x))
    def _():
        below[...] = x_e[...]
        above[...] = jnp.where(place == final, 0.0, x_o[...])

    face_a, coef_a = edges[pl.ds(0, rows), :], edges[pl.ds(rows, rows), :]
    ends, first, coef_x = (edges[pl.ds(2 * rows + 4 * k, cells), :] for k in range(3))

    def joined(msg, lane):
        return jnp.concatenate([msg[pl.ds(2 * rows, 8), pl.ds(lane + 128 * k, radial)] for k in range(rows // 8)], axis=0)

    for k, lane in enumerate((AT_C1, AT_B2, AT_C2)):
        packed[pl.ds(k * rows, rows), :] = two_terms(joined(up, lane))
    singles = [below[1, pl.ds(2, 1), pl.ds(128 * k, radial)] for k in range(14)]
    singles += [msg[pl.ds(2 * rows, 1), pl.ds(AT_COEF, radial)] for msg in (up, down)]
    packed[pl.ds(3 * rows, 16), :] = two_terms(jnp.concatenate(singles, axis=0))
    spread_all(packed, [spread], radial, dirs)
    in_c1, in_b2, in_c2 = (spread[pl.ds(k * rows, rows), :] for k in range(3))
    below_c = spread[pl.ds(3 * rows, 6), :]
    below_b2, below_c2 = spread[pl.ds(3 * rows + 6, 4), :], spread[pl.ds(3 * rows + 10, 4), :]
    own_c = jnp.concatenate([coef_x, spread[pl.ds(3 * rows + 14, 2), :]], axis=0)

    starts = jnp.concatenate([first, gathered_row(up, 2 * rows, AT_ROW_B, lanes), down[pl.ds(0, 1), :]], axis=0)
    enter = jnp.concatenate([below[0], below[1, pl.ds(0, 2), :]], axis=0) + below_c * starts
    leave = own_c * jnp.concatenate([above[0], above[1, pl.ds(0, 2), :]], axis=0)
    crossing = in_c1 * edges[pl.ds(2 * rows + 16, rows), :]
    beyond = coef_a * down[pl.ds(0, rows), :]
    at_x = lax.broadcasted_iota(jnp.int32, (rows, 1), 0)

    def with_edges(block, k):
        return block + jnp.where(at_x == 0, enter[k:k + 1], 0.0) - jnp.where(at_x == end, leave[k:k + 1], 0.0)

    for a in range(cells):
        f = partial[a]
        if a == 0:
            f = f + up[pl.ds(0, rows), :] + crossing
        if a == last:
            f = f - beyond
        now[a] = with_edges(f, a)
    now[cells] = with_edges(down[pl.ds(rows, rows), :] + face_a + beyond, 5)
    lower = up[pl.ds(rows, rows), :] + in_b2 * (
        jnp.where(at_x == 0, enter[4:5], 0.0) - jnp.where(at_x == end, leave[4:5], 0.0) - crossing
    )
    before = lower + in_c2 * now[0]

    first_now = jnp.concatenate([now[a, pl.ds(0, 1), :] for a in range(cells)], axis=0)
    enter_2 = below[2] - below_b2 * (below_c[0:4] * first) + below_c2 * first_now
    inside = jnp.where(place == final, 0.0, 1.0)
    edge[...] = inside * (above[2] + ends + leave[0:4])

    def low(c, a):
        return mixed[pl.ds((a * 6 + c) * rows, rows), :]

    def high(c, a):
        return mixed[pl.ds((a * 6 + 3 + c) * rows, rows), :]

    copies = []
    for a in range(cells):
        loads[a].wait()
        f = now[a]
        face = low(0, a) * f + high(0, a) * now[a + 1]
        change = fixed[a] + (face - before)
        before = face
        face = low(1, a) * f + high(1, a) * ahead_x(f, edge[pl.ds(a, 1), :])
        change = change + (face - behind_x(face, enter_2[a:a + 1]))
        face = low(2, a) * f + high(2, a) * ahead_r(f, dirs)
        change = change + (face - behind_r(face, dirs))
        result[a] = f - change
        copies.append(pltpu.make_async_copy(result.at[a], out.at[a], sems.at[a]))
        copies[a].start()

    share = film_out.shape[1]
    total = film_own[pl.ds(cells, 1), :] + film_1[pl.ds(cells, 1), :]
    for msg in (x_e, x_o):
        total = total + msg[1, pl.ds(3, 1), pl.ds(128 * cells, 128)]
    mean = total / (cells * lax.axis_size("az"))
    factor = mean / edges[pl.ds(2 * rows + 12, cells), pl.ds(0, 128)]
    for k, source in enumerate((x_o, film_1, x_e, film_own)):

        @pl.when(place == k)
        def _():
            if len(source.shape) == 2:
                film = source[pl.ds(0, cells), :]
            else:
                film = jnp.concatenate([source[1, pl.ds(3, 1), pl.ds(128 * a, 128)] for a in range(cells)], axis=0)
            film_out[...] = (film * factor)[:, k * share:(k + 1) * share]

    for copy in copies:
        copy.wait()


def swap(value, axis, pairing):
    count = lax.axis_size(axis)
    if axis == "ax":
        other = [i ^ pairing for i in range(count)]
    elif pairing == 0:
        other = [i ^ 1 for i in range(count)]
    else:
        other = [(i - 1 if i % 2 == 0 else i + 1) % count for i in range(count)]
    return lax.ppermute(value, axis, list(enumerate(other)))


def quarter_sums(value):
    count, quarters = lax.axis_size("az"), lax.axis_size("ax")
    part = count // quarters
    pairs = [
        ((i + part * j) % count * quarters + j, i * quarters + j) for i in range(count) for j in range(quarters)
    ]
    value = lax.ppermute(value, ("az", "ax"), pairs)
    groups = [list(range(part * k, part * (k + 1))) for k in range(quarters)]
    return lax.all_to_all(value, "az", 0, 0, axis_index_groups=groups)


def pinned(value, space):
    return pltpu.with_memory_space_constraint(value, space)


def placed(space, shape, dtype):
    return space(shape, dtype)


def call(kernel, args, outs, scratch, in_hbm=0, out_hbm=0, free=0, sems=0, cost=None):
    vmem, hbm = pl.BlockSpec(memory_space=pltpu.VMEM), pl.BlockSpec(memory_space=pl.ANY)
    shapes = [pltpu.VMEM(shape, dtype) for shape, dtype in scratch]
    pinned_outs = len(outs) - free
    shapes_out = [placed(pltpu.HBM if i < out_hbm else pltpu.VMEM, *out) for i, out in enumerate(outs[:pinned_outs])]
    shapes_out += [jax.ShapeDtypeStruct(*out) for out in outs[pinned_outs:]]
    args = [pinned(arg, pltpu.HBM if i < in_hbm else pltpu.VMEM) for i, arg in enumerate(args)]
    if sems:
        shapes.append(pltpu.SemaphoreType.DMA((sems,)))
    return pl.pallas_call(
        kernel,
        out_shape=shapes_out,
        in_specs=[hbm] * in_hbm + [vmem] * (len(args) - in_hbm),
        out_specs=[hbm] * out_hbm + [vmem] * (len(outs) - out_hbm),
        scratch_shapes=shapes,
        compiler_params=pltpu.CompilerParams(vmem_limit_bytes=32 * 2**20),
        cost_estimate=cost,
        name=kernel.__name__,
    )(*args)


def local(tangent, velocity, face_frac, branch, basis, design, exit_film):
    cells, rows, lanes = tangent.shape
    radial = velocity.shape[-1]
    dirs = design.shape[1]
    n = cells * rows
    devices = lax.axis_size("az")
    layer, cell_layer = (rows, lanes), (rows, radial)
    z_msg, x_msg, line = (2 * rows + 8, lanes), (3, cells, lanes), (cells, lanes)
    inputs = (tangent, velocity, face_frac, branch, basis, design, exit_film)
    count = (3 * len(EDGE) + 2) * rows
    z_e, z_o, sums = call(
        edge_kernel,
        inputs,
        [(z_msg, F32), (z_msg, F32), ((devices // lax.axis_size("ax"), 1, 128), F32)],
        [
            (tangent.shape, F32), (velocity.shape, F32), (velocity.shape, F32), (cell_layer, F32),
            (velocity.shape, branch.dtype), (cell_layer, branch.dtype), ((len(EDGE) * rows, lanes), BF16),
            (design.shape, BF16), (exit_film.shape, F32), ((len(EDGE) * rows, lanes), BF16),
            ((count, 2 * radial), BF16), ((count, lanes), F32), (layer, F32), ((2, lanes), F32),
            ((2, *layer), F32), ((2, *layer), F32), (layer, F32),
        ],
        in_hbm=7,
        sems=8 + len(EDGE),
    )
    in_e, in_o = swap(z_e, "az", 0), swap(z_o, "az", 1)
    totals = quarter_sums(sums)
    velocity_tangent, coef_2, middle, partial, fixed, edges = call(
        local_kernel,
        inputs,
        [
            (basis.shape, BF16), ((6 * n, lanes), F32), ((32, lanes), F32), (tangent.shape, F32), (tangent.shape, F32),
            ((3 * rows + 16, lanes), F32),
        ],
        [
            (tangent.shape, F32), (velocity.shape, F32), (face_frac.shape, F32), (branch.shape, branch.dtype),
            (basis.shape, BF16), (design.shape, BF16), (exit_film.shape, F32), (basis.shape, BF16),
            ((18 * n, 2 * radial), BF16), ((12 * n, lanes), F32), ((6 * n, lanes), F32),
        ],
        in_hbm=7,
        out_hbm=2,
        sems=9,
        cost=pl.CostEstimate(flops=10**9, bytes_accessed=16 * 10**6, transcendentals=0),
    )
    x_e, x_o, film = call(
        middle_kernel, (middle, in_e, in_o, totals), [(x_msg, F32), (x_msg, F32), ((8, 128), F32)], []
    )
    from_o, from_e, film_1 = swap(x_o, "ax", 3), swap(x_e, "ax", 1), swap(film, "ax", 2)
    count = 3 * rows + 16
    out, film_out = call(
        last_kernel,
        (coef_2, partial, fixed, edges, in_e, in_o, from_e, from_o, film, film_1),
        [(tangent.shape, F32), ((cells, dirs // lax.axis_size("ax")), F32)],
        [
            ((count, 2 * radial), BF16), ((count, lanes), F32), (z_msg, F32), (z_msg, F32), (x_msg, F32), (x_msg, F32),
            ((cells + 1, *layer), F32), (line, F32), (tangent.shape, F32), ((6 * n, lanes), F32),
        ],
        in_hbm=1,
        out_hbm=1,
        free=1,
        sems=2 * cells,
    )
    return out, velocity_tangent, film_out


def solution(mesh):
    in_specs = (
        P("az", "ax", None),
        P(None, "az", "ax", None),
        P(None, None, "az", "ax", None),
        P(None, None, "az", "ax", None),
        P(None, "az", "ax", None),
        P(),
        P("az", None),
    )
    out_specs = (P("az", "ax", None), P(None, "az", "ax", None), P("az", "ax"))
    return jax.shard_map(local, mesh=mesh, in_specs=in_specs, out_specs=out_specs, check_vma=False)
```

```python
import jax
import jax.numpy as jnp
from jax import lax
from jax.experimental import pallas as pl
from jax.experimental.pallas import tpu as pltpu
from jax.sharding import PartitionSpec as P

F32, BF16 = jnp.float32, jnp.bfloat16
CHUNK = 256
RADIAL = 64
CELLS = 4
UNROLL = 8
AT_C1, AT_B2, AT_C2, AT_ROW_A, AT_ROW_B, AT_COEF, AT_FIRST, AT_END = 0, 256, 512, 768, 1024, 1280, 1408, 1664


def mix(speed, branch):
    part = speed * (0.25 * branch.astype(F32))
    rest = speed - part
    ahead = speed > 0
    return jnp.where(ahead, rest, part), jnp.where(ahead, part, rest)


def two_terms(values):
    high = values.astype(BF16)
    low = (values - high.astype(F32)).astype(BF16)
    return jnp.concatenate([high, low], axis=-1)


def spreader(offset, lanes, radial, dirs):
    row = lax.broadcasted_iota(jnp.int32, (2 * radial, lanes), 0)
    lane = lax.broadcasted_iota(jnp.int32, (2 * radial, lanes), 1) + offset
    shift = dirs.bit_length() - 1
    return jnp.where((row & (radial - 1)) == (lane >> shift), 1.0, 0.0).astype(BF16)


def spread_all(packed, outs, radial, dirs):
    lanes = outs[0].shape[1]

    @pl.loop(0, lanes // CHUNK, unroll=UNROLL)
    def _(k):
        at = pl.multiple_of(k * CHUNK, CHUNK)
        ones = spreader(at, CHUNK, radial, dirs)
        row = 0
        for out in outs:
            count = out.shape[0]
            left = packed[pl.ds(row, count), :]
            out[:, pl.ds(at, CHUNK)] = jnp.dot(left, ones, preferred_element_type=F32)
            row += count


def blocks_of(design):
    dirs = design.shape[1]
    row = lax.broadcasted_iota(jnp.int32, (CHUNK, dirs), 0)
    col = lax.broadcasted_iota(jnp.int32, (CHUNK, dirs), 1)
    pick = jnp.where((row & (dirs - 1)) == col, 1.0, 0.0).astype(BF16)
    tiled = jnp.dot(pick, design, preferred_element_type=F32).astype(BF16)
    tiled = lax.dot_general(tiled, pick, (((1,), (1,)), ((), ())), preferred_element_type=F32)
    row = lax.broadcasted_iota(jnp.int32, (CHUNK, CHUNK), 0)
    col = lax.broadcasted_iota(jnp.int32, (CHUNK, CHUNK), 1)
    shift = dirs.bit_length() - 1
    return jnp.where((row >> shift) == (col >> shift), tiled, 0.0).astype(BF16)


def wall(radial):
    lane = lax.broadcasted_iota(jnp.int32, (1, radial), 1)
    return jnp.where(lane < radial - 1, 1.0, 0.0)


def ahead_x(rows, last):
    n = rows.shape[0]
    at = lax.broadcasted_iota(jnp.int32, rows.shape, 0)
    return jnp.where(at == n - 1, last, pltpu.roll(rows, n - 1, 0))


def behind_x(rows, first):
    at = lax.broadcasted_iota(jnp.int32, rows.shape, 0)
    return jnp.where(at == 0, first, pltpu.roll(rows, 1, 0))


def ahead_r(rows, dirs):
    return pltpu.roll(rows, rows.shape[1] - dirs, 1)


def behind_r(rows, dirs):
    return pltpu.roll(rows, dirs, 1)


def even_az():
    return lax.rem(lax.axis_index("az"), 2) == 0


def radial_weights(radial):
    return (lax.broadcasted_iota(jnp.int32, (1, radial), 1).astype(F32) + 0.5) / radial


EDGE = ((0, 0), (0, 2), (0, 3), (1, 0), (1, 3), (2, 0), (2, 3))


def edge_kernel(
    tangent, velocity, frac, branch, basis, design, exit_film,
    msg_e, msg_o, sums,
    field, vel, share, share_2, kind, kind_2, left, mat, film, vel_tan, packed, spread, work, ends, edge, faces, face_a, sems,
):
    cells, rows, lanes = field.shape
    radial = vel.shape[-1]
    dirs = lanes // radial
    last, end = cells - 1, rows - 1
    inner = wall(radial)
    pairs = [
        (exit_film, film), (velocity, vel), (branch.at[0], kind), (frac.at[0], share), (frac.at[1, 0, last], share_2),
        (branch.at[1, 0, last], kind_2), (design, mat), (tangent, field),
    ]
    copies = [pltpu.make_async_copy(src, dst, sems.at[i]) for i, (src, dst) in enumerate(pairs)]
    base = len(copies)
    copies += [
        pltpu.make_async_copy(basis.at[c, a], left.at[pl.ds(i * rows, rows)], sems.at[base + i])
        for i, (c, a) in enumerate(EDGE)
    ]
    for copy in copies:
        copy.start()
    copies[0].wait()
    sums[...] = jnp.full(sums.shape, jnp.sum(film[...] * radial_weights(radial)), F32)
    for copy in copies[1:6]:
        copy.wait()

    at = {}
    row = 0
    for c, a in EDGE:
        low, high = mix(vel[c, a], kind[c, a])
        if (c, a) == (0, last):
            high_a = high
        if c == 1:
            at["high", a] = high
        for name, part in zip("plh", (share[c, a], low, high), strict=True):
            packed[pl.ds(row, rows), :] = two_terms(part * inner if c == 2 else part)
            at[name, c, a] = row
            row += rows
    low_2, high_2 = mix(vel[0, last], kind_2[...])
    for name, part in zip("pl", (share_2[...], low_2), strict=True):
        packed[pl.ds(row, rows), :] = two_terms(part)
        at[name] = row
        row += rows
    spread_all(packed, [spread], radial, dirs)

    for copy in copies[6:]:
        copy.wait()
    weights = blocks_of(mat[...])

    @pl.loop(0, lanes // CHUNK, unroll=UNROLL)
    def _(k):
        lane = pl.ds(pl.multiple_of(k * CHUNK, CHUNK), CHUNK)
        vel_tan[:, lane] = jnp.dot(left[:, lane], weights, preferred_element_type=F32).astype(BF16)

    def sp(*key):
        return spread[pl.ds(at[key], rows), :]

    def speed(c, a):
        return vel_tan[pl.ds(EDGE.index((c, a)) * rows, rows), :].astype(F32)

    def along_az(a):
        f = field[a]
        face = speed(0, a) * sp("p", 0, a) + sp("l", 0, a) * f
        return face if a == last else face + sp("h", 0, a) * field[a + 1]

    faces[0] = along_az(0)
    faces[1] = along_az(last - 1)
    face_a[...] = along_az(last)
    for i, a in enumerate((0, last)):
        f = field[a]
        change = faces[0] if a == 0 else face_a[...] - faces[1]
        face = speed(1, a) * sp("p", 1, a) + sp("l", 1, a) * f + sp("h", 1, a) * ahead_x(f, 0.0)
        ends[pl.ds(i, 1), :] = face[end:, :]
        change = change + (face - behind_x(face, 0.0))
        face = speed(2, a) * sp("p", 2, a) + sp("l", 2, a) * f + sp("h", 2, a) * ahead_r(f, dirs)
        change = change + (face - behind_r(face, dirs))
        edge[i] = f - change
    work[...] = speed(0, last) * spread[pl.ds(at["p"], rows), :] + spread[pl.ds(at["l"], rows), :] * edge[1]

    def small_rows(msg, lane, block):
        for k in range(lanes // CHUNK):
            msg[pl.ds(2 * rows + k, 1), pl.ds(lane, CHUNK)] = block[:, k * CHUNK:(k + 1) * CHUNK]

    def halves(msg, lane, block):
        for k in range(rows // 8):
            msg[pl.ds(2 * rows, 8), pl.ds(lane + 128 * k, radial)] = block[8 * k:8 * k + 8]

    def fill(up_msg, down_msg):
        for msg in (up_msg, down_msg):
            msg[pl.ds(2 * rows, 8), :] = jnp.zeros((8, lanes), F32)
        up_msg[pl.ds(0, rows), :] = face_a[...]
        up_msg[pl.ds(rows, rows), :] = work[...]
        halves(up_msg, AT_C1, high_a)
        halves(up_msg, AT_B2, low_2)
        halves(up_msg, AT_C2, high_2)
        small_rows(up_msg, AT_ROW_A, ends[pl.ds(1, 1), :])
        small_rows(up_msg, AT_ROW_B, field[last, pl.ds(0, 1), :])
        small_rows(up_msg, AT_FIRST, sp("h", 0, last)[0:1])
        small_rows(up_msg, AT_END, sp("h", 0, last)[end:])
        up_msg[pl.ds(2 * rows, 1), pl.ds(AT_COEF, radial)] = at["high", last][end:, :]
        down_msg[pl.ds(0, rows), :] = field[0]
        down_msg[pl.ds(rows, rows), :] = edge[0]
        small_rows(down_msg, AT_ROW_A, ends[pl.ds(0, 1), :])
        down_msg[pl.ds(2 * rows, 1), pl.ds(AT_COEF, radial)] = at["high", 0][end:, :]

    even = even_az()

    @pl.when(even)
    def _():
        fill(msg_e, msg_o)

    @pl.when(jnp.logical_not(even))
    def _():
        fill(msg_o, msg_e)


MIDDLE = dict(
    ends=0, end_fixed=4, low_end=8, first=12, partial_first=16, partial_end=20, front=24, coef_a=26, coefs=28
)


def local_kernel(
    tangent, velocity, frac, branch, basis, design, exit_film,
    vel_tan, coef_2, middle, partial, fixed, edges,
    field, vel, share, kind, left, mat, film, product, packed, spread, mixed, sems,
):
    cells, rows, lanes = field.shape
    radial = vel.shape[-1]
    dirs = lanes // radial
    n = cells * rows
    last, end = cells - 1, rows - 1
    inner = wall(radial)
    pairs = [
        (velocity, vel), (branch, kind), (frac, share), (design, mat), (basis, left), (tangent, field), (exit_film, film),
    ]
    copies = [pltpu.make_async_copy(src, dst, sems.at[i]) for i, (src, dst) in enumerate(pairs)]
    for copy in copies:
        copy.start()
    for copy in copies[:3]:
        copy.wait()

    for step in range(2):
        for c in range(3):
            low, high = mix(vel[c], kind[step, c])
            for k, part in enumerate((share[step, c], low, high)):
                part = part.reshape(n, radial)
                part = two_terms(part * inner if c == 2 else part)
                if step == 0 or k == 0:
                    packed[pl.ds(((step * 3 + k) * 3 + c) * n, n), :] = part
                else:
                    for a in range(cells):
                        row = 12 * n + ((a * 2 + k - 1) * 3 + c) * rows
                        packed[pl.ds(row, rows), :] = part[a * rows:(a + 1) * rows]
            if c == 1:
                segments = [(0, high)] if step == 0 else [(6, low), (10, high)]
                if step == 0:
                    middle[pl.ds(MIDDLE["coefs"], 1), :] = jnp.zeros((1, lanes), F32)
                for start, part in segments:
                    for a in range(cells):
                        middle[pl.ds(MIDDLE["coefs"], 1), pl.ds(128 * (start + a), radial)] = part[a, end:, :]
    spread_all(packed, [spread, mixed], radial, dirs)
    done = [pltpu.make_async_copy(mixed, coef_2, sems.at[len(copies) + 1])]
    done[0].start()
    for copy in copies[3:5]:
        copy.wait()
    weights = blocks_of(mat[...])

    @pl.loop(0, lanes // CHUNK, unroll=UNROLL)
    def _(k):
        lane = pl.ds(pl.multiple_of(k * CHUNK, CHUNK), CHUNK)
        block = jnp.dot(left[:, :, :, lane].reshape(3 * n, CHUNK), weights, preferred_element_type=F32)
        product[:, :, :, lane] = block.astype(BF16).reshape(3, cells, rows, CHUNK)

    done.append(pltpu.make_async_copy(product, vel_tan, sems.at[len(copies)]))
    done[-1].start()
    for copy in copies[5:]:
        copy.wait()

    def sp(k, c, a):
        return spread[pl.ds((k * 3 + c) * n + a * rows, rows), :]

    def speed(c, a):
        return product[c, a].astype(F32)

    def put(name, a, block):
        middle[pl.ds(MIDDLE[name] + a, block.shape[0]), :] = block

    before = before_2 = None
    for a in range(cells):
        f = field[a]
        here = speed(0, a) * sp(0, 0, a) + sp(1, 0, a) * f
        if a < last:
            here = here + sp(2, 0, a) * field[a + 1]
        change = here if before is None else here - before
        before = here
        face = speed(1, a) * sp(0, 1, a) + sp(1, 1, a) * f + sp(2, 1, a) * ahead_x(f, 0.0)
        put("ends", a, face[end:])
        edges[pl.ds(2 * rows + a, 1), :] = face[end:]
        change = change + (face - behind_x(face, 0.0))
        face = speed(2, a) * sp(0, 2, a) + sp(1, 2, a) * f + sp(2, 2, a) * ahead_r(f, dirs)
        change = change + (face - behind_r(face, dirs))
        block = f - change
        partial[a] = block
        put("first", a, f[0:1])
        edges[pl.ds(2 * rows + 4 + a, 1), :] = f[0:1]
        put("partial_first", a, block[0:1])
        put("partial_end", a, block[end:])
        put("low_end", a, mixed[pl.ds((a * 6 + 1) * rows + end, 1), :])
        edges[pl.ds(2 * rows + 8 + a, 1), :] = sp(2, 1, a)[end:]
        here_2 = speed(0, a) * sp(3, 0, a)
        change = here_2 if before_2 is None else here_2 - before_2
        before_2 = here_2
        face = speed(1, a) * sp(3, 1, a)
        put("end_fixed", a, face[end:])
        change = change + (face - behind_x(face, 0.0))
        face = speed(2, a) * sp(3, 2, a)
        fixed[a] = change + (face - behind_r(face, dirs))
    edges[pl.ds(0, rows), :] = before
    edges[pl.ds(2 * rows + 16, rows), :] = field[0]
    edges[pl.ds(rows, rows), :] = sp(2, 0, last)
    for k, x in enumerate((0, end)):
        put("front", k, field[0, pl.ds(x, 1), :])
        put("coef_a", k, sp(2, 0, last)[x:x + 1])
    row_film = jnp.sum(film[...] * radial_weights(radial), axis=1, keepdims=True)
    edges[pl.ds(2 * rows + 12, cells), :] = jnp.broadcast_to(row_film, (cells, lanes))
    for copy in done:
        copy.wait()


def after_kernel(done, value, out):
    del done
    out[...] = value[...]


def gathered_row(msg, row, lane, lanes):
    return jnp.concatenate([msg[pl.ds(row + k, 1), pl.ds(lane, CHUNK)] for k in range(lanes // CHUNK)], axis=1)


def middle_kernel(
    middle, in_e, in_o, totals,
    msg_e, msg_o, film_msg,
):
    cells, rows, lanes = CELLS, (in_e.shape[0] - 8) // 2, in_e.shape[1]
    radial, dirs = RADIAL, lanes // RADIAL
    last, end = cells - 1, rows - 1

    def take(name, count=CELLS, at=0):
        return middle[pl.ds(MIDDLE[name] + at, count), :]

    even = even_az()

    def work(up, down, out_up, out_down):
        at_a = lax.broadcasted_iota(jnp.int32, (cells, 1), 0)
        partial_x = []
        for k, (x, lane, name) in enumerate(((0, AT_FIRST, "partial_first"), (end, AT_END, "partial_end"))):
            face = up[pl.ds(x, 1), :] + gathered_row(up, 2 * rows, lane, lanes) * take("front", 1, k)
            beyond = take("coef_a", 1, k) * down[pl.ds(x, 1), :]
            partial_x.append(take(name) + jnp.where(at_a == 0, face, 0.0) - jnp.where(at_a == last, beyond, 0.0))
        second = take("end_fixed") + take("low_end") * partial_x[1]

        lane = lax.broadcasted_iota(jnp.int32, (1, lanes), 1)
        weight = ((lane // dirs).astype(F32) + 0.5) / radial
        raw = (take("ends") + second) * weight
        film = raw[:, 0:128]
        for k in range(1, lanes // 128):
            film = film + raw[:, 128 * k:128 * k + 128]
        shift = 64
        while shift >= dirs:
            film = film + pltpu.roll(film, shift, 1)
            shift //= 2
        quarter = jnp.sum(totals[...], axis=0)
        film_msg[...] = jnp.zeros(film_msg.shape, F32)
        film_msg[pl.ds(0, cells), :] = film
        film_msg[pl.ds(cells, 1), :] = quarter

        def finish(up_msg, down_msg):
            for msg in (up_msg, down_msg):
                msg[1, pl.ds(2, 2), :] = jnp.zeros((2, lanes), F32)
                for a in range(cells):
                    msg[1, pl.ds(3, 1), pl.ds(128 * a, 128)] = film[a:a + 1]
                msg[1, pl.ds(3, 1), pl.ds(128 * cells, 128)] = quarter
            up_msg[0] = take("ends")
            up_msg[1, pl.ds(0, 1), :] = gathered_row(up, 2 * rows, AT_ROW_A, lanes)
            up_msg[1, pl.ds(1, 1), :] = gathered_row(down, 2 * rows, AT_ROW_A, lanes)
            up_msg[1, pl.ds(2, 1), :] = take("coefs", 1)
            up_msg[1, pl.ds(2, 1), pl.ds(128 * 4, radial)] = up[pl.ds(2 * rows, 1), pl.ds(AT_COEF, radial)]
            up_msg[1, pl.ds(2, 1), pl.ds(128 * 5, radial)] = down[pl.ds(2 * rows, 1), pl.ds(AT_COEF, radial)]
            up_msg[2] = second
            down_msg[0] = take("first")
            down_msg[1, pl.ds(0, 1), :] = gathered_row(up, 2 * rows, AT_ROW_B, lanes)
            down_msg[1, pl.ds(1, 1), :] = down[pl.ds(0, 1), :]
            down_msg[2] = partial_x[0]

        even_x = lax.rem(lax.axis_index("ax"), 2) == 0

        @pl.when(even_x)
        def _():
            finish(out_up, out_down)

        @pl.when(jnp.logical_not(even_x))
        def _():
            finish(out_down, out_up)

    @pl.when(even)
    def _():
        work(in_o, in_e, msg_e, msg_o)

    @pl.when(jnp.logical_not(even))
    def _():
        work(in_e, in_o, msg_e, msg_o)


def last_kernel(
    coef_2, partial, fixed, edges, in_e, in_o, film_own, film_1, x_o, x_e,
    out, film_out,
    packed, spread, up, down, below, above, now, edge, result, mixed, sems,
):
    cells, rows, lanes = partial.shape
    radial = packed.shape[1] // 2
    dirs = lanes // radial
    n = cells * rows
    last, end = cells - 1, rows - 1
    even = even_az()
    place = lax.axis_index("ax")
    even_x = lax.rem(place, 2) == 0
    final = lax.axis_size("ax") - 1
    layer = 6 * rows
    loads = [
        pltpu.make_async_copy(coef_2.at[pl.ds(a * layer, layer)], mixed.at[pl.ds(a * layer, layer)], sems.at[cells + a])
        for a in range(cells)
    ]
    for copy in loads:
        copy.start()

    @pl.when(even)
    def _():
        up[...] = in_o[...]
        down[...] = in_e[...]

    @pl.when(jnp.logical_not(even))
    def _():
        up[...] = in_e[...]
        down[...] = in_o[...]

    @pl.when(even_x)
    def _():
        below[...] = jnp.where(place == 0, 0.0, x_o[...])
        above[...] = x_e[...]

    @pl.when(jnp.logical_not(even_x))
    def _():
        below[...] = x_e[...]
        above[...] = jnp.where(place == final, 0.0, x_o[...])

    face_a, coef_a = edges[pl.ds(0, rows), :], edges[pl.ds(rows, rows), :]
    ends, first, coef_x = (edges[pl.ds(2 * rows + 4 * k, cells), :] for k in range(3))

    def joined(msg, lane):
        return jnp.concatenate([msg[pl.ds(2 * rows, 8), pl.ds(lane + 128 * k, radial)] for k in range(rows // 8)], axis=0)

    for k, lane in enumerate((AT_C1, AT_B2, AT_C2)):
        packed[pl.ds(k * rows, rows), :] = two_terms(joined(up, lane))
    singles = [below[1, pl.ds(2, 1), pl.ds(128 * k, radial)] for k in range(14)]
    singles += [msg[pl.ds(2 * rows, 1), pl.ds(AT_COEF, radial)] for msg in (up, down)]
    packed[pl.ds(3 * rows, 16), :] = two_terms(jnp.concatenate(singles, axis=0))
    spread_all(packed, [spread], radial, dirs)
    in_c1, in_b2, in_c2 = (spread[pl.ds(k * rows, rows), :] for k in range(3))
    below_c = spread[pl.ds(3 * rows, 6), :]
    below_b2, below_c2 = spread[pl.ds(3 * rows + 6, 4), :], spread[pl.ds(3 * rows + 10, 4), :]
    own_c = jnp.concatenate([coef_x, spread[pl.ds(3 * rows + 14, 2), :]], axis=0)

    starts = jnp.concatenate([first, gathered_row(up, 2 * rows, AT_ROW_B, lanes), down[pl.ds(0, 1), :]], axis=0)
    enter = jnp.concatenate([below[0], below[1, pl.ds(0, 2), :]], axis=0) + below_c * starts
    leave = own_c * jnp.concatenate([above[0], above[1, pl.ds(0, 2), :]], axis=0)
    crossing = in_c1 * edges[pl.ds(2 * rows + 16, rows), :]
    beyond = coef_a * down[pl.ds(0, rows), :]
    at_x = lax.broadcasted_iota(jnp.int32, (rows, 1), 0)

    def with_edges(block, k):
        return block + jnp.where(at_x == 0, enter[k:k + 1], 0.0) - jnp.where(at_x == end, leave[k:k + 1], 0.0)

    for a in range(cells):
        f = partial[a]
        if a == 0:
            f = f + up[pl.ds(0, rows), :] + crossing
        if a == last:
            f = f - beyond
        now[a] = with_edges(f, a)
    now[cells] = with_edges(down[pl.ds(rows, rows), :] + face_a + beyond, 5)
    lower = up[pl.ds(rows, rows), :] + in_b2 * (
        jnp.where(at_x == 0, enter[4:5], 0.0) - jnp.where(at_x == end, leave[4:5], 0.0) - crossing
    )
    before = lower + in_c2 * now[0]

    first_now = jnp.concatenate([now[a, pl.ds(0, 1), :] for a in range(cells)], axis=0)
    enter_2 = below[2] - below_b2 * (below_c[0:4] * first) + below_c2 * first_now
    inside = jnp.where(place == final, 0.0, 1.0)
    edge[...] = inside * (above[2] + ends + leave[0:4])

    def low(c, a):
        return mixed[pl.ds((a * 6 + c) * rows, rows), :]

    def high(c, a):
        return mixed[pl.ds((a * 6 + 3 + c) * rows, rows), :]

    copies = []
    for a in range(cells):
        loads[a].wait()
        f = now[a]
        face = low(0, a) * f + high(0, a) * now[a + 1]
        change = fixed[a] + (face - before)
        before = face
        face = low(1, a) * f + high(1, a) * ahead_x(f, edge[pl.ds(a, 1), :])
        change = change + (face - behind_x(face, enter_2[a:a + 1]))
        face = low(2, a) * f + high(2, a) * ahead_r(f, dirs)
        change = change + (face - behind_r(face, dirs))
        result[a] = f - change
        copies.append(pltpu.make_async_copy(result.at[a], out.at[a], sems.at[a]))
        copies[a].start()

    share = film_out.shape[1]
    total = film_own[pl.ds(cells, 1), :] + film_1[pl.ds(cells, 1), :]
    for msg in (x_e, x_o):
        total = total + msg[1, pl.ds(3, 1), pl.ds(128 * cells, 128)]
    mean = total / (cells * lax.axis_size("az"))
    factor = mean / edges[pl.ds(2 * rows + 12, cells), pl.ds(0, 128)]
    for k, source in enumerate((x_o, film_1, x_e, film_own)):

        @pl.when(place == k)
        def _():
            if len(source.shape) == 2:
                film = source[pl.ds(0, cells), :]
            else:
                film = jnp.concatenate([source[1, pl.ds(3, 1), pl.ds(128 * a, 128)] for a in range(cells)], axis=0)
            film_out[...] = (film * factor)[:, k * share:(k + 1) * share]

    for copy in copies:
        copy.wait()


def swap(value, axis, pairing):
    count = lax.axis_size(axis)
    if axis == "ax":
        other = [i ^ pairing for i in range(count)]
    elif pairing == 0:
        other = [i ^ 1 for i in range(count)]
    else:
        other = [(i - 1 if i % 2 == 0 else i + 1) % count for i in range(count)]
    return lax.ppermute(value, axis, list(enumerate(other)))


def shifted_by_quarters(value):
    count, quarters = lax.axis_size("az"), lax.axis_size("ax")
    part = count // quarters
    pairs = [
        ((i + part * j) % count * quarters + j, i * quarters + j) for i in range(count) for j in range(quarters)
    ]
    return lax.ppermute(value, ("az", "ax"), pairs)


def quarter_sums(value):
    count, quarters = lax.axis_size("az"), lax.axis_size("ax")
    part = count // quarters
    groups = [list(range(part * k, part * (k + 1))) for k in range(quarters)]
    return lax.all_to_all(value, "az", 0, 0, axis_index_groups=groups)


def pinned(value, space):
    return pltpu.with_memory_space_constraint(value, space)


def placed(space, shape, dtype):
    return space(shape, dtype)


def call(kernel, args, outs, scratch, in_hbm=0, out_hbm=0, free=0, sems=0, cost=None):
    vmem, hbm = pl.BlockSpec(memory_space=pltpu.VMEM), pl.BlockSpec(memory_space=pl.ANY)
    shapes = [pltpu.VMEM(shape, dtype) for shape, dtype in scratch]
    pinned_outs = len(outs) - free
    shapes_out = [placed(pltpu.HBM if i < out_hbm else pltpu.VMEM, *out) for i, out in enumerate(outs[:pinned_outs])]
    shapes_out += [jax.ShapeDtypeStruct(*out) for out in outs[pinned_outs:]]
    args = [pinned(arg, pltpu.HBM if i < in_hbm else pltpu.VMEM) for i, arg in enumerate(args)]
    if sems:
        shapes.append(pltpu.SemaphoreType.DMA((sems,)))
    return pl.pallas_call(
        kernel,
        out_shape=shapes_out,
        in_specs=[hbm] * in_hbm + [vmem] * (len(args) - in_hbm),
        out_specs=[hbm] * out_hbm + [vmem] * (len(outs) - out_hbm),
        scratch_shapes=shapes,
        compiler_params=pltpu.CompilerParams(vmem_limit_bytes=32 * 2**20),
        cost_estimate=cost,
        name=kernel.__name__,
    )(*args)


def local(tangent, velocity, face_frac, branch, basis, design, exit_film):
    cells, rows, lanes = tangent.shape
    radial = velocity.shape[-1]
    dirs = design.shape[1]
    n = cells * rows
    devices = lax.axis_size("az")
    layer, cell_layer = (rows, lanes), (rows, radial)
    z_msg, x_msg, line = (2 * rows + 8, lanes), (3, cells, lanes), (cells, lanes)
    inputs = (tangent, velocity, face_frac, branch, basis, design, exit_film)
    count = (3 * len(EDGE) + 2) * rows
    z_e, z_o, sums = call(
        edge_kernel,
        inputs,
        [(z_msg, F32), (z_msg, F32), ((devices // lax.axis_size("ax"), 1, 128), F32)],
        [
            (tangent.shape, F32), (velocity.shape, F32), (velocity.shape, F32), (cell_layer, F32),
            (velocity.shape, branch.dtype), (cell_layer, branch.dtype), ((len(EDGE) * rows, lanes), BF16),
            (design.shape, BF16), (exit_film.shape, F32), ((len(EDGE) * rows, lanes), BF16),
            ((count, 2 * radial), BF16), ((count, lanes), F32), (layer, F32), ((2, lanes), F32),
            ((2, *layer), F32), ((2, *layer), F32), (layer, F32),
        ],
        in_hbm=7,
        sems=8 + len(EDGE),
    )
    other_sums = shifted_by_quarters(sums)
    in_e, in_o = swap(z_e, "az", 0), swap(z_o, "az", 1)
    velocity_tangent, coef_2, middle, partial, fixed, edges = call(
        local_kernel,
        inputs,
        [
            (basis.shape, BF16), ((6 * n, lanes), F32), ((32, lanes), F32), (tangent.shape, F32), (tangent.shape, F32),
            ((3 * rows + 16, lanes), F32),
        ],
        [
            (tangent.shape, F32), (velocity.shape, F32), (face_frac.shape, F32), (branch.shape, branch.dtype),
            (basis.shape, BF16), (design.shape, BF16), (exit_film.shape, F32), (basis.shape, BF16),
            ((18 * n, 2 * radial), BF16), ((12 * n, lanes), F32), ((6 * n, lanes), F32),
        ],
        in_hbm=7,
        out_hbm=2,
        sems=9,
        cost=pl.CostEstimate(flops=10**9, bytes_accessed=16 * 10**6, transcendentals=0),
    )
    (ready_sums,) = call(after_kernel, (coef_2, other_sums), [(sums.shape, F32)], [], in_hbm=1)
    totals = quarter_sums(ready_sums)
    x_e, x_o, film = call(
        middle_kernel, (middle, in_e, in_o, totals), [(x_msg, F32), (x_msg, F32), ((8, 128), F32)], []
    )
    film_1 = swap(film, "ax", 2)
    from_o, from_e = swap(x_o, "ax", 3), swap(x_e, "ax", 1)
    count = 3 * rows + 16
    out, film_out = call(
        last_kernel,
        (coef_2, partial, fixed, edges, in_e, in_o, film, film_1, from_o, from_e),
        [(tangent.shape, F32), ((cells, dirs // lax.axis_size("ax")), F32)],
        [
            ((count, 2 * radial), BF16), ((count, lanes), F32), (z_msg, F32), (z_msg, F32), (x_msg, F32), (x_msg, F32),
            ((cells + 1, *layer), F32), (line, F32), (tangent.shape, F32), ((6 * n, lanes), F32),
        ],
        in_hbm=1,
        out_hbm=1,
        free=1,
        sems=2 * cells,
    )
    return out, velocity_tangent, film_out


def solution(mesh):
    in_specs = (
        P("az", "ax", None),
        P(None, "az", "ax", None),
        P(None, None, "az", "ax", None),
        P(None, None, "az", "ax", None),
        P(None, "az", "ax", None),
        P(),
        P("az", None),
    )
    out_specs = (P("az", "ax", None), P(None, "az", "ax", None), P("az", "ax"))
    return jax.shard_map(local, mesh=mesh, in_specs=in_specs, out_specs=out_specs, check_vma=False)
```

```python
import jax
import jax.numpy as jnp
from jax import lax
from jax.experimental import pallas as pl
from jax.experimental.pallas import tpu as pltpu
from jax.sharding import PartitionSpec as P

F32, BF16 = jnp.float32, jnp.bfloat16
CHUNK = 256
RADIAL = 64
CELLS = 4
UNROLL = 8
AT_C1, AT_B2, AT_C2, AT_ROW_A, AT_ROW_B, AT_COEF, AT_FIRST, AT_END = 0, 256, 512, 768, 1024, 1280, 1408, 1664


def mix(speed, branch):
    part = speed * (0.25 * branch.astype(F32))
    rest = speed - part
    ahead = speed > 0
    return jnp.where(ahead, rest, part), jnp.where(ahead, part, rest)


def two_terms(values):
    high = values.astype(BF16)
    low = (values - high.astype(F32)).astype(BF16)
    return jnp.concatenate([high, low], axis=-1)


def spreader(offset, lanes, radial, dirs):
    row = lax.broadcasted_iota(jnp.int32, (2 * radial, lanes), 0)
    lane = lax.broadcasted_iota(jnp.int32, (2 * radial, lanes), 1) + offset
    shift = dirs.bit_length() - 1
    return jnp.where((row & (radial - 1)) == (lane >> shift), 1.0, 0.0).astype(BF16)


def spread_all(packed, outs, radial, dirs):
    lanes = outs[0].shape[1]

    @pl.loop(0, lanes // CHUNK, unroll=UNROLL)
    def _(k):
        at = pl.multiple_of(k * CHUNK, CHUNK)
        ones = spreader(at, CHUNK, radial, dirs)
        row = 0
        for out in outs:
            count = out.shape[0]
            left = packed[pl.ds(row, count), :]
            out[:, pl.ds(at, CHUNK)] = jnp.dot(left, ones, preferred_element_type=F32)
            row += count


def blocks_of(design):
    dirs = design.shape[1]
    row = lax.broadcasted_iota(jnp.int32, (CHUNK, dirs), 0)
    col = lax.broadcasted_iota(jnp.int32, (CHUNK, dirs), 1)
    pick = jnp.where((row & (dirs - 1)) == col, 1.0, 0.0).astype(BF16)
    tiled = jnp.dot(pick, design, preferred_element_type=F32).astype(BF16)
    tiled = lax.dot_general(tiled, pick, (((1,), (1,)), ((), ())), preferred_element_type=F32)
    row = lax.broadcasted_iota(jnp.int32, (CHUNK, CHUNK), 0)
    col = lax.broadcasted_iota(jnp.int32, (CHUNK, CHUNK), 1)
    shift = dirs.bit_length() - 1
    return jnp.where((row >> shift) == (col >> shift), tiled, 0.0).astype(BF16)


def wall(radial):
    lane = lax.broadcasted_iota(jnp.int32, (1, radial), 1)
    return jnp.where(lane < radial - 1, 1.0, 0.0)


def ahead_x(rows, last):
    n = rows.shape[0]
    at = lax.broadcasted_iota(jnp.int32, rows.shape, 0)
    return jnp.where(at == n - 1, last, pltpu.roll(rows, n - 1, 0))


def behind_x(rows, first):
    at = lax.broadcasted_iota(jnp.int32, rows.shape, 0)
    return jnp.where(at == 0, first, pltpu.roll(rows, 1, 0))


def ahead_r(rows, dirs):
    return pltpu.roll(rows, rows.shape[1] - dirs, 1)


def behind_r(rows, dirs):
    return pltpu.roll(rows, dirs, 1)


def even_az():
    return lax.rem(lax.axis_index("az"), 2) == 0


def radial_weights(radial):
    return (lax.broadcasted_iota(jnp.int32, (1, radial), 1).astype(F32) + 0.5) / radial


EDGE = ((0, 0), (0, 2), (0, 3), (1, 0), (1, 3), (2, 0), (2, 3))


def edge_kernel(
    tangent, velocity, frac, branch, basis, design, exit_film,
    msg_e, msg_o, sums,
    field, vel, share, share_2, kind, kind_2, left, mat, film, vel_tan, packed, spread, work, ends, edge, faces, face_a, sems,
):
    cells, rows, lanes = field.shape
    radial = vel.shape[-1]
    dirs = lanes // radial
    last, end = cells - 1, rows - 1
    inner = wall(radial)
    pairs = [
        (exit_film, film), (velocity, vel), (branch.at[0], kind), (frac.at[0], share), (frac.at[1, 0, last], share_2),
        (branch.at[1, 0, last], kind_2), (design, mat), (tangent, field),
    ]
    copies = [pltpu.make_async_copy(src, dst, sems.at[i]) for i, (src, dst) in enumerate(pairs)]
    base = len(copies)
    copies += [
        pltpu.make_async_copy(basis.at[c, a], left.at[pl.ds(i * rows, rows)], sems.at[base + i])
        for i, (c, a) in enumerate(EDGE)
    ]
    for copy in copies:
        copy.start()
    copies[0].wait()
    sums[...] = jnp.full(sums.shape, jnp.sum(film[...] * radial_weights(radial)), F32)
    for copy in copies[1:6]:
        copy.wait()

    at = {}
    row = 0
    for c, a in EDGE:
        low, high = mix(vel[c, a], kind[c, a])
        if (c, a) == (0, last):
            high_a = high
        if c == 1:
            at["high", a] = high
        for name, part in zip("plh", (share[c, a], low, high), strict=True):
            packed[pl.ds(row, rows), :] = two_terms(part * inner if c == 2 else part)
            at[name, c, a] = row
            row += rows
    low_2, high_2 = mix(vel[0, last], kind_2[...])
    for name, part in zip("pl", (share_2[...], low_2), strict=True):
        packed[pl.ds(row, rows), :] = two_terms(part)
        at[name] = row
        row += rows
    spread_all(packed, [spread], radial, dirs)

    for copy in copies[6:]:
        copy.wait()
    weights = blocks_of(mat[...])

    @pl.loop(0, lanes // CHUNK, unroll=UNROLL)
    def _(k):
        lane = pl.ds(pl.multiple_of(k * CHUNK, CHUNK), CHUNK)
        vel_tan[:, lane] = jnp.dot(left[:, lane], weights, preferred_element_type=F32).astype(BF16)

    def sp(*key):
        return spread[pl.ds(at[key], rows), :]

    def speed(c, a):
        return vel_tan[pl.ds(EDGE.index((c, a)) * rows, rows), :].astype(F32)

    def along_az(a):
        f = field[a]
        face = speed(0, a) * sp("p", 0, a) + sp("l", 0, a) * f
        return face if a == last else face + sp("h", 0, a) * field[a + 1]

    faces[0] = along_az(0)
    faces[1] = along_az(last - 1)
    face_a[...] = along_az(last)
    for i, a in enumerate((0, last)):
        f = field[a]
        change = faces[0] if a == 0 else face_a[...] - faces[1]
        face = speed(1, a) * sp("p", 1, a) + sp("l", 1, a) * f + sp("h", 1, a) * ahead_x(f, 0.0)
        ends[pl.ds(i, 1), :] = face[end:, :]
        change = change + (face - behind_x(face, 0.0))
        face = speed(2, a) * sp("p", 2, a) + sp("l", 2, a) * f + sp("h", 2, a) * ahead_r(f, dirs)
        change = change + (face - behind_r(face, dirs))
        edge[i] = f - change
    work[...] = speed(0, last) * spread[pl.ds(at["p"], rows), :] + spread[pl.ds(at["l"], rows), :] * edge[1]

    def small_rows(msg, lane, block):
        for k in range(lanes // CHUNK):
            msg[pl.ds(2 * rows + k, 1), pl.ds(lane, CHUNK)] = block[:, k * CHUNK:(k + 1) * CHUNK]

    def halves(msg, lane, block):
        for k in range(rows // 8):
            msg[pl.ds(2 * rows, 8), pl.ds(lane + 128 * k, radial)] = block[8 * k:8 * k + 8]

    def fill(up_msg, down_msg):
        for msg in (up_msg, down_msg):
            msg[pl.ds(2 * rows, 8), :] = jnp.zeros((8, lanes), F32)
        up_msg[pl.ds(0, rows), :] = face_a[...]
        up_msg[pl.ds(rows, rows), :] = work[...]
        halves(up_msg, AT_C1, high_a)
        halves(up_msg, AT_B2, low_2)
        halves(up_msg, AT_C2, high_2)
        small_rows(up_msg, AT_ROW_A, ends[pl.ds(1, 1), :])
        small_rows(up_msg, AT_ROW_B, field[last, pl.ds(0, 1), :])
        small_rows(up_msg, AT_FIRST, sp("h", 0, last)[0:1])
        small_rows(up_msg, AT_END, sp("h", 0, last)[end:])
        up_msg[pl.ds(2 * rows, 1), pl.ds(AT_COEF, radial)] = at["high", last][end:, :]
        down_msg[pl.ds(0, rows), :] = field[0]
        down_msg[pl.ds(rows, rows), :] = edge[0]
        small_rows(down_msg, AT_ROW_A, ends[pl.ds(0, 1), :])
        down_msg[pl.ds(2 * rows, 1), pl.ds(AT_COEF, radial)] = at["high", 0][end:, :]

    even = even_az()

    @pl.when(even)
    def _():
        fill(msg_e, msg_o)

    @pl.when(jnp.logical_not(even))
    def _():
        fill(msg_o, msg_e)


MIDDLE = dict(
    ends=0, end_fixed=4, low_end=8, first=12, partial_first=16, partial_end=20, front=24, coef_a=26, coefs=28
)


def local_kernel(
    tangent, velocity, frac, branch, basis, design, exit_film,
    vel_tan, coef_2, middle, partial, fixed, edges,
    field, vel, share, kind, left, mat, film, product, packed, spread, mixed, sems,
):
    cells, rows, lanes = field.shape
    radial = vel.shape[-1]
    dirs = lanes // radial
    n = cells * rows
    last, end = cells - 1, rows - 1
    inner = wall(radial)
    pairs = [
        (velocity, vel), (branch, kind), (frac, share), (design, mat), (basis, left), (tangent, field), (exit_film, film),
    ]
    copies = [pltpu.make_async_copy(src, dst, sems.at[i]) for i, (src, dst) in enumerate(pairs)]
    for copy in copies:
        copy.start()
    for copy in copies[:3]:
        copy.wait()

    for step in range(2):
        for c in range(3):
            low, high = mix(vel[c], kind[step, c])
            for k, part in enumerate((share[step, c], low, high)):
                part = part.reshape(n, radial)
                part = two_terms(part * inner if c == 2 else part)
                if step == 0 or k == 0:
                    packed[pl.ds(((step * 3 + k) * 3 + c) * n, n), :] = part
                else:
                    for a in range(cells):
                        row = 12 * n + ((a * 2 + k - 1) * 3 + c) * rows
                        packed[pl.ds(row, rows), :] = part[a * rows:(a + 1) * rows]
            if c == 1:
                segments = [(0, high)] if step == 0 else [(6, low), (10, high)]
                if step == 0:
                    middle[pl.ds(MIDDLE["coefs"], 1), :] = jnp.zeros((1, lanes), F32)
                for start, part in segments:
                    for a in range(cells):
                        middle[pl.ds(MIDDLE["coefs"], 1), pl.ds(128 * (start + a), radial)] = part[a, end:, :]
    spread_all(packed, [spread, mixed], radial, dirs)
    done = [pltpu.make_async_copy(mixed, coef_2, sems.at[len(copies) + 1])]
    done[0].start()
    for copy in copies[3:5]:
        copy.wait()
    weights = blocks_of(mat[...])

    @pl.loop(0, lanes // CHUNK, unroll=UNROLL)
    def _(k):
        lane = pl.ds(pl.multiple_of(k * CHUNK, CHUNK), CHUNK)
        block = jnp.dot(left[:, :, :, lane].reshape(3 * n, CHUNK), weights, preferred_element_type=F32)
        product[:, :, :, lane] = block.astype(BF16).reshape(3, cells, rows, CHUNK)

    done.append(pltpu.make_async_copy(product, vel_tan, sems.at[len(copies)]))
    done[-1].start()
    for copy in copies[5:]:
        copy.wait()

    def sp(k, c, a):
        return spread[pl.ds((k * 3 + c) * n + a * rows, rows), :]

    def speed(c, a):
        return product[c, a].astype(F32)

    def put(name, a, block):
        middle[pl.ds(MIDDLE[name] + a, block.shape[0]), :] = block

    before = before_2 = None
    for a in range(cells):
        f = field[a]
        here = speed(0, a) * sp(0, 0, a) + sp(1, 0, a) * f
        if a < last:
            here = here + sp(2, 0, a) * field[a + 1]
        change = here if before is None else here - before
        before = here
        face = speed(1, a) * sp(0, 1, a) + sp(1, 1, a) * f + sp(2, 1, a) * ahead_x(f, 0.0)
        put("ends", a, face[end:])
        edges[pl.ds(2 * rows + a, 1), :] = face[end:]
        change = change + (face - behind_x(face, 0.0))
        face = speed(2, a) * sp(0, 2, a) + sp(1, 2, a) * f + sp(2, 2, a) * ahead_r(f, dirs)
        change = change + (face - behind_r(face, dirs))
        block = f - change
        partial[a] = block
        put("first", a, f[0:1])
        edges[pl.ds(2 * rows + 4 + a, 1), :] = f[0:1]
        put("partial_first", a, block[0:1])
        put("partial_end", a, block[end:])
        put("low_end", a, mixed[pl.ds((a * 6 + 1) * rows + end, 1), :])
        edges[pl.ds(2 * rows + 8 + a, 1), :] = sp(2, 1, a)[end:]
        here_2 = speed(0, a) * sp(3, 0, a)
        change = here_2 if before_2 is None else here_2 - before_2
        before_2 = here_2
        face = speed(1, a) * sp(3, 1, a)
        put("end_fixed", a, face[end:])
        change = change + (face - behind_x(face, 0.0))
        face = speed(2, a) * sp(3, 2, a)
        fixed[a] = change + (face - behind_r(face, dirs))
    edges[pl.ds(0, rows), :] = before
    edges[pl.ds(2 * rows + 16, rows), :] = field[0]
    edges[pl.ds(rows, rows), :] = sp(2, 0, last)
    for k, x in enumerate((0, end)):
        put("front", k, field[0, pl.ds(x, 1), :])
        put("coef_a", k, sp(2, 0, last)[x:x + 1])
    row_film = jnp.sum(film[...] * radial_weights(radial), axis=1, keepdims=True)
    edges[pl.ds(2 * rows + 12, cells), :] = jnp.broadcast_to(row_film, (cells, lanes))
    for copy in done:
        copy.wait()


def gathered_row(msg, row, lane, lanes):
    return jnp.concatenate([msg[pl.ds(row + k, 1), pl.ds(lane, CHUNK)] for k in range(lanes // CHUNK)], axis=1)


def middle_kernel(
    middle, in_e, in_o,
    msg_e, msg_o, film_msg,
):
    cells, rows, lanes = CELLS, (in_e.shape[0] - 8) // 2, in_e.shape[1]
    radial, dirs = RADIAL, lanes // RADIAL
    last, end = cells - 1, rows - 1

    def take(name, count=CELLS, at=0):
        return middle[pl.ds(MIDDLE[name] + at, count), :]

    even = even_az()

    def work(up, down, out_up, out_down):
        at_a = lax.broadcasted_iota(jnp.int32, (cells, 1), 0)
        partial_x = []
        for k, (x, lane, name) in enumerate(((0, AT_FIRST, "partial_first"), (end, AT_END, "partial_end"))):
            face = up[pl.ds(x, 1), :] + gathered_row(up, 2 * rows, lane, lanes) * take("front", 1, k)
            beyond = take("coef_a", 1, k) * down[pl.ds(x, 1), :]
            partial_x.append(take(name) + jnp.where(at_a == 0, face, 0.0) - jnp.where(at_a == last, beyond, 0.0))
        second = take("end_fixed") + take("low_end") * partial_x[1]

        lane = lax.broadcasted_iota(jnp.int32, (1, lanes), 1)
        weight = ((lane // dirs).astype(F32) + 0.5) / radial
        raw = (take("ends") + second) * weight
        film = raw[:, 0:128]
        for k in range(1, lanes // 128):
            film = film + raw[:, 128 * k:128 * k + 128]
        shift = 64
        while shift >= dirs:
            film = film + pltpu.roll(film, shift, 1)
            shift //= 2
        film_msg[...] = jnp.zeros(film_msg.shape, F32)
        film_msg[pl.ds(0, cells), :] = film

        def finish(up_msg, down_msg):
            for msg in (up_msg, down_msg):
                msg[1, pl.ds(2, 2), :] = jnp.zeros((2, lanes), F32)
                for a in range(cells):
                    msg[1, pl.ds(3, 1), pl.ds(128 * a, 128)] = film[a:a + 1]
            up_msg[0] = take("ends")
            up_msg[1, pl.ds(0, 1), :] = gathered_row(up, 2 * rows, AT_ROW_A, lanes)
            up_msg[1, pl.ds(1, 1), :] = gathered_row(down, 2 * rows, AT_ROW_A, lanes)
            up_msg[1, pl.ds(2, 1), :] = take("coefs", 1)
            up_msg[1, pl.ds(2, 1), pl.ds(128 * 4, radial)] = up[pl.ds(2 * rows, 1), pl.ds(AT_COEF, radial)]
            up_msg[1, pl.ds(2, 1), pl.ds(128 * 5, radial)] = down[pl.ds(2 * rows, 1), pl.ds(AT_COEF, radial)]
            up_msg[2] = second
            down_msg[0] = take("first")
            down_msg[1, pl.ds(0, 1), :] = gathered_row(up, 2 * rows, AT_ROW_B, lanes)
            down_msg[1, pl.ds(1, 1), :] = down[pl.ds(0, 1), :]
            down_msg[2] = partial_x[0]

        even_x = lax.rem(lax.axis_index("ax"), 2) == 0

        @pl.when(even_x)
        def _():
            finish(out_up, out_down)

        @pl.when(jnp.logical_not(even_x))
        def _():
            finish(out_down, out_up)

    @pl.when(even)
    def _():
        work(in_o, in_e, msg_e, msg_o)

    @pl.when(jnp.logical_not(even))
    def _():
        work(in_e, in_o, msg_e, msg_o)


def last_kernel(
    coef_2, partial, fixed, edges, in_e, in_o, film_own, film_1, x_o, x_e, totals,
    out, film_out,
    packed, spread, up, down, below, above, now, edge, result, mixed, sems,
):
    cells, rows, lanes = partial.shape
    radial = packed.shape[1] // 2
    dirs = lanes // radial
    n = cells * rows
    last, end = cells - 1, rows - 1
    even = even_az()
    place = lax.axis_index("ax")
    even_x = lax.rem(place, 2) == 0
    final = lax.axis_size("ax") - 1
    layer = 6 * rows
    loads = [
        pltpu.make_async_copy(coef_2.at[pl.ds(a * layer, layer)], mixed.at[pl.ds(a * layer, layer)], sems.at[cells + a])
        for a in range(cells)
    ]
    for copy in loads:
        copy.start()

    @pl.when(even)
    def _():
        up[...] = in_o[...]
        down[...] = in_e[...]

    @pl.when(jnp.logical_not(even))
    def _():
        up[...] = in_e[...]
        down[...] = in_o[...]

    @pl.when(even_x)
    def _():
        below[...] = jnp.where(place == 0, 0.0, x_o[...])
        above[...] = x_e[...]

    @pl.when(jnp.logical_not(even_x))
    def _():
        below[...] = x_e[...]
        above[...] = jnp.where(place == final, 0.0, x_o[...])

    face_a, coef_a = edges[pl.ds(0, rows), :], edges[pl.ds(rows, rows), :]
    ends, first, coef_x = (edges[pl.ds(2 * rows + 4 * k, cells), :] for k in range(3))

    def joined(msg, lane):
        return jnp.concatenate([msg[pl.ds(2 * rows, 8), pl.ds(lane + 128 * k, radial)] for k in range(rows // 8)], axis=0)

    for k, lane in enumerate((AT_C1, AT_B2, AT_C2)):
        packed[pl.ds(k * rows, rows), :] = two_terms(joined(up, lane))
    singles = [below[1, pl.ds(2, 1), pl.ds(128 * k, radial)] for k in range(14)]
    singles += [msg[pl.ds(2 * rows, 1), pl.ds(AT_COEF, radial)] for msg in (up, down)]
    packed[pl.ds(3 * rows, 16), :] = two_terms(jnp.concatenate(singles, axis=0))
    spread_all(packed, [spread], radial, dirs)
    in_c1, in_b2, in_c2 = (spread[pl.ds(k * rows, rows), :] for k in range(3))
    below_c = spread[pl.ds(3 * rows, 6), :]
    below_b2, below_c2 = spread[pl.ds(3 * rows + 6, 4), :], spread[pl.ds(3 * rows + 10, 4), :]
    own_c = jnp.concatenate([coef_x, spread[pl.ds(3 * rows + 14, 2), :]], axis=0)

    starts = jnp.concatenate([first, gathered_row(up, 2 * rows, AT_ROW_B, lanes), down[pl.ds(0, 1), :]], axis=0)
    enter = jnp.concatenate([below[0], below[1, pl.ds(0, 2), :]], axis=0) + below_c * starts
    leave = own_c * jnp.concatenate([above[0], above[1, pl.ds(0, 2), :]], axis=0)
    crossing = in_c1 * edges[pl.ds(2 * rows + 16, rows), :]
    beyond = coef_a * down[pl.ds(0, rows), :]
    at_x = lax.broadcasted_iota(jnp.int32, (rows, 1), 0)

    def with_edges(block, k):
        return block + jnp.where(at_x == 0, enter[k:k + 1], 0.0) - jnp.where(at_x == end, leave[k:k + 1], 0.0)

    for a in range(cells):
        f = partial[a]
        if a == 0:
            f = f + up[pl.ds(0, rows), :] + crossing
        if a == last:
            f = f - beyond
        now[a] = with_edges(f, a)
    now[cells] = with_edges(down[pl.ds(rows, rows), :] + face_a + beyond, 5)
    lower = up[pl.ds(rows, rows), :] + in_b2 * (
        jnp.where(at_x == 0, enter[4:5], 0.0) - jnp.where(at_x == end, leave[4:5], 0.0) - crossing
    )
    before = lower + in_c2 * now[0]

    first_now = jnp.concatenate([now[a, pl.ds(0, 1), :] for a in range(cells)], axis=0)
    enter_2 = below[2] - below_b2 * (below_c[0:4] * first) + below_c2 * first_now
    inside = jnp.where(place == final, 0.0, 1.0)
    edge[...] = inside * (above[2] + ends + leave[0:4])

    def low(c, a):
        return mixed[pl.ds((a * 6 + c) * rows, rows), :]

    def high(c, a):
        return mixed[pl.ds((a * 6 + 3 + c) * rows, rows), :]

    copies = []
    for a in range(cells):
        loads[a].wait()
        f = now[a]
        face = low(0, a) * f + high(0, a) * now[a + 1]
        change = fixed[a] + (face - before)
        before = face
        face = low(1, a) * f + high(1, a) * ahead_x(f, edge[pl.ds(a, 1), :])
        change = change + (face - behind_x(face, enter_2[a:a + 1]))
        face = low(2, a) * f + high(2, a) * ahead_r(f, dirs)
        change = change + (face - behind_r(face, dirs))
        result[a] = f - change
        copies.append(pltpu.make_async_copy(result.at[a], out.at[a], sems.at[a]))
        copies[a].start()

    share = film_out.shape[1]
    mean = jnp.sum(totals[:, 0:1, :], axis=0) / (cells * totals.shape[0])
    factor = mean / edges[pl.ds(2 * rows + 12, cells), pl.ds(0, 128)]
    for k, source in enumerate((x_o, film_1, x_e, film_own)):

        @pl.when(place == k)
        def _():
            if len(source.shape) == 2:
                film = source[pl.ds(0, cells), :]
            else:
                film = jnp.concatenate([source[1, pl.ds(3, 1), pl.ds(128 * a, 128)] for a in range(cells)], axis=0)
            film_out[...] = (film * factor)[:, k * share:(k + 1) * share]

    for copy in copies:
        copy.wait()


def swap(value, axis, pairing):
    count = lax.axis_size(axis)
    if axis == "ax":
        other = [i ^ pairing for i in range(count)]
    elif pairing == 0:
        other = [i ^ 1 for i in range(count)]
    else:
        other = [(i - 1 if i % 2 == 0 else i + 1) % count for i in range(count)]
    return lax.ppermute(value, axis, list(enumerate(other)))


def pinned(value, space):
    return pltpu.with_memory_space_constraint(value, space)


def placed(space, shape, dtype):
    return space(shape, dtype)


def call(kernel, args, outs, scratch, in_hbm=0, out_hbm=0, free=0, sems=0, cost=None):
    vmem, hbm = pl.BlockSpec(memory_space=pltpu.VMEM), pl.BlockSpec(memory_space=pl.ANY)
    shapes = [pltpu.VMEM(shape, dtype) for shape, dtype in scratch]
    pinned_outs = len(outs) - free
    shapes_out = [placed(pltpu.HBM if i < out_hbm else pltpu.VMEM, *out) for i, out in enumerate(outs[:pinned_outs])]
    shapes_out += [jax.ShapeDtypeStruct(*out) for out in outs[pinned_outs:]]
    args = [pinned(arg, pltpu.HBM if i < in_hbm else pltpu.VMEM) for i, arg in enumerate(args)]
    if sems:
        shapes.append(pltpu.SemaphoreType.DMA((sems,)))
    return pl.pallas_call(
        kernel,
        out_shape=shapes_out,
        in_specs=[hbm] * in_hbm + [vmem] * (len(args) - in_hbm),
        out_specs=[hbm] * out_hbm + [vmem] * (len(outs) - out_hbm),
        scratch_shapes=shapes,
        compiler_params=pltpu.CompilerParams(vmem_limit_bytes=32 * 2**20),
        cost_estimate=cost,
        name=kernel.__name__,
    )(*args)


def local(tangent, velocity, face_frac, branch, basis, design, exit_film):
    cells, rows, lanes = tangent.shape
    radial = velocity.shape[-1]
    dirs = design.shape[1]
    n = cells * rows
    devices = lax.axis_size("az")
    layer, cell_layer = (rows, lanes), (rows, radial)
    z_msg, x_msg, line = (2 * rows + 8, lanes), (3, cells, lanes), (cells, lanes)
    inputs = (tangent, velocity, face_frac, branch, basis, design, exit_film)
    count = (3 * len(EDGE) + 2) * rows
    z_e, z_o, sums = call(
        edge_kernel,
        inputs,
        [(z_msg, F32), (z_msg, F32), ((devices, 2, 128), F32)],
        [
            (tangent.shape, F32), (velocity.shape, F32), (velocity.shape, F32), (cell_layer, F32),
            (velocity.shape, branch.dtype), (cell_layer, branch.dtype), ((len(EDGE) * rows, lanes), BF16),
            (design.shape, BF16), (exit_film.shape, F32), ((len(EDGE) * rows, lanes), BF16),
            ((count, 2 * radial), BF16), ((count, lanes), F32), (layer, F32), ((2, lanes), F32),
            ((2, *layer), F32), ((2, *layer), F32), (layer, F32),
        ],
        in_hbm=7,
        sems=8 + len(EDGE),
    )
    in_e, in_o = swap(z_e, "az", 0), swap(z_o, "az", 1)
    totals = lax.all_to_all(sums, "az", 0, 0)
    velocity_tangent, coef_2, middle, partial, fixed, edges = call(
        local_kernel,
        inputs,
        [
            (basis.shape, BF16), ((6 * n, lanes), F32), ((32, lanes), F32), (tangent.shape, F32), (tangent.shape, F32),
            ((3 * rows + 16, lanes), F32),
        ],
        [
            (tangent.shape, F32), (velocity.shape, F32), (face_frac.shape, F32), (branch.shape, branch.dtype),
            (basis.shape, BF16), (design.shape, BF16), (exit_film.shape, F32), (basis.shape, BF16),
            ((18 * n, 2 * radial), BF16), ((12 * n, lanes), F32), ((6 * n, lanes), F32),
        ],
        in_hbm=7,
        out_hbm=2,
        sems=9,
        cost=pl.CostEstimate(flops=10**9, bytes_accessed=16 * 10**6, transcendentals=0),
    )
    x_e, x_o, film = call(
        middle_kernel, (middle, in_e, in_o), [(x_msg, F32), (x_msg, F32), ((8, 128), F32)], []
    )
    from_o, from_e, film_1 = swap(x_o, "ax", 3), swap(x_e, "ax", 1), swap(film, "ax", 2)
    count = 3 * rows + 16
    out, film_out = call(
        last_kernel,
        (coef_2, partial, fixed, edges, in_e, in_o, film, film_1, from_o, from_e, totals),
        [(tangent.shape, F32), ((cells, dirs // lax.axis_size("ax")), F32)],
        [
            ((count, 2 * radial), BF16), ((count, lanes), F32), (z_msg, F32), (z_msg, F32), (x_msg, F32), (x_msg, F32),
            ((cells + 1, *layer), F32), (line, F32), (tangent.shape, F32), ((6 * n, lanes), F32),
        ],
        in_hbm=1,
        out_hbm=1,
        free=1,
        sems=2 * cells,
    )
    return out, velocity_tangent, film_out


def solution(mesh):
    in_specs = (
        P("az", "ax", None),
        P(None, "az", "ax", None),
        P(None, None, "az", "ax", None),
        P(None, None, "az", "ax", None),
        P(None, "az", "ax", None),
        P(),
        P("az", None),
    )
    out_specs = (P("az", "ax", None), P(None, "az", "ax", None), P("az", "ax"))
    return jax.shard_map(local, mesh=mesh, in_specs=in_specs, out_specs=out_specs, check_vma=False)
```

```python
import jax
import jax.numpy as jnp
from jax import lax
from jax.experimental import pallas as pl
from jax.experimental.pallas import tpu as pltpu
from jax.sharding import PartitionSpec as P

F32, BF16 = jnp.float32, jnp.bfloat16
CHUNK = 256
RADIAL = 64
CELLS = 4
UNROLL = 8
AT_C1, AT_B2, AT_C2, AT_ROW_A, AT_ROW_B, AT_COEF, AT_FIRST, AT_END = 0, 256, 512, 768, 1024, 1280, 1408, 1664


def mix(speed, branch):
    part = speed * (0.25 * branch.astype(F32))
    rest = speed - part
    ahead = speed > 0
    return jnp.where(ahead, rest, part), jnp.where(ahead, part, rest)


def two_terms(values):
    high = values.astype(BF16)
    low = (values - high.astype(F32)).astype(BF16)
    return jnp.concatenate([high, low], axis=-1)


def spreader(offset, lanes, radial, dirs):
    row = lax.broadcasted_iota(jnp.int32, (2 * radial, lanes), 0)
    lane = lax.broadcasted_iota(jnp.int32, (2 * radial, lanes), 1) + offset
    shift = dirs.bit_length() - 1
    return jnp.where((row & (radial - 1)) == (lane >> shift), 1.0, 0.0).astype(BF16)


def spread_all(packed, outs, radial, dirs):
    lanes = outs[0].shape[1]

    @pl.loop(0, lanes // CHUNK, unroll=UNROLL)
    def _(k):
        at = pl.multiple_of(k * CHUNK, CHUNK)
        ones = spreader(at, CHUNK, radial, dirs)
        row = 0
        for out in outs:
            count = out.shape[0]
            left = packed[pl.ds(row, count), :]
            out[:, pl.ds(at, CHUNK)] = jnp.dot(left, ones, preferred_element_type=F32)
            row += count


def blocks_of(design):
    dirs = design.shape[1]
    row = lax.broadcasted_iota(jnp.int32, (CHUNK, dirs), 0)
    col = lax.broadcasted_iota(jnp.int32, (CHUNK, dirs), 1)
    pick = jnp.where((row & (dirs - 1)) == col, 1.0, 0.0).astype(BF16)
    tiled = jnp.dot(pick, design, preferred_element_type=F32).astype(BF16)
    tiled = lax.dot_general(tiled, pick, (((1,), (1,)), ((), ())), preferred_element_type=F32)
    row = lax.broadcasted_iota(jnp.int32, (CHUNK, CHUNK), 0)
    col = lax.broadcasted_iota(jnp.int32, (CHUNK, CHUNK), 1)
    shift = dirs.bit_length() - 1
    return jnp.where((row >> shift) == (col >> shift), tiled, 0.0).astype(BF16)


def wall(radial):
    lane = lax.broadcasted_iota(jnp.int32, (1, radial), 1)
    return jnp.where(lane < radial - 1, 1.0, 0.0)


def ahead_x(rows, last):
    n = rows.shape[0]
    at = lax.broadcasted_iota(jnp.int32, rows.shape, 0)
    return jnp.where(at == n - 1, last, pltpu.roll(rows, n - 1, 0))


def behind_x(rows, first):
    at = lax.broadcasted_iota(jnp.int32, rows.shape, 0)
    return jnp.where(at == 0, first, pltpu.roll(rows, 1, 0))


def ahead_r(rows, dirs):
    return pltpu.roll(rows, rows.shape[1] - dirs, 1)


def behind_r(rows, dirs):
    return pltpu.roll(rows, dirs, 1)


def even_az():
    return lax.rem(lax.axis_index("az"), 2) == 0


def radial_weights(radial):
    return (lax.broadcasted_iota(jnp.int32, (1, radial), 1).astype(F32) + 0.5) / radial


EDGE = ((0, 0), (0, 2), (0, 3), (1, 0), (1, 3), (2, 0), (2, 3))


def edge_kernel(
    tangent, velocity, frac, branch, basis, design, exit_film,
    msg_e, msg_o, sums,
    field, vel, share, share_2, kind, kind_2, left, mat, film, vel_tan, packed, spread, work, ends, edge, faces, face_a, sems,
):
    cells, rows, lanes = field.shape
    radial = vel.shape[-1]
    dirs = lanes // radial
    last, end = cells - 1, rows - 1
    inner = wall(radial)
    pairs = [
        (exit_film, film), (velocity, vel), (branch.at[0], kind), (frac.at[0], share), (frac.at[1, 0, last], share_2),
        (branch.at[1, 0, last], kind_2), (design, mat), (tangent, field),
    ]
    copies = [pltpu.make_async_copy(src, dst, sems.at[i]) for i, (src, dst) in enumerate(pairs)]
    base = len(copies)
    copies += [
        pltpu.make_async_copy(basis.at[c, a], left.at[pl.ds(i * rows, rows)], sems.at[base + i])
        for i, (c, a) in enumerate(EDGE)
    ]
    for copy in copies:
        copy.start()
    copies[0].wait()
    sums[...] = jnp.full(sums.shape, jnp.sum(film[...] * radial_weights(radial)), F32)
    for copy in copies[1:6]:
        copy.wait()

    at = {}
    row = 0
    for c, a in EDGE:
        low, high = mix(vel[c, a], kind[c, a])
        if (c, a) == (0, last):
            high_a = high
        if c == 1:
            at["high", a] = high
        for name, part in zip("plh", (share[c, a], low, high), strict=True):
            packed[pl.ds(row, rows), :] = two_terms(part * inner if c == 2 else part)
            at[name, c, a] = row
            row += rows
    low_2, high_2 = mix(vel[0, last], kind_2[...])
    for name, part in zip("pl", (share_2[...], low_2), strict=True):
        packed[pl.ds(row, rows), :] = two_terms(part)
        at[name] = row
        row += rows
    spread_all(packed, [spread], radial, dirs)

    for copy in copies[6:]:
        copy.wait()
    weights = blocks_of(mat[...])

    @pl.loop(0, lanes // CHUNK, unroll=UNROLL)
    def _(k):
        lane = pl.ds(pl.multiple_of(k * CHUNK, CHUNK), CHUNK)
        vel_tan[:, lane] = jnp.dot(left[:, lane], weights, preferred_element_type=F32).astype(BF16)

    def sp(*key):
        return spread[pl.ds(at[key], rows), :]

    def speed(c, a):
        return vel_tan[pl.ds(EDGE.index((c, a)) * rows, rows), :].astype(F32)

    def along_az(a):
        f = field[a]
        face = speed(0, a) * sp("p", 0, a) + sp("l", 0, a) * f
        return face if a == last else face + sp("h", 0, a) * field[a + 1]

    faces[0] = along_az(0)
    faces[1] = along_az(last - 1)
    face_a[...] = along_az(last)
    for i, a in enumerate((0, last)):
        f = field[a]
        change = faces[0] if a == 0 else face_a[...] - faces[1]
        face = speed(1, a) * sp("p", 1, a) + sp("l", 1, a) * f + sp("h", 1, a) * ahead_x(f, 0.0)
        ends[pl.ds(i, 1), :] = face[end:, :]
        change = change + (face - behind_x(face, 0.0))
        face = speed(2, a) * sp("p", 2, a) + sp("l", 2, a) * f + sp("h", 2, a) * ahead_r(f, dirs)
        change = change + (face - behind_r(face, dirs))
        edge[i] = f - change
    work[...] = speed(0, last) * spread[pl.ds(at["p"], rows), :] + spread[pl.ds(at["l"], rows), :] * edge[1]

    def small_rows(msg, lane, block):
        for k in range(lanes // CHUNK):
            msg[pl.ds(2 * rows + k, 1), pl.ds(lane, CHUNK)] = block[:, k * CHUNK:(k + 1) * CHUNK]

    def halves(msg, lane, block):
        for k in range(rows // 8):
            msg[pl.ds(2 * rows, 8), pl.ds(lane + 128 * k, radial)] = block[8 * k:8 * k + 8]

    def fill(up_msg, down_msg):
        for msg in (up_msg, down_msg):
            msg[pl.ds(2 * rows, 8), :] = jnp.zeros((8, lanes), F32)
        up_msg[pl.ds(0, rows), :] = face_a[...]
        up_msg[pl.ds(rows, rows), :] = work[...]
        halves(up_msg, AT_C1, high_a)
        halves(up_msg, AT_B2, low_2)
        halves(up_msg, AT_C2, high_2)
        small_rows(up_msg, AT_ROW_A, ends[pl.ds(1, 1), :])
        small_rows(up_msg, AT_ROW_B, field[last, pl.ds(0, 1), :])
        small_rows(up_msg, AT_FIRST, sp("h", 0, last)[0:1])
        small_rows(up_msg, AT_END, sp("h", 0, last)[end:])
        up_msg[pl.ds(2 * rows, 1), pl.ds(AT_COEF, radial)] = at["high", last][end:, :]
        down_msg[pl.ds(0, rows), :] = field[0]
        down_msg[pl.ds(rows, rows), :] = edge[0]
        small_rows(down_msg, AT_ROW_A, ends[pl.ds(0, 1), :])
        down_msg[pl.ds(2 * rows, 1), pl.ds(AT_COEF, radial)] = at["high", 0][end:, :]

    even = even_az()

    @pl.when(even)
    def _():
        fill(msg_e, msg_o)

    @pl.when(jnp.logical_not(even))
    def _():
        fill(msg_o, msg_e)


MIDDLE = dict(
    ends=0, end_fixed=4, low_end=8, first=12, partial_first=16, partial_end=20, front=24, coef_a=26, coefs=28
)


def local_kernel(
    tangent, velocity, frac, branch, basis, design, exit_film,
    vel_tan, coef_2, middle, partial, fixed, edges, weighted,
    field, vel, share, kind, left, mat, film, product, packed, spread, mixed, sems,
):
    cells, rows, lanes = field.shape
    radial = vel.shape[-1]
    dirs = lanes // radial
    n = cells * rows
    last, end = cells - 1, rows - 1
    inner = wall(radial)
    pairs = [
        (velocity, vel), (branch, kind), (frac, share), (design, mat), (basis, left), (tangent, field), (exit_film, film),
    ]
    copies = [pltpu.make_async_copy(src, dst, sems.at[i]) for i, (src, dst) in enumerate(pairs)]
    for copy in copies:
        copy.start()
    for copy in copies[:3]:
        copy.wait()

    for step in range(2):
        for c in range(3):
            low, high = mix(vel[c], kind[step, c])
            for k, part in enumerate((share[step, c], low, high)):
                part = part.reshape(n, radial)
                part = two_terms(part * inner if c == 2 else part)
                if step == 0 or k == 0:
                    packed[pl.ds(((step * 3 + k) * 3 + c) * n, n), :] = part
                else:
                    for a in range(cells):
                        row = 12 * n + ((a * 2 + k - 1) * 3 + c) * rows
                        packed[pl.ds(row, rows), :] = part[a * rows:(a + 1) * rows]
            if c == 1:
                segments = [(0, high)] if step == 0 else [(6, low), (10, high)]
                if step == 0:
                    middle[pl.ds(MIDDLE["coefs"], 1), :] = jnp.zeros((1, lanes), F32)
                for start, part in segments:
                    for a in range(cells):
                        middle[pl.ds(MIDDLE["coefs"], 1), pl.ds(128 * (start + a), radial)] = part[a, end:, :]
    spread_all(packed, [spread, mixed], radial, dirs)
    done = [pltpu.make_async_copy(mixed, coef_2, sems.at[len(copies) + 1])]
    done[0].start()
    for copy in copies[3:5]:
        copy.wait()
    weights = blocks_of(mat[...])

    @pl.loop(0, lanes // CHUNK, unroll=UNROLL)
    def _(k):
        lane = pl.ds(pl.multiple_of(k * CHUNK, CHUNK), CHUNK)
        block = jnp.dot(left[:, :, :, lane].reshape(3 * n, CHUNK), weights, preferred_element_type=F32)
        product[:, :, :, lane] = block.astype(BF16).reshape(3, cells, rows, CHUNK)

    done.append(pltpu.make_async_copy(product, vel_tan, sems.at[len(copies)]))
    done[-1].start()
    for copy in copies[5:]:
        copy.wait()

    def sp(k, c, a):
        return spread[pl.ds((k * 3 + c) * n + a * rows, rows), :]

    def speed(c, a):
        return product[c, a].astype(F32)

    def put(name, a, block):
        middle[pl.ds(MIDDLE[name] + a, block.shape[0]), :] = block

    before = before_2 = None
    for a in range(cells):
        f = field[a]
        here = speed(0, a) * sp(0, 0, a) + sp(1, 0, a) * f
        if a < last:
            here = here + sp(2, 0, a) * field[a + 1]
        change = here if before is None else here - before
        before = here
        face = speed(1, a) * sp(0, 1, a) + sp(1, 1, a) * f + sp(2, 1, a) * ahead_x(f, 0.0)
        put("ends", a, face[end:])
        edges[pl.ds(2 * rows + a, 1), :] = face[end:]
        change = change + (face - behind_x(face, 0.0))
        face = speed(2, a) * sp(0, 2, a) + sp(1, 2, a) * f + sp(2, 2, a) * ahead_r(f, dirs)
        change = change + (face - behind_r(face, dirs))
        block = f - change
        partial[a] = block
        put("first", a, f[0:1])
        edges[pl.ds(2 * rows + 4 + a, 1), :] = f[0:1]
        put("partial_first", a, block[0:1])
        put("partial_end", a, block[end:])
        put("low_end", a, mixed[pl.ds((a * 6 + 1) * rows + end, 1), :])
        edges[pl.ds(2 * rows + 8 + a, 1), :] = sp(2, 1, a)[end:]
        here_2 = speed(0, a) * sp(3, 0, a)
        change = here_2 if before_2 is None else here_2 - before_2
        before_2 = here_2
        face = speed(1, a) * sp(3, 1, a)
        put("end_fixed", a, face[end:])
        change = change + (face - behind_x(face, 0.0))
        face = speed(2, a) * sp(3, 2, a)
        fixed[a] = change + (face - behind_r(face, dirs))
    edges[pl.ds(0, rows), :] = before
    edges[pl.ds(2 * rows + 16, rows), :] = field[0]
    edges[pl.ds(rows, rows), :] = sp(2, 0, last)
    for k, x in enumerate((0, end)):
        put("front", k, field[0, pl.ds(x, 1), :])
        put("coef_a", k, sp(2, 0, last)[x:x + 1])
    row_film = jnp.sum(film[...] * radial_weights(radial), axis=1, keepdims=True)
    weighted[...] = jnp.broadcast_to(row_film, weighted.shape)
    edges[pl.ds(2 * rows + 12, 4), :] = jnp.zeros((4, lanes), F32)
    for copy in done:
        copy.wait()


def gathered_row(msg, row, lane, lanes):
    return jnp.concatenate([msg[pl.ds(row + k, 1), pl.ds(lane, CHUNK)] for k in range(lanes // CHUNK)], axis=1)


def middle_kernel(
    middle, in_e, in_o,
    msg_e, msg_o, film_msg,
):
    cells, rows, lanes = CELLS, (in_e.shape[0] - 8) // 2, in_e.shape[1]
    radial, dirs = RADIAL, lanes // RADIAL
    last, end = cells - 1, rows - 1

    def take(name, count=CELLS, at=0):
        return middle[pl.ds(MIDDLE[name] + at, count), :]

    even = even_az()

    def work(up, down, out_up, out_down):
        at_a = lax.broadcasted_iota(jnp.int32, (cells, 1), 0)
        partial_x = []
        for k, (x, lane, name) in enumerate(((0, AT_FIRST, "partial_first"), (end, AT_END, "partial_end"))):
            face = up[pl.ds(x, 1), :] + gathered_row(up, 2 * rows, lane, lanes) * take("front", 1, k)
            beyond = take("coef_a", 1, k) * down[pl.ds(x, 1), :]
            partial_x.append(take(name) + jnp.where(at_a == 0, face, 0.0) - jnp.where(at_a == last, beyond, 0.0))
        second = take("end_fixed") + take("low_end") * partial_x[1]

        lane = lax.broadcasted_iota(jnp.int32, (1, lanes), 1)
        weight = ((lane // dirs).astype(F32) + 0.5) / radial
        raw = (take("ends") + second) * weight
        film = raw[:, 0:128]
        for k in range(1, lanes // 128):
            film = film + raw[:, 128 * k:128 * k + 128]
        shift = 64
        while shift >= dirs:
            film = film + pltpu.roll(film, shift, 1)
            shift //= 2
        film_msg[...] = jnp.zeros(film_msg.shape, F32)
        film_msg[pl.ds(0, cells), :] = film

        def finish(up_msg, down_msg):
            for msg in (up_msg, down_msg):
                msg[1, pl.ds(2, 2), :] = jnp.zeros((2, lanes), F32)
                for a in range(cells):
                    msg[1, pl.ds(3, 1), pl.ds(128 * a, 128)] = film[a:a + 1]
            up_msg[0] = take("ends")
            up_msg[1, pl.ds(0, 1), :] = gathered_row(up, 2 * rows, AT_ROW_A, lanes)
            up_msg[1, pl.ds(1, 1), :] = gathered_row(down, 2 * rows, AT_ROW_A, lanes)
            up_msg[1, pl.ds(2, 1), :] = take("coefs", 1)
            up_msg[1, pl.ds(2, 1), pl.ds(128 * 4, radial)] = up[pl.ds(2 * rows, 1), pl.ds(AT_COEF, radial)]
            up_msg[1, pl.ds(2, 1), pl.ds(128 * 5, radial)] = down[pl.ds(2 * rows, 1), pl.ds(AT_COEF, radial)]
            up_msg[2] = second
            down_msg[0] = take("first")
            down_msg[1, pl.ds(0, 1), :] = gathered_row(up, 2 * rows, AT_ROW_B, lanes)
            down_msg[1, pl.ds(1, 1), :] = down[pl.ds(0, 1), :]
            down_msg[2] = partial_x[0]

        even_x = lax.rem(lax.axis_index("ax"), 2) == 0

        @pl.when(even_x)
        def _():
            finish(out_up, out_down)

        @pl.when(jnp.logical_not(even_x))
        def _():
            finish(out_down, out_up)

    @pl.when(even)
    def _():
        work(in_o, in_e, msg_e, msg_o)

    @pl.when(jnp.logical_not(even))
    def _():
        work(in_e, in_o, msg_e, msg_o)


def last_kernel(
    coef_2, partial, fixed, edges, in_e, in_o, x_o, x_e,
    out,
    packed, spread, up, down, below, above, now, edge, result, mixed, sems,
):
    cells, rows, lanes = partial.shape
    radial = packed.shape[1] // 2
    dirs = lanes // radial
    n = cells * rows
    last, end = cells - 1, rows - 1
    even = even_az()
    place = lax.axis_index("ax")
    even_x = lax.rem(place, 2) == 0
    final = lax.axis_size("ax") - 1
    layer = 6 * rows
    loads = [
        pltpu.make_async_copy(coef_2.at[pl.ds(a * layer, layer)], mixed.at[pl.ds(a * layer, layer)], sems.at[cells + a])
        for a in range(cells)
    ]
    for copy in loads:
        copy.start()

    @pl.when(even)
    def _():
        up[...] = in_o[...]
        down[...] = in_e[...]

    @pl.when(jnp.logical_not(even))
    def _():
        up[...] = in_e[...]
        down[...] = in_o[...]

    @pl.when(even_x)
    def _():
        below[...] = jnp.where(place == 0, 0.0, x_o[...])
        above[...] = x_e[...]

    @pl.when(jnp.logical_not(even_x))
    def _():
        below[...] = x_e[...]
        above[...] = jnp.where(place == final, 0.0, x_o[...])

    face_a, coef_a = edges[pl.ds(0, rows), :], edges[pl.ds(rows, rows), :]
    ends, first, coef_x = (edges[pl.ds(2 * rows + 4 * k, cells), :] for k in range(3))

    def joined(msg, lane):
        return jnp.concatenate([msg[pl.ds(2 * rows, 8), pl.ds(lane + 128 * k, radial)] for k in range(rows // 8)], axis=0)

    for k, lane in enumerate((AT_C1, AT_B2, AT_C2)):
        packed[pl.ds(k * rows, rows), :] = two_terms(joined(up, lane))
    singles = [below[1, pl.ds(2, 1), pl.ds(128 * k, radial)] for k in range(14)]
    singles += [msg[pl.ds(2 * rows, 1), pl.ds(AT_COEF, radial)] for msg in (up, down)]
    packed[pl.ds(3 * rows, 16), :] = two_terms(jnp.concatenate(singles, axis=0))
    spread_all(packed, [spread], radial, dirs)
    in_c1, in_b2, in_c2 = (spread[pl.ds(k * rows, rows), :] for k in range(3))
    below_c = spread[pl.ds(3 * rows, 6), :]
    below_b2, below_c2 = spread[pl.ds(3 * rows + 6, 4), :], spread[pl.ds(3 * rows + 10, 4), :]
    own_c = jnp.concatenate([coef_x, spread[pl.ds(3 * rows + 14, 2), :]], axis=0)

    starts = jnp.concatenate([first, gathered_row(up, 2 * rows, AT_ROW_B, lanes), down[pl.ds(0, 1), :]], axis=0)
    enter = jnp.concatenate([below[0], below[1, pl.ds(0, 2), :]], axis=0) + below_c * starts
    leave = own_c * jnp.concatenate([above[0], above[1, pl.ds(0, 2), :]], axis=0)
    crossing = in_c1 * edges[pl.ds(2 * rows + 16, rows), :]
    beyond = coef_a * down[pl.ds(0, rows), :]
    at_x = lax.broadcasted_iota(jnp.int32, (rows, 1), 0)

    def with_edges(block, k):
        return block + jnp.where(at_x == 0, enter[k:k + 1], 0.0) - jnp.where(at_x == end, leave[k:k + 1], 0.0)

    for a in range(cells):
        f = partial[a]
        if a == 0:
            f = f + up[pl.ds(0, rows), :] + crossing
        if a == last:
            f = f - beyond
        now[a] = with_edges(f, a)
    now[cells] = with_edges(down[pl.ds(rows, rows), :] + face_a + beyond, 5)
    lower = up[pl.ds(rows, rows), :] + in_b2 * (
        jnp.where(at_x == 0, enter[4:5], 0.0) - jnp.where(at_x == end, leave[4:5], 0.0) - crossing
    )
    before = lower + in_c2 * now[0]

    first_now = jnp.concatenate([now[a, pl.ds(0, 1), :] for a in range(cells)], axis=0)
    enter_2 = below[2] - below_b2 * (below_c[0:4] * first) + below_c2 * first_now
    inside = jnp.where(place == final, 0.0, 1.0)
    edge[...] = inside * (above[2] + ends + leave[0:4])

    def low(c, a):
        return mixed[pl.ds((a * 6 + c) * rows, rows), :]

    def high(c, a):
        return mixed[pl.ds((a * 6 + 3 + c) * rows, rows), :]

    copies = []
    for a in range(cells):
        loads[a].wait()
        f = now[a]
        face = low(0, a) * f + high(0, a) * now[a + 1]
        change = fixed[a] + (face - before)
        before = face
        face = low(1, a) * f + high(1, a) * ahead_x(f, edge[pl.ds(a, 1), :])
        change = change + (face - behind_x(face, enter_2[a:a + 1]))
        face = low(2, a) * f + high(2, a) * ahead_r(f, dirs)
        change = change + (face - behind_r(face, dirs))
        result[a] = f - change
        copies.append(pltpu.make_async_copy(result.at[a], out.at[a], sems.at[a]))
        copies[a].start()

    for copy in copies:
        copy.wait()


def film_kernel(done, row_film, film_own, film_1, x_o, x_e, totals, film_out):
    del done
    cells, share = film_out.shape
    place = lax.axis_index("ax")
    mean = jnp.sum(totals[:, 0:1, :], axis=0) / (cells * totals.shape[0])
    factor = mean / row_film[...]
    for k, source in enumerate((x_o, film_1, x_e, film_own)):

        @pl.when(place == k)
        def _():
            if len(source.shape) == 2:
                film = source[pl.ds(0, cells), :]
            else:
                film = jnp.concatenate([source[1, pl.ds(3, 1), pl.ds(128 * a, 128)] for a in range(cells)], axis=0)
            film_out[...] = (film * factor)[:, k * share:(k + 1) * share]


def swap(value, axis, pairing):
    count = lax.axis_size(axis)
    if axis == "ax":
        other = [i ^ pairing for i in range(count)]
    elif pairing == 0:
        other = [i ^ 1 for i in range(count)]
    else:
        other = [(i - 1 if i % 2 == 0 else i + 1) % count for i in range(count)]
    return lax.ppermute(value, axis, list(enumerate(other)))


def pinned(value, space):
    return pltpu.with_memory_space_constraint(value, space)


def placed(space, shape, dtype):
    return space(shape, dtype)


def call(kernel, args, outs, scratch, in_hbm=0, out_hbm=0, free=0, sems=0, cost=None):
    vmem, hbm = pl.BlockSpec(memory_space=pltpu.VMEM), pl.BlockSpec(memory_space=pl.ANY)
    shapes = [pltpu.VMEM(shape, dtype) for shape, dtype in scratch]
    pinned_outs = len(outs) - free
    shapes_out = [placed(pltpu.HBM if i < out_hbm else pltpu.VMEM, *out) for i, out in enumerate(outs[:pinned_outs])]
    shapes_out += [jax.ShapeDtypeStruct(*out) for out in outs[pinned_outs:]]
    args = [pinned(arg, pltpu.HBM if i < in_hbm else pltpu.VMEM) for i, arg in enumerate(args)]
    if sems:
        shapes.append(pltpu.SemaphoreType.DMA((sems,)))
    return pl.pallas_call(
        kernel,
        out_shape=shapes_out,
        in_specs=[hbm] * in_hbm + [vmem] * (len(args) - in_hbm),
        out_specs=[hbm] * out_hbm + [vmem] * (len(outs) - out_hbm),
        scratch_shapes=shapes,
        compiler_params=pltpu.CompilerParams(vmem_limit_bytes=32 * 2**20),
        cost_estimate=cost,
        name=kernel.__name__,
    )(*args)


def local(tangent, velocity, face_frac, branch, basis, design, exit_film):
    cells, rows, lanes = tangent.shape
    radial = velocity.shape[-1]
    dirs = design.shape[1]
    n = cells * rows
    devices = lax.axis_size("az")
    layer, cell_layer = (rows, lanes), (rows, radial)
    z_msg, x_msg, line = (2 * rows + 8, lanes), (3, cells, lanes), (cells, lanes)
    inputs = (tangent, velocity, face_frac, branch, basis, design, exit_film)
    count = (3 * len(EDGE) + 2) * rows
    z_e, z_o, sums = call(
        edge_kernel,
        inputs,
        [(z_msg, F32), (z_msg, F32), ((devices, 2, 128), F32)],
        [
            (tangent.shape, F32), (velocity.shape, F32), (velocity.shape, F32), (cell_layer, F32),
            (velocity.shape, branch.dtype), (cell_layer, branch.dtype), ((len(EDGE) * rows, lanes), BF16),
            (design.shape, BF16), (exit_film.shape, F32), ((len(EDGE) * rows, lanes), BF16),
            ((count, 2 * radial), BF16), ((count, lanes), F32), (layer, F32), ((2, lanes), F32),
            ((2, *layer), F32), ((2, *layer), F32), (layer, F32),
        ],
        in_hbm=7,
        sems=8 + len(EDGE),
    )
    in_e, in_o = swap(z_e, "az", 0), swap(z_o, "az", 1)
    totals = lax.all_to_all(sums, "az", 0, 0)
    velocity_tangent, coef_2, middle, partial, fixed, edges, row_film = call(
        local_kernel,
        inputs,
        [
            (basis.shape, BF16), ((6 * n, lanes), F32), ((32, lanes), F32), (tangent.shape, F32), (tangent.shape, F32),
            ((3 * rows + 16, lanes), F32), ((cells, 128), F32),
        ],
        [
            (tangent.shape, F32), (velocity.shape, F32), (face_frac.shape, F32), (branch.shape, branch.dtype),
            (basis.shape, BF16), (design.shape, BF16), (exit_film.shape, F32), (basis.shape, BF16),
            ((18 * n, 2 * radial), BF16), ((12 * n, lanes), F32), ((6 * n, lanes), F32),
        ],
        in_hbm=7,
        out_hbm=2,
        sems=9,
        cost=pl.CostEstimate(flops=10**9, bytes_accessed=16 * 10**6, transcendentals=0),
    )
    x_e, x_o, film = call(
        middle_kernel, (middle, in_e, in_o), [(x_msg, F32), (x_msg, F32), ((8, 128), F32)], []
    )
    from_o, from_e, film_1 = swap(x_o, "ax", 3), swap(x_e, "ax", 1), swap(film, "ax", 2)
    count = 3 * rows + 16
    (out,) = call(
        last_kernel,
        (coef_2, partial, fixed, edges, in_e, in_o, from_o, from_e),
        [(tangent.shape, F32)],
        [
            ((count, 2 * radial), BF16), ((count, lanes), F32), (z_msg, F32), (z_msg, F32), (x_msg, F32), (x_msg, F32),
            ((cells + 1, *layer), F32), (line, F32), (tangent.shape, F32), ((6 * n, lanes), F32),
        ],
        in_hbm=1,
        out_hbm=1,
        sems=2 * cells,
    )
    (film_out,) = call(
        film_kernel,
        (out, row_film, film, film_1, from_o, from_e, totals),
        [((cells, dirs // lax.axis_size("ax")), F32)],
        [],
        in_hbm=1,
        free=1,
    )
    return out, velocity_tangent, film_out


def solution(mesh):
    in_specs = (
        P("az", "ax", None),
        P(None, "az", "ax", None),
        P(None, None, "az", "ax", None),
        P(None, None, "az", "ax", None),
        P(None, "az", "ax", None),
        P(),
        P("az", None),
    )
    out_specs = (P("az", "ax", None), P(None, "az", "ax", None), P("az", "ax"))
    return jax.shard_map(local, mesh=mesh, in_specs=in_specs, out_specs=out_specs, check_vma=False)
```

```python
import jax
import jax.numpy as jnp
from jax import lax
from jax.experimental import pallas as pl
from jax.experimental.pallas import tpu as pltpu
from jax.sharding import PartitionSpec as P

F32, BF16 = jnp.float32, jnp.bfloat16
CHUNK = 256
RADIAL = 64
CELLS = 4
UNROLL = 8
AT_C1, AT_B2, AT_C2, AT_ROW_A, AT_ROW_B, AT_COEF, AT_FIRST, AT_END = 0, 256, 512, 768, 1024, 1280, 1408, 1664


def mix(speed, branch):
    part = speed * (0.25 * branch.astype(F32))
    rest = speed - part
    ahead = speed > 0
    return jnp.where(ahead, rest, part), jnp.where(ahead, part, rest)


def two_terms(values):
    high = values.astype(BF16)
    low = (values - high.astype(F32)).astype(BF16)
    return jnp.concatenate([high, low], axis=-1)


def spreader(offset, lanes, radial, dirs):
    row = lax.broadcasted_iota(jnp.int32, (2 * radial, lanes), 0)
    lane = lax.broadcasted_iota(jnp.int32, (2 * radial, lanes), 1) + offset
    shift = dirs.bit_length() - 1
    return jnp.where((row & (radial - 1)) == (lane >> shift), 1.0, 0.0).astype(BF16)


def spread_all(packed, outs, radial, dirs):
    lanes = outs[0].shape[1]

    @pl.loop(0, lanes // CHUNK, unroll=UNROLL)
    def _(k):
        at = pl.multiple_of(k * CHUNK, CHUNK)
        ones = spreader(at, CHUNK, radial, dirs)
        row = 0
        for out in outs:
            count = out.shape[0]
            left = packed[pl.ds(row, count), :]
            out[:, pl.ds(at, CHUNK)] = jnp.dot(left, ones, preferred_element_type=F32)
            row += count


def blocks_of(design):
    dirs = design.shape[1]
    row = lax.broadcasted_iota(jnp.int32, (CHUNK, dirs), 0)
    col = lax.broadcasted_iota(jnp.int32, (CHUNK, dirs), 1)
    pick = jnp.where((row & (dirs - 1)) == col, 1.0, 0.0).astype(BF16)
    tiled = jnp.dot(pick, design, preferred_element_type=F32).astype(BF16)
    tiled = lax.dot_general(tiled, pick, (((1,), (1,)), ((), ())), preferred_element_type=F32)
    row = lax.broadcasted_iota(jnp.int32, (CHUNK, CHUNK), 0)
    col = lax.broadcasted_iota(jnp.int32, (CHUNK, CHUNK), 1)
    shift = dirs.bit_length() - 1
    return jnp.where((row >> shift) == (col >> shift), tiled, 0.0).astype(BF16)


def wall(radial):
    lane = lax.broadcasted_iota(jnp.int32, (1, radial), 1)
    return jnp.where(lane < radial - 1, 1.0, 0.0)


def ahead_x(rows, last):
    n = rows.shape[0]
    at = lax.broadcasted_iota(jnp.int32, rows.shape, 0)
    return jnp.where(at == n - 1, last, pltpu.roll(rows, n - 1, 0))


def behind_x(rows, first):
    at = lax.broadcasted_iota(jnp.int32, rows.shape, 0)
    return jnp.where(at == 0, first, pltpu.roll(rows, 1, 0))


def ahead_r(rows, dirs):
    return pltpu.roll(rows, rows.shape[1] - dirs, 1)


def behind_r(rows, dirs):
    return pltpu.roll(rows, dirs, 1)


def even_az():
    return lax.rem(lax.axis_index("az"), 2) == 0


def radial_weights(radial):
    return (lax.broadcasted_iota(jnp.int32, (1, radial), 1).astype(F32) + 0.5) / radial


EDGE = ((0, 0), (0, 2), (0, 3), (1, 0), (1, 3), (2, 0), (2, 3))


def edge_kernel(
    tangent, velocity, frac, branch, basis, design, exit_film,
    msg_e, msg_o, sums,
    field, vel, share, share_2, kind, kind_2, left, mat, film, vel_tan, packed, spread, work, ends, edge, faces, face_a, sems,
):
    cells, rows, lanes = field.shape
    radial = vel.shape[-1]
    dirs = lanes // radial
    last, end = cells - 1, rows - 1
    inner = wall(radial)
    pairs = [
        (exit_film, film), (velocity, vel), (branch.at[0], kind), (frac.at[0], share), (frac.at[1, 0, last], share_2),
        (branch.at[1, 0, last], kind_2), (design, mat), (tangent, field),
    ]
    copies = [pltpu.make_async_copy(src, dst, sems.at[i]) for i, (src, dst) in enumerate(pairs)]
    base = len(copies)
    copies += [
        pltpu.make_async_copy(basis.at[c, a], left.at[pl.ds(i * rows, rows)], sems.at[base + i])
        for i, (c, a) in enumerate(EDGE)
    ]
    for copy in copies:
        copy.start()
    copies[0].wait()
    sums[...] = jnp.full(sums.shape, jnp.sum(film[...] * radial_weights(radial)), F32)
    for copy in copies[1:6]:
        copy.wait()

    at = {}
    row = 0
    for c, a in EDGE:
        low, high = mix(vel[c, a], kind[c, a])
        if (c, a) == (0, last):
            high_a = high
        if c == 1:
            at["high", a] = high
        for name, part in zip("plh", (share[c, a], low, high), strict=True):
            packed[pl.ds(row, rows), :] = two_terms(part * inner if c == 2 else part)
            at[name, c, a] = row
            row += rows
    low_2, high_2 = mix(vel[0, last], kind_2[...])
    for name, part in zip("pl", (share_2[...], low_2), strict=True):
        packed[pl.ds(row, rows), :] = two_terms(part)
        at[name] = row
        row += rows
    spread_all(packed, [spread], radial, dirs)

    for copy in copies[6:]:
        copy.wait()
    weights = blocks_of(mat[...])

    @pl.loop(0, lanes // CHUNK, unroll=UNROLL)
    def _(k):
        lane = pl.ds(pl.multiple_of(k * CHUNK, CHUNK), CHUNK)
        vel_tan[:, lane] = jnp.dot(left[:, lane], weights, preferred_element_type=F32).astype(BF16)

    def sp(*key):
        return spread[pl.ds(at[key], rows), :]

    def speed(c, a):
        return vel_tan[pl.ds(EDGE.index((c, a)) * rows, rows), :].astype(F32)

    def along_az(a):
        f = field[a]
        face = speed(0, a) * sp("p", 0, a) + sp("l", 0, a) * f
        return face if a == last else face + sp("h", 0, a) * field[a + 1]

    faces[0] = along_az(0)
    faces[1] = along_az(last - 1)
    face_a[...] = along_az(last)
    for i, a in enumerate((0, last)):
        f = field[a]
        change = faces[0] if a == 0 else face_a[...] - faces[1]
        face = speed(1, a) * sp("p", 1, a) + sp("l", 1, a) * f + sp("h", 1, a) * ahead_x(f, 0.0)
        ends[pl.ds(i, 1), :] = face[end:, :]
        change = change + (face - behind_x(face, 0.0))
        face = speed(2, a) * sp("p", 2, a) + sp("l", 2, a) * f + sp("h", 2, a) * ahead_r(f, dirs)
        change = change + (face - behind_r(face, dirs))
        edge[i] = f - change
    work[...] = speed(0, last) * spread[pl.ds(at["p"], rows), :] + spread[pl.ds(at["l"], rows), :] * edge[1]

    def small_rows(msg, lane, block):
        for k in range(lanes // CHUNK):
            msg[pl.ds(2 * rows + k, 1), pl.ds(lane, CHUNK)] = block[:, k * CHUNK:(k + 1) * CHUNK]

    def halves(msg, lane, block):
        for k in range(rows // 8):
            msg[pl.ds(2 * rows, 8), pl.ds(lane + 128 * k, radial)] = block[8 * k:8 * k + 8]

    def fill(up_msg, down_msg):
        for msg in (up_msg, down_msg):
            msg[pl.ds(2 * rows, 8), :] = jnp.zeros((8, lanes), F32)
        up_msg[pl.ds(0, rows), :] = face_a[...]
        up_msg[pl.ds(rows, rows), :] = work[...]
        halves(up_msg, AT_C1, high_a)
        halves(up_msg, AT_B2, low_2)
        halves(up_msg, AT_C2, high_2)
        small_rows(up_msg, AT_ROW_A, ends[pl.ds(1, 1), :])
        small_rows(up_msg, AT_ROW_B, field[last, pl.ds(0, 1), :])
        small_rows(up_msg, AT_FIRST, sp("h", 0, last)[0:1])
        small_rows(up_msg, AT_END, sp("h", 0, last)[end:])
        up_msg[pl.ds(2 * rows, 1), pl.ds(AT_COEF, radial)] = at["high", last][end:, :]
        down_msg[pl.ds(0, rows), :] = field[0]
        down_msg[pl.ds(rows, rows), :] = edge[0]
        small_rows(down_msg, AT_ROW_A, ends[pl.ds(0, 1), :])
        down_msg[pl.ds(2 * rows, 1), pl.ds(AT_COEF, radial)] = at["high", 0][end:, :]

    even = even_az()

    @pl.when(even)
    def _():
        fill(msg_e, msg_o)

    @pl.when(jnp.logical_not(even))
    def _():
        fill(msg_o, msg_e)


MIDDLE = dict(
    ends=0, end_fixed=4, low_end=8, first=12, partial_first=16, partial_end=20, front=24, coef_a=26, coefs=28
)


def local_kernel(
    tangent, velocity, frac, branch, basis, design, exit_film,
    vel_tan, middle, partial, edges, row_film,
    field, vel, share, kind, left, mat, film, product, packed, spread, sems,
):
    cells, rows, lanes = field.shape
    radial = vel.shape[-1]
    dirs = lanes // radial
    n = cells * rows
    last, end = cells - 1, rows - 1
    inner = wall(radial)
    pairs = [
        (velocity, vel), (branch, kind), (frac, share), (design, mat), (basis, left), (tangent, field), (exit_film, film),
    ]
    copies = [pltpu.make_async_copy(src, dst, sems.at[i]) for i, (src, dst) in enumerate(pairs)]
    for copy in copies:
        copy.start()
    for copy in copies[:3]:
        copy.wait()

    for c in range(3):
        low, high = mix(vel[c], kind[0, c])
        for k, part in enumerate((share[0, c], low, high)):
            part = part.reshape(n, radial)
            packed[pl.ds((k * 3 + c) * n, n), :] = two_terms(part * inner if c == 2 else part)
        if c == 1:
            high_1 = high
    low_2, high_2 = mix(vel[1], kind[1, 1])
    tail = [share[1, 1, :, end, :], low_2[:, end, :], jnp.zeros((8, radial), F32)]
    packed[pl.ds(9 * n, 16), :] = two_terms(jnp.concatenate(tail, axis=0))
    middle[pl.ds(MIDDLE["coefs"], 1), :] = jnp.zeros((1, lanes), F32)
    for start, part in ((0, high_1), (6, low_2), (10, high_2)):
        for a in range(cells):
            middle[pl.ds(MIDDLE["coefs"], 1), pl.ds(128 * (start + a), radial)] = part[a, end:, :]
    spread_all(packed, [spread], radial, dirs)
    for copy in copies[3:5]:
        copy.wait()
    weights = blocks_of(mat[...])

    @pl.loop(0, lanes // CHUNK, unroll=UNROLL)
    def _(k):
        lane = pl.ds(pl.multiple_of(k * CHUNK, CHUNK), CHUNK)
        block = jnp.dot(left[:, :, :, lane].reshape(3 * n, CHUNK), weights, preferred_element_type=F32)
        product[:, :, :, lane] = block.astype(BF16).reshape(3, cells, rows, CHUNK)

    output = pltpu.make_async_copy(product, vel_tan, sems.at[len(copies)])
    output.start()
    for copy in copies[5:]:
        copy.wait()

    def sp(k, c, a):
        return spread[pl.ds((k * 3 + c) * n + a * rows, rows), :]

    def speed(c, a):
        return product[c, a].astype(F32)

    def put(name, a, block):
        middle[pl.ds(MIDDLE[name] + a, block.shape[0]), :] = block

    before = None
    for a in range(cells):
        f = field[a]
        here = speed(0, a) * sp(0, 0, a) + sp(1, 0, a) * f
        if a < last:
            here = here + sp(2, 0, a) * field[a + 1]
        change = here if before is None else here - before
        before = here
        speed_x = speed(1, a)
        face = speed_x * sp(0, 1, a) + sp(1, 1, a) * f + sp(2, 1, a) * ahead_x(f, 0.0)
        put("ends", a, face[end:])
        edges[pl.ds(2 * rows + a, 1), :] = face[end:]
        change = change + (face - behind_x(face, 0.0))
        face = speed(2, a) * sp(0, 2, a) + sp(1, 2, a) * f + sp(2, 2, a) * ahead_r(f, dirs)
        change = change + (face - behind_r(face, dirs))
        block = f - change
        partial[a] = block
        put("first", a, f[0:1])
        edges[pl.ds(2 * rows + 4 + a, 1), :] = f[0:1]
        put("partial_first", a, block[0:1])
        put("partial_end", a, block[end:])
        put("low_end", a, spread[pl.ds(9 * n + cells + a, 1), :])
        put("end_fixed", a, speed_x[end:] * spread[pl.ds(9 * n + a, 1), :])
        edges[pl.ds(2 * rows + 8 + a, 1), :] = sp(2, 1, a)[end:]
    edges[pl.ds(0, rows), :] = before
    edges[pl.ds(2 * rows + 12, 4), :] = jnp.zeros((4, lanes), F32)
    edges[pl.ds(2 * rows + 16, rows), :] = field[0]
    edges[pl.ds(rows, rows), :] = sp(2, 0, last)
    for k, x in enumerate((0, end)):
        put("front", k, field[0, pl.ds(x, 1), :])
        put("coef_a", k, sp(2, 0, last)[x:x + 1])
    total = jnp.sum(film[...] * radial_weights(radial), axis=1, keepdims=True)
    row_film[...] = jnp.broadcast_to(total, row_film.shape)
    output.wait()


def step_kernel(
    velocity, frac, branch, vel_tan, after,
    coef_2, fixed,
    vel, share, kind, product, packed, spread, mixed, sems,
):
    del after
    _, cells, rows, lanes = product.shape
    radial = vel.shape[-1]
    dirs = lanes // radial
    n = cells * rows
    inner = wall(radial)
    pairs = [(velocity, vel), (branch.at[1], kind), (frac.at[1], share), (vel_tan, product)]
    copies = [pltpu.make_async_copy(src, dst, sems.at[i]) for i, (src, dst) in enumerate(pairs)]
    for copy in copies:
        copy.start()
    for copy in copies[:3]:
        copy.wait()
    for c in range(3):
        for k, part in enumerate((share[c], *mix(vel[c], kind[c]))):
            part = part.reshape(n, radial)
            part = two_terms(part * inner if c == 2 else part)
            if k == 0:
                packed[pl.ds(c * n, n), :] = part
                continue
            for a in range(cells):
                row = 3 * n + ((a * 2 + k - 1) * 3 + c) * rows
                packed[pl.ds(row, rows), :] = part[a * rows:(a + 1) * rows]
    spread_all(packed, [spread, mixed], radial, dirs)
    output = pltpu.make_async_copy(mixed, coef_2, sems.at[len(copies)])
    output.start()
    copies[3].wait()
    before = None
    for a in range(cells):
        faces = [product[c, a].astype(F32) * spread[pl.ds(c * n + a * rows, rows), :] for c in range(3)]
        change = faces[0] if before is None else faces[0] - before
        before = faces[0]
        change = change + (faces[1] - behind_x(faces[1], 0.0))
        fixed[a] = change + (faces[2] - behind_r(faces[2], dirs))
    output.wait()


def gathered_row(msg, row, lane, lanes):
    return jnp.concatenate([msg[pl.ds(row + k, 1), pl.ds(lane, CHUNK)] for k in range(lanes // CHUNK)], axis=1)


def middle_kernel(
    middle, in_e, in_o,
    msg_e, msg_o, film_msg,
):
    cells, rows, lanes = CELLS, (in_e.shape[0] - 8) // 2, in_e.shape[1]
    radial, dirs = RADIAL, lanes // RADIAL
    last, end = cells - 1, rows - 1

    def take(name, count=CELLS, at=0):
        return middle[pl.ds(MIDDLE[name] + at, count), :]

    even = even_az()

    def work(up, down, out_up, out_down):
        at_a = lax.broadcasted_iota(jnp.int32, (cells, 1), 0)
        partial_x = []
        for k, (x, lane, name) in enumerate(((0, AT_FIRST, "partial_first"), (end, AT_END, "partial_end"))):
            face = up[pl.ds(x, 1), :] + gathered_row(up, 2 * rows, lane, lanes) * take("front", 1, k)
            beyond = take("coef_a", 1, k) * down[pl.ds(x, 1), :]
            partial_x.append(take(name) + jnp.where(at_a == 0, face, 0.0) - jnp.where(at_a == last, beyond, 0.0))
        second = take("end_fixed") + take("low_end") * partial_x[1]

        lane = lax.broadcasted_iota(jnp.int32, (1, lanes), 1)
        weight = ((lane // dirs).astype(F32) + 0.5) / radial
        raw = (take("ends") + second) * weight
        film = raw[:, 0:128]
        for k in range(1, lanes // 128):
            film = film + raw[:, 128 * k:128 * k + 128]
        shift = 64
        while shift >= dirs:
            film = film + pltpu.roll(film, shift, 1)
            shift //= 2
        film_msg[...] = jnp.zeros(film_msg.shape, F32)
        film_msg[pl.ds(0, cells), :] = film

        def finish(up_msg, down_msg):
            for msg in (up_msg, down_msg):
                msg[1, pl.ds(2, 2), :] = jnp.zeros((2, lanes), F32)
                for a in range(cells):
                    msg[1, pl.ds(3, 1), pl.ds(128 * a, 128)] = film[a:a + 1]
            up_msg[0] = take("ends")
            up_msg[1, pl.ds(0, 1), :] = gathered_row(up, 2 * rows, AT_ROW_A, lanes)
            up_msg[1, pl.ds(1, 1), :] = gathered_row(down, 2 * rows, AT_ROW_A, lanes)
            up_msg[1, pl.ds(2, 1), :] = take("coefs", 1)
            up_msg[1, pl.ds(2, 1), pl.ds(128 * 4, radial)] = up[pl.ds(2 * rows, 1), pl.ds(AT_COEF, radial)]
            up_msg[1, pl.ds(2, 1), pl.ds(128 * 5, radial)] = down[pl.ds(2 * rows, 1), pl.ds(AT_COEF, radial)]
            up_msg[2] = second
            down_msg[0] = take("first")
            down_msg[1, pl.ds(0, 1), :] = gathered_row(up, 2 * rows, AT_ROW_B, lanes)
            down_msg[1, pl.ds(1, 1), :] = down[pl.ds(0, 1), :]
            down_msg[2] = partial_x[0]

        even_x = lax.rem(lax.axis_index("ax"), 2) == 0

        @pl.when(even_x)
        def _():
            finish(out_up, out_down)

        @pl.when(jnp.logical_not(even_x))
        def _():
            finish(out_down, out_up)

    @pl.when(even)
    def _():
        work(in_o, in_e, msg_e, msg_o)

    @pl.when(jnp.logical_not(even))
    def _():
        work(in_e, in_o, msg_e, msg_o)


def last_kernel(
    coef_2, partial, fixed, edges, in_e, in_o, x_o, x_e,
    out,
    packed, spread, up, down, below, above, now, edge, result, mixed, sems,
):
    cells, rows, lanes = partial.shape
    radial = packed.shape[1] // 2
    dirs = lanes // radial
    n = cells * rows
    last, end = cells - 1, rows - 1
    even = even_az()
    place = lax.axis_index("ax")
    even_x = lax.rem(place, 2) == 0
    final = lax.axis_size("ax") - 1
    layer = 6 * rows
    loads = [
        pltpu.make_async_copy(coef_2.at[pl.ds(a * layer, layer)], mixed.at[pl.ds(a * layer, layer)], sems.at[cells + a])
        for a in range(cells)
    ]
    for copy in loads:
        copy.start()

    @pl.when(even)
    def _():
        up[...] = in_o[...]
        down[...] = in_e[...]

    @pl.when(jnp.logical_not(even))
    def _():
        up[...] = in_e[...]
        down[...] = in_o[...]

    @pl.when(even_x)
    def _():
        below[...] = jnp.where(place == 0, 0.0, x_o[...])
        above[...] = x_e[...]

    @pl.when(jnp.logical_not(even_x))
    def _():
        below[...] = x_e[...]
        above[...] = jnp.where(place == final, 0.0, x_o[...])

    face_a, coef_a = edges[pl.ds(0, rows), :], edges[pl.ds(rows, rows), :]
    ends, first, coef_x = (edges[pl.ds(2 * rows + 4 * k, cells), :] for k in range(3))

    def joined(msg, lane):
        return jnp.concatenate([msg[pl.ds(2 * rows, 8), pl.ds(lane + 128 * k, radial)] for k in range(rows // 8)], axis=0)

    for k, lane in enumerate((AT_C1, AT_B2, AT_C2)):
        packed[pl.ds(k * rows, rows), :] = two_terms(joined(up, lane))
    singles = [below[1, pl.ds(2, 1), pl.ds(128 * k, radial)] for k in range(14)]
    singles += [msg[pl.ds(2 * rows, 1), pl.ds(AT_COEF, radial)] for msg in (up, down)]
    packed[pl.ds(3 * rows, 16), :] = two_terms(jnp.concatenate(singles, axis=0))
    spread_all(packed, [spread], radial, dirs)
    in_c1, in_b2, in_c2 = (spread[pl.ds(k * rows, rows), :] for k in range(3))
    below_c = spread[pl.ds(3 * rows, 6), :]
    below_b2, below_c2 = spread[pl.ds(3 * rows + 6, 4), :], spread[pl.ds(3 * rows + 10, 4), :]
    own_c = jnp.concatenate([coef_x, spread[pl.ds(3 * rows + 14, 2), :]], axis=0)

    starts = jnp.concatenate([first, gathered_row(up, 2 * rows, AT_ROW_B, lanes), down[pl.ds(0, 1), :]], axis=0)
    enter = jnp.concatenate([below[0], below[1, pl.ds(0, 2), :]], axis=0) + below_c * starts
    leave = own_c * jnp.concatenate([above[0], above[1, pl.ds(0, 2), :]], axis=0)
    crossing = in_c1 * edges[pl.ds(2 * rows + 16, rows), :]
    beyond = coef_a * down[pl.ds(0, rows), :]
    at_x = lax.broadcasted_iota(jnp.int32, (rows, 1), 0)

    def with_edges(block, k):
        return block + jnp.where(at_x == 0, enter[k:k + 1], 0.0) - jnp.where(at_x == end, leave[k:k + 1], 0.0)

    for a in range(cells):
        f = partial[a]
        if a == 0:
            f = f + up[pl.ds(0, rows), :] + crossing
        if a == last:
            f = f - beyond
        now[a] = with_edges(f, a)
    now[cells] = with_edges(down[pl.ds(rows, rows), :] + face_a + beyond, 5)
    lower = up[pl.ds(rows, rows), :] + in_b2 * (
        jnp.where(at_x == 0, enter[4:5], 0.0) - jnp.where(at_x == end, leave[4:5], 0.0) - crossing
    )
    before = lower + in_c2 * now[0]

    first_now = jnp.concatenate([now[a, pl.ds(0, 1), :] for a in range(cells)], axis=0)
    enter_2 = below[2] - below_b2 * (below_c[0:4] * first) + below_c2 * first_now
    inside = jnp.where(place == final, 0.0, 1.0)
    edge[...] = inside * (above[2] + ends + leave[0:4])

    def low(c, a):
        return mixed[pl.ds((a * 6 + c) * rows, rows), :]

    def high(c, a):
        return mixed[pl.ds((a * 6 + 3 + c) * rows, rows), :]

    copies = []
    for a in range(cells):
        loads[a].wait()
        f = now[a]
        face = low(0, a) * f + high(0, a) * now[a + 1]
        change = fixed[a] + (face - before)
        before = face
        face = low(1, a) * f + high(1, a) * ahead_x(f, edge[pl.ds(a, 1), :])
        change = change + (face - behind_x(face, enter_2[a:a + 1]))
        face = low(2, a) * f + high(2, a) * ahead_r(f, dirs)
        change = change + (face - behind_r(face, dirs))
        result[a] = f - change
        copies.append(pltpu.make_async_copy(result.at[a], out.at[a], sems.at[a]))
        copies[a].start()

    for copy in copies:
        copy.wait()


def film_kernel(done, row_film, film_own, film_1, x_o, x_e, totals, film_out):
    del done
    cells, share = film_out.shape
    place = lax.axis_index("ax")
    mean = jnp.sum(totals[:, 0:1, :], axis=0) / (cells * totals.shape[0])
    factor = mean / row_film[...]
    for k, source in enumerate((x_o, film_1, x_e, film_own)):

        @pl.when(place == k)
        def _():
            if len(source.shape) == 2:
                film = source[pl.ds(0, cells), :]
            else:
                film = jnp.concatenate([source[1, pl.ds(3, 1), pl.ds(128 * a, 128)] for a in range(cells)], axis=0)
            film_out[...] = (film * factor)[:, k * share:(k + 1) * share]


def swap(value, axis, pairing):
    count = lax.axis_size(axis)
    if axis == "ax":
        other = [i ^ pairing for i in range(count)]
    elif pairing == 0:
        other = [i ^ 1 for i in range(count)]
    else:
        other = [(i - 1 if i % 2 == 0 else i + 1) % count for i in range(count)]
    return lax.ppermute(value, axis, list(enumerate(other)))


def pinned(value, space):
    return pltpu.with_memory_space_constraint(value, space)


def placed(space, shape, dtype):
    return space(shape, dtype)


def call(kernel, args, outs, scratch, in_hbm=0, out_hbm=0, free=0, sems=0, cost=None):
    vmem, hbm = pl.BlockSpec(memory_space=pltpu.VMEM), pl.BlockSpec(memory_space=pl.ANY)
    shapes = [pltpu.VMEM(shape, dtype) for shape, dtype in scratch]
    pinned_outs = len(outs) - free
    shapes_out = [placed(pltpu.HBM if i < out_hbm else pltpu.VMEM, *out) for i, out in enumerate(outs[:pinned_outs])]
    shapes_out += [jax.ShapeDtypeStruct(*out) for out in outs[pinned_outs:]]
    args = [pinned(arg, pltpu.HBM if i < in_hbm else pltpu.VMEM) for i, arg in enumerate(args)]
    if sems:
        shapes.append(pltpu.SemaphoreType.DMA((sems,)))
    return pl.pallas_call(
        kernel,
        out_shape=shapes_out,
        in_specs=[hbm] * in_hbm + [vmem] * (len(args) - in_hbm),
        out_specs=[hbm] * out_hbm + [vmem] * (len(outs) - out_hbm),
        scratch_shapes=shapes,
        compiler_params=pltpu.CompilerParams(vmem_limit_bytes=32 * 2**20),
        cost_estimate=cost,
        name=kernel.__name__,
    )(*args)


def local(tangent, velocity, face_frac, branch, basis, design, exit_film):
    cells, rows, lanes = tangent.shape
    radial = velocity.shape[-1]
    dirs = design.shape[1]
    n = cells * rows
    devices = lax.axis_size("az")
    layer, cell_layer = (rows, lanes), (rows, radial)
    z_msg, x_msg, line = (2 * rows + 8, lanes), (3, cells, lanes), (cells, lanes)
    inputs = (tangent, velocity, face_frac, branch, basis, design, exit_film)
    count = (3 * len(EDGE) + 2) * rows
    z_e, z_o, sums = call(
        edge_kernel,
        inputs,
        [(z_msg, F32), (z_msg, F32), ((devices, 2, 128), F32)],
        [
            (tangent.shape, F32), (velocity.shape, F32), (velocity.shape, F32), (cell_layer, F32),
            (velocity.shape, branch.dtype), (cell_layer, branch.dtype), ((len(EDGE) * rows, lanes), BF16),
            (design.shape, BF16), (exit_film.shape, F32), ((len(EDGE) * rows, lanes), BF16),
            ((count, 2 * radial), BF16), ((count, lanes), F32), (layer, F32), ((2, lanes), F32),
            ((2, *layer), F32), ((2, *layer), F32), (layer, F32),
        ],
        in_hbm=7,
        sems=8 + len(EDGE),
    )
    in_e, in_o = swap(z_e, "az", 0), swap(z_o, "az", 1)
    totals = lax.all_to_all(sums, "az", 0, 0)
    velocity_tangent, middle, partial, edges, row_film = call(
        local_kernel,
        inputs,
        [
            (basis.shape, BF16), ((32, lanes), F32), (tangent.shape, F32), ((3 * rows + 16, lanes), F32),
            ((cells, 128), F32),
        ],
        [
            (tangent.shape, F32), (velocity.shape, F32), (face_frac.shape, F32), (branch.shape, branch.dtype),
            (basis.shape, BF16), (design.shape, BF16), (exit_film.shape, F32), (basis.shape, BF16),
            ((9 * n + 16, 2 * radial), BF16), ((9 * n + 16, lanes), F32),
        ],
        in_hbm=7,
        out_hbm=1,
        sems=8,
        cost=pl.CostEstimate(flops=10**9, bytes_accessed=10 * 10**6, transcendentals=0),
    )
    x_e, x_o, film = call(
        middle_kernel, (middle, in_e, in_o), [(x_msg, F32), (x_msg, F32), ((8, 128), F32)], []
    )
    from_o, from_e, film_1 = swap(x_o, "ax", 3), swap(x_e, "ax", 1), swap(film, "ax", 2)
    coef_2, fixed = call(
        step_kernel,
        (velocity, face_frac, branch, velocity_tangent, film),
        [((6 * n, lanes), F32), (tangent.shape, F32)],
        [
            (velocity.shape, F32), (velocity.shape, F32), (velocity.shape, branch.dtype), (basis.shape, BF16),
            ((9 * n, 2 * radial), BF16), ((3 * n, lanes), F32), ((6 * n, lanes), F32),
        ],
        in_hbm=4,
        out_hbm=1,
        sems=5,
        cost=pl.CostEstimate(flops=10**9, bytes_accessed=10 * 10**6, transcendentals=0),
    )
    count = 3 * rows + 16
    (out,) = call(
        last_kernel,
        (coef_2, partial, fixed, edges, in_e, in_o, from_o, from_e),
        [(tangent.shape, F32)],
        [
            ((count, 2 * radial), BF16), ((count, lanes), F32), (z_msg, F32), (z_msg, F32), (x_msg, F32), (x_msg, F32),
            ((cells + 1, *layer), F32), (line, F32), (tangent.shape, F32), ((6 * n, lanes), F32),
        ],
        in_hbm=1,
        out_hbm=1,
        sems=2 * cells,
    )
    (film_out,) = call(
        film_kernel,
        (out, row_film, film, film_1, from_o, from_e, totals),
        [((cells, dirs // lax.axis_size("ax")), F32)],
        [],
        in_hbm=1,
        free=1,
    )
    return out, velocity_tangent, film_out


def solution(mesh):
    in_specs = (
        P("az", "ax", None),
        P(None, "az", "ax", None),
        P(None, None, "az", "ax", None),
        P(None, None, "az", "ax", None),
        P(None, "az", "ax", None),
        P(),
        P("az", None),
    )
    out_specs = (P("az", "ax", None), P(None, "az", "ax", None), P("az", "ax"))
    return jax.shard_map(local, mesh=mesh, in_specs=in_specs, out_specs=out_specs, check_vma=False)
```

```python
import jax
import jax.numpy as jnp
from jax import lax
from jax.experimental import pallas as pl
from jax.experimental.pallas import tpu as pltpu
from jax.sharding import PartitionSpec as P

F32, BF16 = jnp.float32, jnp.bfloat16
CHUNK = 256
RADIAL = 64
CELLS = 4
UNROLL = 8
AT_C1, AT_B2, AT_C2, AT_ROW_A, AT_ROW_B, AT_COEF, AT_FIRST, AT_END = 0, 256, 512, 768, 1024, 1280, 1408, 1664


def mix(speed, branch):
    part = speed * (0.25 * branch.astype(F32))
    rest = speed - part
    ahead = speed > 0
    return jnp.where(ahead, rest, part), jnp.where(ahead, part, rest)


def two_terms(values):
    high = values.astype(BF16)
    low = (values - high.astype(F32)).astype(BF16)
    return jnp.concatenate([high, low], axis=-1)


def spreader(offset, lanes, radial, dirs):
    row = lax.broadcasted_iota(jnp.int32, (2 * radial, lanes), 0)
    lane = lax.broadcasted_iota(jnp.int32, (2 * radial, lanes), 1) + offset
    shift = dirs.bit_length() - 1
    return jnp.where((row & (radial - 1)) == (lane >> shift), 1.0, 0.0).astype(BF16)


def spread_all(packed, outs, radial, dirs):
    lanes = outs[0].shape[1]

    @pl.loop(0, lanes // CHUNK, unroll=UNROLL)
    def _(k):
        at = pl.multiple_of(k * CHUNK, CHUNK)
        ones = spreader(at, CHUNK, radial, dirs)
        row = 0
        for out in outs:
            count = out.shape[0]
            left = packed[pl.ds(row, count), :]
            out[:, pl.ds(at, CHUNK)] = jnp.dot(left, ones, preferred_element_type=F32)
            row += count


def blocks_of(design):
    dirs = design.shape[1]
    row = lax.broadcasted_iota(jnp.int32, (CHUNK, dirs), 0)
    col = lax.broadcasted_iota(jnp.int32, (CHUNK, dirs), 1)
    pick = jnp.where((row & (dirs - 1)) == col, 1.0, 0.0).astype(BF16)
    tiled = jnp.dot(pick, design, preferred_element_type=F32).astype(BF16)
    tiled = lax.dot_general(tiled, pick, (((1,), (1,)), ((), ())), preferred_element_type=F32)
    row = lax.broadcasted_iota(jnp.int32, (CHUNK, CHUNK), 0)
    col = lax.broadcasted_iota(jnp.int32, (CHUNK, CHUNK), 1)
    shift = dirs.bit_length() - 1
    return jnp.where((row >> shift) == (col >> shift), tiled, 0.0).astype(BF16)


def wall(radial):
    lane = lax.broadcasted_iota(jnp.int32, (1, radial), 1)
    return jnp.where(lane < radial - 1, 1.0, 0.0)


def ahead_x(rows, last):
    n = rows.shape[0]
    at = lax.broadcasted_iota(jnp.int32, rows.shape, 0)
    return jnp.where(at == n - 1, last, pltpu.roll(rows, n - 1, 0))


def behind_x(rows, first):
    at = lax.broadcasted_iota(jnp.int32, rows.shape, 0)
    return jnp.where(at == 0, first, pltpu.roll(rows, 1, 0))


def ahead_r(rows, dirs):
    return pltpu.roll(rows, rows.shape[1] - dirs, 1)


def behind_r(rows, dirs):
    return pltpu.roll(rows, dirs, 1)


def even_az():
    return lax.rem(lax.axis_index("az"), 2) == 0


def radial_weights(radial):
    return (lax.broadcasted_iota(jnp.int32, (1, radial), 1).astype(F32) + 0.5) / radial


EDGE = ((0, 0), (0, 2), (0, 3), (1, 0), (1, 3), (2, 0), (2, 3))


def edge_kernel(
    tangent, velocity, frac, branch, basis, design, exit_film,
    msg_e, msg_o, sums, field, vel, share, kind, left, mat, film,
    vel_tan, packed, spread, work, ends, edge, faces, face_a, sems,
):
    cells, rows, lanes = field.shape
    radial = vel.shape[-1]
    dirs = lanes // radial
    last, end = cells - 1, rows - 1
    inner = wall(radial)
    pairs = [
        (exit_film, film), (velocity, vel), (branch, kind), (frac, share), (design, mat), (tangent, field), (basis, left),
    ]
    copies = [pltpu.make_async_copy(src, dst, sems.at[i]) for i, (src, dst) in enumerate(pairs)]
    for copy in copies:
        copy.start()
    copies[0].wait()
    sums[...] = jnp.full(sums.shape, jnp.sum(film[...] * radial_weights(radial)), F32)
    for copy in copies[1:4]:
        copy.wait()

    at = {}
    row = 0
    for c, a in EDGE:
        low, high = mix(vel[c, a], kind[0, c, a])
        if (c, a) == (0, last):
            high_a = high
        if c == 1:
            at["high", a] = high
        for name, part in zip("plh", (share[0, c, a], low, high), strict=True):
            packed[pl.ds(row, rows), :] = two_terms(part * inner if c == 2 else part)
            at[name, c, a] = row
            row += rows
    low_2, high_2 = mix(vel[0, last], kind[1, 0, last])
    for name, part in zip("pl", (share[1, 0, last], low_2), strict=True):
        packed[pl.ds(row, rows), :] = two_terms(part)
        at[name] = row
        row += rows
    spread_all(packed, [spread], radial, dirs)

    for copy in copies[4:]:
        copy.wait()
    weights = blocks_of(mat[...])

    @pl.loop(0, lanes // CHUNK, unroll=UNROLL)
    def _(k):
        lane = pl.ds(pl.multiple_of(k * CHUNK, CHUNK), CHUNK)
        part = jnp.concatenate([left[c, a, :, lane] for c, a in EDGE], axis=0)
        vel_tan[:, lane] = jnp.dot(part, weights, preferred_element_type=F32).astype(BF16)

    def sp(*key):
        return spread[pl.ds(at[key], rows), :]

    def speed(c, a):
        return vel_tan[pl.ds(EDGE.index((c, a)) * rows, rows), :].astype(F32)

    def along_az(a):
        f = field[a]
        face = speed(0, a) * sp("p", 0, a) + sp("l", 0, a) * f
        return face if a == last else face + sp("h", 0, a) * field[a + 1]

    faces[0] = along_az(0)
    faces[1] = along_az(last - 1)
    face_a[...] = along_az(last)
    for i, a in enumerate((0, last)):
        f = field[a]
        change = faces[0] if a == 0 else face_a[...] - faces[1]
        face = speed(1, a) * sp("p", 1, a) + sp("l", 1, a) * f + sp("h", 1, a) * ahead_x(f, 0.0)
        ends[pl.ds(i, 1), :] = face[end:, :]
        change = change + (face - behind_x(face, 0.0))
        face = speed(2, a) * sp("p", 2, a) + sp("l", 2, a) * f + sp("h", 2, a) * ahead_r(f, dirs)
        change = change + (face - behind_r(face, dirs))
        edge[i] = f - change
    work[...] = speed(0, last) * spread[pl.ds(at["p"], rows), :] + spread[pl.ds(at["l"], rows), :] * edge[1]

    def small_rows(msg, lane, block):
        for k in range(lanes // CHUNK):
            msg[pl.ds(2 * rows + k, 1), pl.ds(lane, CHUNK)] = block[:, k * CHUNK:(k + 1) * CHUNK]

    def halves(msg, lane, block):
        for k in range(rows // 8):
            msg[pl.ds(2 * rows, 8), pl.ds(lane + 128 * k, radial)] = block[8 * k:8 * k + 8]

    def fill(up_msg, down_msg):
        for msg in (up_msg, down_msg):
            msg[pl.ds(2 * rows, 8), :] = jnp.zeros((8, lanes), F32)
        up_msg[pl.ds(0, rows), :] = face_a[...]
        up_msg[pl.ds(rows, rows), :] = work[...]
        halves(up_msg, AT_C1, high_a)
        halves(up_msg, AT_B2, low_2)
        halves(up_msg, AT_C2, high_2)
        small_rows(up_msg, AT_ROW_A, ends[pl.ds(1, 1), :])
        small_rows(up_msg, AT_ROW_B, field[last, pl.ds(0, 1), :])
        small_rows(up_msg, AT_FIRST, sp("h", 0, last)[0:1])
        small_rows(up_msg, AT_END, sp("h", 0, last)[end:])
        up_msg[pl.ds(2 * rows, 1), pl.ds(AT_COEF, radial)] = at["high", last][end:, :]
        down_msg[pl.ds(0, rows), :] = field[0]
        down_msg[pl.ds(rows, rows), :] = edge[0]
        small_rows(down_msg, AT_ROW_A, ends[pl.ds(0, 1), :])
        down_msg[pl.ds(2 * rows, 1), pl.ds(AT_COEF, radial)] = at["high", 0][end:, :]

    even = even_az()

    @pl.when(even)
    def _():
        fill(msg_e, msg_o)

    @pl.when(jnp.logical_not(even))
    def _():
        fill(msg_o, msg_e)


MIDDLE = dict(
    ends=0, end_fixed=4, low_end=8, first=12, partial_first=16, partial_end=20, front=24, coef_a=26, coefs=28
)


def local_kernel(
    field, vel, share, kind, left, mat, film,
    vel_tan, middle, partial, edges, row_film,
    product, packed, spread, sems,
):
    cells, rows, lanes = field.shape
    radial = vel.shape[-1]
    dirs = lanes // radial
    n = cells * rows
    last, end = cells - 1, rows - 1
    inner = wall(radial)
    for c in range(3):
        low, high = mix(vel[c], kind[0, c])
        for k, part in enumerate((share[0, c], low, high)):
            part = part.reshape(n, radial)
            packed[pl.ds((k * 3 + c) * n, n), :] = two_terms(part * inner if c == 2 else part)
        if c == 1:
            high_1 = high
    low_2, high_2 = mix(vel[1], kind[1, 1])
    tail = [share[1, 1, :, end, :], low_2[:, end, :], jnp.zeros((8, radial), F32)]
    packed[pl.ds(9 * n, 16), :] = two_terms(jnp.concatenate(tail, axis=0))
    middle[pl.ds(MIDDLE["coefs"], 1), :] = jnp.zeros((1, lanes), F32)
    for start, part in ((0, high_1), (6, low_2), (10, high_2)):
        for a in range(cells):
            middle[pl.ds(MIDDLE["coefs"], 1), pl.ds(128 * (start + a), radial)] = part[a, end:, :]
    spread_all(packed, [spread], radial, dirs)
    weights = blocks_of(mat[...])

    @pl.loop(0, lanes // CHUNK, unroll=UNROLL)
    def _(k):
        lane = pl.ds(pl.multiple_of(k * CHUNK, CHUNK), CHUNK)
        block = jnp.dot(left[:, :, :, lane].reshape(3 * n, CHUNK), weights, preferred_element_type=F32)
        product[:, :, :, lane] = block.astype(BF16).reshape(3, cells, rows, CHUNK)

    output = pltpu.make_async_copy(product, vel_tan, sems.at[0])
    output.start()

    def sp(k, c, a):
        return spread[pl.ds((k * 3 + c) * n + a * rows, rows), :]

    def speed(c, a):
        return product[c, a].astype(F32)

    def put(name, a, block):
        middle[pl.ds(MIDDLE[name] + a, block.shape[0]), :] = block

    before = None
    for a in range(cells):
        f = field[a]
        here = speed(0, a) * sp(0, 0, a) + sp(1, 0, a) * f
        if a < last:
            here = here + sp(2, 0, a) * field[a + 1]
        change = here if before is None else here - before
        before = here
        speed_x = speed(1, a)
        face = speed_x * sp(0, 1, a) + sp(1, 1, a) * f + sp(2, 1, a) * ahead_x(f, 0.0)
        put("ends", a, face[end:])
        edges[pl.ds(2 * rows + a, 1), :] = face[end:]
        change = change + (face - behind_x(face, 0.0))
        face = speed(2, a) * sp(0, 2, a) + sp(1, 2, a) * f + sp(2, 2, a) * ahead_r(f, dirs)
        change = change + (face - behind_r(face, dirs))
        block = f - change
        partial[a] = block
        put("first", a, f[0:1])
        edges[pl.ds(2 * rows + 4 + a, 1), :] = f[0:1]
        put("partial_first", a, block[0:1])
        put("partial_end", a, block[end:])
        put("low_end", a, spread[pl.ds(9 * n + cells + a, 1), :])
        put("end_fixed", a, speed_x[end:] * spread[pl.ds(9 * n + a, 1), :])
        edges[pl.ds(2 * rows + 8 + a, 1), :] = sp(2, 1, a)[end:]
    edges[pl.ds(0, rows), :] = before
    edges[pl.ds(2 * rows + 12, 4), :] = jnp.zeros((4, lanes), F32)
    edges[pl.ds(2 * rows + 16, rows), :] = field[0]
    edges[pl.ds(rows, rows), :] = sp(2, 0, last)
    for k, x in enumerate((0, end)):
        put("front", k, field[0, pl.ds(x, 1), :])
        put("coef_a", k, sp(2, 0, last)[x:x + 1])
    total = jnp.sum(film[...] * radial_weights(radial), axis=1, keepdims=True)
    row_film[...] = jnp.broadcast_to(total, row_film.shape)
    output.wait()


def step_kernel(
    vel_tan, vel, share, kind, after,
    coef_2, fixed,
    product, packed, spread, mixed, sems,
):
    del after
    _, cells, rows, lanes = product.shape
    radial = vel.shape[-1]
    dirs = lanes // radial
    n = cells * rows
    inner = wall(radial)
    fetch = pltpu.make_async_copy(vel_tan, product, sems.at[0])
    fetch.start()
    for c in range(3):
        for k, part in enumerate((share[1, c], *mix(vel[c], kind[1, c]))):
            part = part.reshape(n, radial)
            part = two_terms(part * inner if c == 2 else part)
            if k == 0:
                packed[pl.ds(c * n, n), :] = part
                continue
            for a in range(cells):
                row = 3 * n + ((a * 2 + k - 1) * 3 + c) * rows
                packed[pl.ds(row, rows), :] = part[a * rows:(a + 1) * rows]
    copies = []
    for k in range(lanes // CHUNK):
        lane = pl.ds(k * CHUNK, CHUNK)
        ones = spreader(k * CHUNK, CHUNK, radial, dirs)
        mixed[:, lane] = jnp.dot(packed[pl.ds(3 * n, 6 * n), :], ones, preferred_element_type=F32)
        copies.append(pltpu.make_async_copy(mixed.at[:, lane], coef_2.at[:, lane], sems.at[1 + k]))
        copies[k].start()
        spread[:, lane] = jnp.dot(packed[pl.ds(0, 3 * n), :], ones, preferred_element_type=F32)
    fetch.wait()
    before = None
    for a in range(cells):
        faces = [product[c, a].astype(F32) * spread[pl.ds(c * n + a * rows, rows), :] for c in range(3)]
        change = faces[0] if before is None else faces[0] - before
        before = faces[0]
        change = change + (faces[1] - behind_x(faces[1], 0.0))
        fixed[a] = change + (faces[2] - behind_r(faces[2], dirs))
    for copy in copies:
        copy.wait()


def gathered_row(msg, row, lane, lanes):
    return jnp.concatenate([msg[pl.ds(row + k, 1), pl.ds(lane, CHUNK)] for k in range(lanes // CHUNK)], axis=1)


def middle_kernel(
    middle, in_e, in_o,
    msg_e, msg_o, film_msg,
):
    cells, rows, lanes = CELLS, (in_e.shape[0] - 8) // 2, in_e.shape[1]
    radial, dirs = RADIAL, lanes // RADIAL
    last, end = cells - 1, rows - 1

    def take(name, count=CELLS, at=0):
        return middle[pl.ds(MIDDLE[name] + at, count), :]

    even = even_az()

    def work(up, down, out_up, out_down):
        at_a = lax.broadcasted_iota(jnp.int32, (cells, 1), 0)
        partial_x = []
        for k, (x, lane, name) in enumerate(((0, AT_FIRST, "partial_first"), (end, AT_END, "partial_end"))):
            face = up[pl.ds(x, 1), :] + gathered_row(up, 2 * rows, lane, lanes) * take("front", 1, k)
            beyond = take("coef_a", 1, k) * down[pl.ds(x, 1), :]
            partial_x.append(take(name) + jnp.where(at_a == 0, face, 0.0) - jnp.where(at_a == last, beyond, 0.0))
        second = take("end_fixed") + take("low_end") * partial_x[1]

        lane = lax.broadcasted_iota(jnp.int32, (1, lanes), 1)
        weight = ((lane // dirs).astype(F32) + 0.5) / radial
        raw = (take("ends") + second) * weight
        film = raw[:, 0:128]
        for k in range(1, lanes // 128):
            film = film + raw[:, 128 * k:128 * k + 128]
        shift = 64
        while shift >= dirs:
            film = film + pltpu.roll(film, shift, 1)
            shift //= 2
        film_msg[...] = jnp.zeros(film_msg.shape, F32)
        film_msg[pl.ds(0, cells), :] = film

        def finish(up_msg, down_msg):
            for msg in (up_msg, down_msg):
                msg[1, pl.ds(2, 2), :] = jnp.zeros((2, lanes), F32)
                for a in range(cells):
                    msg[1, pl.ds(3, 1), pl.ds(128 * a, 128)] = film[a:a + 1]
            up_msg[0] = take("ends")
            up_msg[1, pl.ds(0, 1), :] = gathered_row(up, 2 * rows, AT_ROW_A, lanes)
            up_msg[1, pl.ds(1, 1), :] = gathered_row(down, 2 * rows, AT_ROW_A, lanes)
            up_msg[1, pl.ds(2, 1), :] = take("coefs", 1)
            up_msg[1, pl.ds(2, 1), pl.ds(128 * 4, radial)] = up[pl.ds(2 * rows, 1), pl.ds(AT_COEF, radial)]
            up_msg[1, pl.ds(2, 1), pl.ds(128 * 5, radial)] = down[pl.ds(2 * rows, 1), pl.ds(AT_COEF, radial)]
            up_msg[2] = second
            down_msg[0] = take("first")
            down_msg[1, pl.ds(0, 1), :] = gathered_row(up, 2 * rows, AT_ROW_B, lanes)
            down_msg[1, pl.ds(1, 1), :] = down[pl.ds(0, 1), :]
            down_msg[2] = partial_x[0]

        even_x = lax.rem(lax.axis_index("ax"), 2) == 0

        @pl.when(even_x)
        def _():
            finish(out_up, out_down)

        @pl.when(jnp.logical_not(even_x))
        def _():
            finish(out_down, out_up)

    @pl.when(even)
    def _():
        work(in_o, in_e, msg_e, msg_o)

    @pl.when(jnp.logical_not(even))
    def _():
        work(in_e, in_o, msg_e, msg_o)


def last_kernel(
    coef_2, partial, fixed, edges, in_e, in_o, x_o, x_e,
    out,
    packed, spread, up, down, below, above, now, edge, result, mixed, sems,
):
    cells, rows, lanes = partial.shape
    radial = packed.shape[1] // 2
    dirs = lanes // radial
    n = cells * rows
    last, end = cells - 1, rows - 1
    even = even_az()
    place = lax.axis_index("ax")
    even_x = lax.rem(place, 2) == 0
    final = lax.axis_size("ax") - 1
    layer = 6 * rows
    loads = [
        pltpu.make_async_copy(coef_2.at[pl.ds(a * layer, layer)], mixed.at[pl.ds(a * layer, layer)], sems.at[cells + a])
        for a in range(cells)
    ]
    for copy in loads:
        copy.start()

    @pl.when(even)
    def _():
        up[...] = in_o[...]
        down[...] = in_e[...]

    @pl.when(jnp.logical_not(even))
    def _():
        up[...] = in_e[...]
        down[...] = in_o[...]

    @pl.when(even_x)
    def _():
        below[...] = jnp.where(place == 0, 0.0, x_o[...])
        above[...] = x_e[...]

    @pl.when(jnp.logical_not(even_x))
    def _():
        below[...] = x_e[...]
        above[...] = jnp.where(place == final, 0.0, x_o[...])

    face_a, coef_a = edges[pl.ds(0, rows), :], edges[pl.ds(rows, rows), :]
    ends, first, coef_x = (edges[pl.ds(2 * rows + 4 * k, cells), :] for k in range(3))

    def joined(msg, lane):
        return jnp.concatenate([msg[pl.ds(2 * rows, 8), pl.ds(lane + 128 * k, radial)] for k in range(rows // 8)], axis=0)

    for k, lane in enumerate((AT_C1, AT_B2, AT_C2)):
        packed[pl.ds(k * rows, rows), :] = two_terms(joined(up, lane))
    singles = [below[1, pl.ds(2, 1), pl.ds(128 * k, radial)] for k in range(14)]
    singles += [msg[pl.ds(2 * rows, 1), pl.ds(AT_COEF, radial)] for msg in (up, down)]
    packed[pl.ds(3 * rows, 16), :] = two_terms(jnp.concatenate(singles, axis=0))
    spread_all(packed, [spread], radial, dirs)
    in_c1, in_b2, in_c2 = (spread[pl.ds(k * rows, rows), :] for k in range(3))
    below_c = spread[pl.ds(3 * rows, 6), :]
    below_b2, below_c2 = spread[pl.ds(3 * rows + 6, 4), :], spread[pl.ds(3 * rows + 10, 4), :]
    own_c = jnp.concatenate([coef_x, spread[pl.ds(3 * rows + 14, 2), :]], axis=0)

    starts = jnp.concatenate([first, gathered_row(up, 2 * rows, AT_ROW_B, lanes), down[pl.ds(0, 1), :]], axis=0)
    enter = jnp.concatenate([below[0], below[1, pl.ds(0, 2), :]], axis=0) + below_c * starts
    leave = own_c * jnp.concatenate([above[0], above[1, pl.ds(0, 2), :]], axis=0)
    crossing = in_c1 * edges[pl.ds(2 * rows + 16, rows), :]
    beyond = coef_a * down[pl.ds(0, rows), :]
    at_x = lax.broadcasted_iota(jnp.int32, (rows, 1), 0)

    def with_edges(block, k):
        return block + jnp.where(at_x == 0, enter[k:k + 1], 0.0) - jnp.where(at_x == end, leave[k:k + 1], 0.0)

    for a in range(cells):
        f = partial[a]
        if a == 0:
            f = f + up[pl.ds(0, rows), :] + crossing
        if a == last:
            f = f - beyond
        now[a] = with_edges(f, a)
    now[cells] = with_edges(down[pl.ds(rows, rows), :] + face_a + beyond, 5)
    lower = up[pl.ds(rows, rows), :] + in_b2 * (
        jnp.where(at_x == 0, enter[4:5], 0.0) - jnp.where(at_x == end, leave[4:5], 0.0) - crossing
    )
    before = lower + in_c2 * now[0]

    first_now = jnp.concatenate([now[a, pl.ds(0, 1), :] for a in range(cells)], axis=0)
    enter_2 = below[2] - below_b2 * (below_c[0:4] * first) + below_c2 * first_now
    inside = jnp.where(place == final, 0.0, 1.0)
    edge[...] = inside * (above[2] + ends + leave[0:4])

    def low(c, a):
        return mixed[pl.ds((a * 6 + c) * rows, rows), :]

    def high(c, a):
        return mixed[pl.ds((a * 6 + 3 + c) * rows, rows), :]

    copies = []
    for a in range(cells):
        loads[a].wait()
        f = now[a]
        face = low(0, a) * f + high(0, a) * now[a + 1]
        change = fixed[a] + (face - before)
        before = face
        face = low(1, a) * f + high(1, a) * ahead_x(f, edge[pl.ds(a, 1), :])
        change = change + (face - behind_x(face, enter_2[a:a + 1]))
        face = low(2, a) * f + high(2, a) * ahead_r(f, dirs)
        change = change + (face - behind_r(face, dirs))
        result[a] = f - change
        copies.append(pltpu.make_async_copy(result.at[a], out.at[a], sems.at[a]))
        copies[a].start()

    for copy in copies:
        copy.wait()


def film_kernel(done, row_film, film_own, film_1, x_o, x_e, totals, film_out):
    del done
    cells, share = film_out.shape
    place = lax.axis_index("ax")
    mean = jnp.sum(totals[:, 0:1, :], axis=0) / (cells * totals.shape[0])
    factor = mean / row_film[...]
    for k, source in enumerate((x_o, film_1, x_e, film_own)):

        @pl.when(place == k)
        def _():
            if len(source.shape) == 2:
                film = source[pl.ds(0, cells), :]
            else:
                film = jnp.concatenate([source[1, pl.ds(3, 1), pl.ds(128 * a, 128)] for a in range(cells)], axis=0)
            film_out[...] = (film * factor)[:, k * share:(k + 1) * share]


def swap(value, axis, pairing):
    count = lax.axis_size(axis)
    if axis == "ax":
        other = [i ^ pairing for i in range(count)]
    elif pairing == 0:
        other = [i ^ 1 for i in range(count)]
    else:
        other = [(i - 1 if i % 2 == 0 else i + 1) % count for i in range(count)]
    return lax.ppermute(value, axis, list(enumerate(other)))


def pinned(value, space):
    return pltpu.with_memory_space_constraint(value, space)


def placed(space, shape, dtype):
    return space(shape, dtype)


def call(kernel, args, outs, scratch, in_hbm=0, out_hbm=0, free=0, sems=0, cost=None):
    vmem, hbm = pl.BlockSpec(memory_space=pltpu.VMEM), pl.BlockSpec(memory_space=pl.ANY)
    shapes = [pltpu.VMEM(shape, dtype) for shape, dtype in scratch]
    pinned_outs = len(outs) - free
    shapes_out = [placed(pltpu.HBM if i < out_hbm else pltpu.VMEM, *out) for i, out in enumerate(outs[:pinned_outs])]
    shapes_out += [jax.ShapeDtypeStruct(*out) for out in outs[pinned_outs:]]
    args = [pinned(arg, pltpu.HBM if i < in_hbm else pltpu.VMEM) for i, arg in enumerate(args)]
    if sems:
        shapes.append(pltpu.SemaphoreType.DMA((sems,)))
    return pl.pallas_call(
        kernel,
        out_shape=shapes_out,
        in_specs=[hbm] * in_hbm + [vmem] * (len(args) - in_hbm),
        out_specs=[hbm] * out_hbm + [vmem] * (len(outs) - out_hbm),
        scratch_shapes=shapes,
        compiler_params=pltpu.CompilerParams(vmem_limit_bytes=32 * 2**20),
        cost_estimate=cost,
        name=kernel.__name__,
    )(*args)


def local(tangent, velocity, face_frac, branch, basis, design, exit_film):
    cells, rows, lanes = tangent.shape
    radial = velocity.shape[-1]
    dirs = design.shape[1]
    n = cells * rows
    devices = lax.axis_size("az")
    layer, cell_layer = (rows, lanes), (rows, radial)
    z_msg, x_msg, line = (2 * rows + 8, lanes), (3, cells, lanes), (cells, lanes)
    inputs = inputs_in_order = (tangent, velocity, face_frac, branch, basis, design, exit_film)
    count = (3 * len(EDGE) + 2) * rows
    z_e, z_o, sums, *inputs = call(
        edge_kernel,
        inputs,
        [(z_msg, F32), (z_msg, F32), ((devices, 2, 128), F32)] + [(value.shape, value.dtype) for value in inputs_in_order],
        [
            ((len(EDGE) * rows, lanes), BF16), ((count, 2 * radial), BF16), ((count, lanes), F32), (layer, F32),
            ((2, lanes), F32), ((2, *layer), F32), ((2, *layer), F32), (layer, F32),
        ],
        in_hbm=7,
        sems=7,
    )
    field, vel, share, kind, left, mat, film_in = inputs
    in_e, in_o = swap(z_e, "az", 0), swap(z_o, "az", 1)
    totals = lax.all_to_all(sums, "az", 0, 0)
    velocity_tangent, middle, partial, edges, row_film = call(
        local_kernel,
        (field, vel, share, kind, left, mat, film_in),
        [
            (basis.shape, BF16), ((32, lanes), F32), (tangent.shape, F32), ((3 * rows + 16, lanes), F32),
            ((cells, 128), F32),
        ],
        [(basis.shape, BF16), ((9 * n + 16, 2 * radial), BF16), ((9 * n + 16, lanes), F32)],
        out_hbm=1,
        sems=1,
        cost=pl.CostEstimate(flops=10**9, bytes_accessed=10 * 10**6, transcendentals=0),
    )
    x_e, x_o, film = call(
        middle_kernel, (middle, in_e, in_o), [(x_msg, F32), (x_msg, F32), ((8, 128), F32)], []
    )
    from_o, from_e, film_1 = swap(x_o, "ax", 3), swap(x_e, "ax", 1), swap(film, "ax", 2)
    coef_2, fixed = call(
        step_kernel,
        (velocity_tangent, vel, share, kind, film),
        [((6 * n, lanes), F32), (tangent.shape, F32)],
        [(basis.shape, BF16), ((9 * n, 2 * radial), BF16), ((3 * n, lanes), F32), ((6 * n, lanes), F32)],
        in_hbm=1,
        out_hbm=1,
        sems=1 + lanes // CHUNK,
        cost=pl.CostEstimate(flops=10**9, bytes_accessed=10 * 10**6, transcendentals=0),
    )
    count = 3 * rows + 16
    (out,) = call(
        last_kernel,
        (coef_2, partial, fixed, edges, in_e, in_o, from_o, from_e),
        [(tangent.shape, F32)],
        [
            ((count, 2 * radial), BF16), ((count, lanes), F32), (z_msg, F32), (z_msg, F32), (x_msg, F32), (x_msg, F32),
            ((cells + 1, *layer), F32), (line, F32), (tangent.shape, F32), ((6 * n, lanes), F32),
        ],
        in_hbm=1,
        out_hbm=1,
        sems=2 * cells,
    )
    (film_out,) = call(
        film_kernel,
        (out, row_film, film, film_1, from_o, from_e, totals),
        [((cells, dirs // lax.axis_size("ax")), F32)],
        [],
        in_hbm=1,
        free=1,
    )
    return out, velocity_tangent, film_out


def solution(mesh):
    in_specs = (
        P("az", "ax", None),
        P(None, "az", "ax", None),
        P(None, None, "az", "ax", None),
        P(None, None, "az", "ax", None),
        P(None, "az", "ax", None),
        P(),
        P("az", None),
    )
    out_specs = (P("az", "ax", None), P(None, "az", "ax", None), P("az", "ax"))
    return jax.shard_map(local, mesh=mesh, in_specs=in_specs, out_specs=out_specs, check_vma=False)
```

```python
import jax
import jax.numpy as jnp
from jax import lax
from jax.experimental import pallas as pl
from jax.experimental.pallas import tpu as pltpu
from jax.sharding import PartitionSpec as P

F32, BF16 = jnp.float32, jnp.bfloat16
CHUNK = 256
RADIAL = 64
CELLS = 4
UNROLL = 8
AT_C1, AT_B2, AT_C2, AT_ROW_A, AT_ROW_B, AT_COEF, AT_FIRST, AT_END = 0, 256, 512, 768, 1024, 1280, 1408, 1664


def mix(speed, branch):
    part = speed * (0.25 * branch.astype(F32))
    rest = speed - part
    ahead = speed > 0
    return jnp.where(ahead, rest, part), jnp.where(ahead, part, rest)


def two_terms(values):
    high = values.astype(BF16)
    low = (values - high.astype(F32)).astype(BF16)
    return jnp.concatenate([high, low], axis=-1)


def spreader(offset, lanes, radial, dirs):
    row = lax.broadcasted_iota(jnp.int32, (2 * radial, lanes), 0)
    lane = lax.broadcasted_iota(jnp.int32, (2 * radial, lanes), 1) + offset
    shift = dirs.bit_length() - 1
    return jnp.where((row & (radial - 1)) == (lane >> shift), 1.0, 0.0).astype(BF16)


def spread_all(packed, outs, radial, dirs):
    lanes = outs[0].shape[1]

    @pl.loop(0, lanes // CHUNK, unroll=UNROLL)
    def _(k):
        at = pl.multiple_of(k * CHUNK, CHUNK)
        ones = spreader(at, CHUNK, radial, dirs)
        row = 0
        for out in outs:
            count = out.shape[0]
            left = packed[pl.ds(row, count), :]
            out[:, pl.ds(at, CHUNK)] = jnp.dot(left, ones, preferred_element_type=F32)
            row += count


def blocks_of(design):
    dirs = design.shape[1]
    row = lax.broadcasted_iota(jnp.int32, (CHUNK, dirs), 0)
    col = lax.broadcasted_iota(jnp.int32, (CHUNK, dirs), 1)
    pick = jnp.where((row & (dirs - 1)) == col, 1.0, 0.0).astype(BF16)
    tiled = jnp.dot(pick, design, preferred_element_type=F32).astype(BF16)
    tiled = lax.dot_general(tiled, pick, (((1,), (1,)), ((), ())), preferred_element_type=F32)
    row = lax.broadcasted_iota(jnp.int32, (CHUNK, CHUNK), 0)
    col = lax.broadcasted_iota(jnp.int32, (CHUNK, CHUNK), 1)
    shift = dirs.bit_length() - 1
    return jnp.where((row >> shift) == (col >> shift), tiled, 0.0).astype(BF16)


def wall(radial):
    lane = lax.broadcasted_iota(jnp.int32, (1, radial), 1)
    return jnp.where(lane < radial - 1, 1.0, 0.0)


def ahead_x(rows, last):
    n = rows.shape[0]
    at = lax.broadcasted_iota(jnp.int32, rows.shape, 0)
    return jnp.where(at == n - 1, last, pltpu.roll(rows, n - 1, 0))


def behind_x(rows, first):
    at = lax.broadcasted_iota(jnp.int32, rows.shape, 0)
    return jnp.where(at == 0, first, pltpu.roll(rows, 1, 0))


def ahead_r(rows, dirs):
    return pltpu.roll(rows, rows.shape[1] - dirs, 1)


def behind_r(rows, dirs):
    return pltpu.roll(rows, dirs, 1)


def even_az():
    return lax.rem(lax.axis_index("az"), 2) == 0


def radial_weights(radial):
    return (lax.broadcasted_iota(jnp.int32, (1, radial), 1).astype(F32) + 0.5) / radial


EDGE = ((0, 0), (0, 2), (0, 3), (1, 0), (1, 3), (2, 0), (2, 3))


def edge_kernel(
    tangent, velocity, frac, branch, basis, design, exit_film,
    msg_e, msg_o, sums, field, vel, share, kind, left, weights, film,
    mat, vel_tan, packed, spread, work, ends, edge, faces, face_a, sems,
):
    cells, rows, lanes = field.shape
    radial = vel.shape[-1]
    dirs = lanes // radial
    last, end = cells - 1, rows - 1
    inner = wall(radial)
    pairs = [
        (exit_film, film), (design, mat), (velocity, vel), (branch, kind), (frac, share), (tangent, field), (basis, left),
    ]
    copies = [pltpu.make_async_copy(src, dst, sems.at[i]) for i, (src, dst) in enumerate(pairs)]
    for copy in copies:
        copy.start()
    copies[0].wait()
    sums[...] = jnp.full(sums.shape, jnp.sum(film[...] * radial_weights(radial)), F32)
    copies[1].wait()
    weights[...] = blocks_of(mat[...])
    for copy in copies[2:5]:
        copy.wait()

    at = {}
    row = 0
    for c, a in EDGE:
        low, high = mix(vel[c, a], kind[0, c, a])
        if (c, a) == (0, last):
            high_a = high
        if c == 1:
            at["high", a] = high
        for name, part in zip("plh", (share[0, c, a], low, high), strict=True):
            packed[pl.ds(row, rows), :] = two_terms(part * inner if c == 2 else part)
            at[name, c, a] = row
            row += rows
    low_2, high_2 = mix(vel[0, last], kind[1, 0, last])
    for name, part in zip("pl", (share[1, 0, last], low_2), strict=True):
        packed[pl.ds(row, rows), :] = two_terms(part)
        at[name] = row
        row += rows
    spread_all(packed, [spread], radial, dirs)

    for copy in copies[5:]:
        copy.wait()

    @pl.loop(0, lanes // CHUNK, unroll=UNROLL)
    def _(k):
        lane = pl.ds(pl.multiple_of(k * CHUNK, CHUNK), CHUNK)
        part = jnp.concatenate([left[c, a, :, lane] for c, a in EDGE], axis=0)
        vel_tan[:, lane] = jnp.dot(part, weights[...], preferred_element_type=F32).astype(BF16)

    def sp(*key):
        return spread[pl.ds(at[key], rows), :]

    def speed(c, a):
        return vel_tan[pl.ds(EDGE.index((c, a)) * rows, rows), :].astype(F32)

    def along_az(a):
        f = field[a]
        face = speed(0, a) * sp("p", 0, a) + sp("l", 0, a) * f
        return face if a == last else face + sp("h", 0, a) * field[a + 1]

    faces[0] = along_az(0)
    faces[1] = along_az(last - 1)
    face_a[...] = along_az(last)
    for i, a in enumerate((0, last)):
        f = field[a]
        change = faces[0] if a == 0 else face_a[...] - faces[1]
        face = speed(1, a) * sp("p", 1, a) + sp("l", 1, a) * f + sp("h", 1, a) * ahead_x(f, 0.0)
        ends[pl.ds(i, 1), :] = face[end:, :]
        change = change + (face - behind_x(face, 0.0))
        face = speed(2, a) * sp("p", 2, a) + sp("l", 2, a) * f + sp("h", 2, a) * ahead_r(f, dirs)
        change = change + (face - behind_r(face, dirs))
        edge[i] = f - change
    work[...] = speed(0, last) * spread[pl.ds(at["p"], rows), :] + spread[pl.ds(at["l"], rows), :] * edge[1]

    def small_rows(msg, lane, block):
        for k in range(lanes // CHUNK):
            msg[pl.ds(2 * rows + k, 1), pl.ds(lane, CHUNK)] = block[:, k * CHUNK:(k + 1) * CHUNK]

    def halves(msg, lane, block):
        for k in range(rows // 8):
            msg[pl.ds(2 * rows, 8), pl.ds(lane + 128 * k, radial)] = block[8 * k:8 * k + 8]

    def fill(up_msg, down_msg):
        for msg in (up_msg, down_msg):
            msg[pl.ds(2 * rows, 8), :] = jnp.zeros((8, lanes), F32)
        up_msg[pl.ds(0, rows), :] = face_a[...]
        up_msg[pl.ds(rows, rows), :] = work[...]
        halves(up_msg, AT_C1, high_a)
        halves(up_msg, AT_B2, low_2)
        halves(up_msg, AT_C2, high_2)
        small_rows(up_msg, AT_ROW_A, ends[pl.ds(1, 1), :])
        small_rows(up_msg, AT_ROW_B, field[last, pl.ds(0, 1), :])
        small_rows(up_msg, AT_FIRST, sp("h", 0, last)[0:1])
        small_rows(up_msg, AT_END, sp("h", 0, last)[end:])
        up_msg[pl.ds(2 * rows, 1), pl.ds(AT_COEF, radial)] = at["high", last][end:, :]
        down_msg[pl.ds(0, rows), :] = field[0]
        down_msg[pl.ds(rows, rows), :] = edge[0]
        small_rows(down_msg, AT_ROW_A, ends[pl.ds(0, 1), :])
        down_msg[pl.ds(2 * rows, 1), pl.ds(AT_COEF, radial)] = at["high", 0][end:, :]

    even = even_az()

    @pl.when(even)
    def _():
        fill(msg_e, msg_o)

    @pl.when(jnp.logical_not(even))
    def _():
        fill(msg_o, msg_e)


MIDDLE = dict(
    ends=0, end_fixed=4, low_end=8, first=12, partial_first=16, partial_end=20, front=24, coef_a=26, coefs=28
)


def local_kernel(
    field, vel, share, kind, left, weights, film,
    vel_tan, middle, partial, edges, row_film,
    product, packed, spread, sems,
):
    cells, rows, lanes = field.shape
    radial = vel.shape[-1]
    dirs = lanes // radial
    n = cells * rows
    last, end = cells - 1, rows - 1
    inner = wall(radial)
    for c in range(3):
        low, high = mix(vel[c], kind[0, c])
        for k, part in enumerate((share[0, c], low, high)):
            part = part.reshape(n, radial)
            packed[pl.ds((k * 3 + c) * n, n), :] = two_terms(part * inner if c == 2 else part)
        if c == 1:
            high_1 = high
    low_2, high_2 = mix(vel[1], kind[1, 1])
    tail = [share[1, 1, :, end, :], low_2[:, end, :], jnp.zeros((8, radial), F32)]
    packed[pl.ds(9 * n, 16), :] = two_terms(jnp.concatenate(tail, axis=0))
    middle[pl.ds(MIDDLE["coefs"], 1), :] = jnp.zeros((1, lanes), F32)
    for start, part in ((0, high_1), (6, low_2), (10, high_2)):
        for a in range(cells):
            middle[pl.ds(MIDDLE["coefs"], 1), pl.ds(128 * (start + a), radial)] = part[a, end:, :]
    spread_all(packed, [spread], radial, dirs)

    @pl.loop(0, lanes // CHUNK, unroll=UNROLL)
    def _(k):
        lane = pl.ds(pl.multiple_of(k * CHUNK, CHUNK), CHUNK)
        block = jnp.dot(left[:, :, :, lane].reshape(3 * n, CHUNK), weights[...], preferred_element_type=F32)
        product[:, :, :, lane] = block.astype(BF16).reshape(3, cells, rows, CHUNK)

    output = pltpu.make_async_copy(product, vel_tan, sems.at[0])
    output.start()

    def sp(k, c, a):
        return spread[pl.ds((k * 3 + c) * n + a * rows, rows), :]

    def speed(c, a):
        return product[c, a].astype(F32)

    def put(name, a, block):
        middle[pl.ds(MIDDLE[name] + a, block.shape[0]), :] = block

    before = None
    for a in range(cells):
        f = field[a]
        here = speed(0, a) * sp(0, 0, a) + sp(1, 0, a) * f
        if a < last:
            here = here + sp(2, 0, a) * field[a + 1]
        change = here if before is None else here - before
        before = here
        speed_x = speed(1, a)
        face = speed_x * sp(0, 1, a) + sp(1, 1, a) * f + sp(2, 1, a) * ahead_x(f, 0.0)
        put("ends", a, face[end:])
        edges[pl.ds(2 * rows + a, 1), :] = face[end:]
        change = change + (face - behind_x(face, 0.0))
        face = speed(2, a) * sp(0, 2, a) + sp(1, 2, a) * f + sp(2, 2, a) * ahead_r(f, dirs)
        change = change + (face - behind_r(face, dirs))
        block = f - change
        partial[a] = block
        put("first", a, f[0:1])
        edges[pl.ds(2 * rows + 4 + a, 1), :] = f[0:1]
        put("partial_first", a, block[0:1])
        put("partial_end", a, block[end:])
        put("low_end", a, spread[pl.ds(9 * n + cells + a, 1), :])
        put("end_fixed", a, speed_x[end:] * spread[pl.ds(9 * n + a, 1), :])
        edges[pl.ds(2 * rows + 8 + a, 1), :] = sp(2, 1, a)[end:]
    edges[pl.ds(0, rows), :] = before
    edges[pl.ds(2 * rows + 12, 4), :] = jnp.zeros((4, lanes), F32)
    edges[pl.ds(2 * rows + 16, rows), :] = field[0]
    edges[pl.ds(rows, rows), :] = sp(2, 0, last)
    for k, x in enumerate((0, end)):
        put("front", k, field[0, pl.ds(x, 1), :])
        put("coef_a", k, sp(2, 0, last)[x:x + 1])
    total = jnp.sum(film[...] * radial_weights(radial), axis=1, keepdims=True)
    row_film[...] = jnp.broadcast_to(total, row_film.shape)
    output.wait()


def step_kernel(
    vel_tan, vel, share, kind, after,
    coef_2, fixed,
    product, packed, spread, mixed, sems,
):
    del after
    _, cells, rows, lanes = product.shape
    radial = vel.shape[-1]
    dirs = lanes // radial
    n = cells * rows
    inner = wall(radial)
    fetch = pltpu.make_async_copy(vel_tan, product, sems.at[0])
    fetch.start()
    for c in range(3):
        for k, part in enumerate((share[1, c], *mix(vel[c], kind[1, c]))):
            part = part.reshape(n, radial)
            part = two_terms(part * inner if c == 2 else part)
            if k == 0:
                packed[pl.ds(c * n, n), :] = part
                continue
            for a in range(cells):
                row = 3 * n + ((a * 2 + k - 1) * 3 + c) * rows
                packed[pl.ds(row, rows), :] = part[a * rows:(a + 1) * rows]
    copies = []
    for k in range(lanes // CHUNK):
        lane = pl.ds(k * CHUNK, CHUNK)
        ones = spreader(k * CHUNK, CHUNK, radial, dirs)
        mixed[:, lane] = jnp.dot(packed[pl.ds(3 * n, 6 * n), :], ones, preferred_element_type=F32)
        copies.append(pltpu.make_async_copy(mixed.at[:, lane], coef_2.at[:, lane], sems.at[1 + k]))
        copies[k].start()
        spread[:, lane] = jnp.dot(packed[pl.ds(0, 3 * n), :], ones, preferred_element_type=F32)
    fetch.wait()
    before = None
    for a in range(cells):
        faces = [product[c, a].astype(F32) * spread[pl.ds(c * n + a * rows, rows), :] for c in range(3)]
        change = faces[0] if before is None else faces[0] - before
        before = faces[0]
        change = change + (faces[1] - behind_x(faces[1], 0.0))
        fixed[a] = change + (faces[2] - behind_r(faces[2], dirs))
    for copy in copies:
        copy.wait()


def gathered_row(msg, row, lane, lanes):
    return jnp.concatenate([msg[pl.ds(row + k, 1), pl.ds(lane, CHUNK)] for k in range(lanes // CHUNK)], axis=1)


def middle_kernel(
    middle, in_e, in_o,
    msg_e, msg_o, film_msg,
):
    cells, rows, lanes = CELLS, (in_e.shape[0] - 8) // 2, in_e.shape[1]
    radial, dirs = RADIAL, lanes // RADIAL
    last, end = cells - 1, rows - 1

    def take(name, count=CELLS, at=0):
        return middle[pl.ds(MIDDLE[name] + at, count), :]

    even = even_az()

    def work(up, down, out_up, out_down):
        at_a = lax.broadcasted_iota(jnp.int32, (cells, 1), 0)
        partial_x = []
        for k, (x, lane, name) in enumerate(((0, AT_FIRST, "partial_first"), (end, AT_END, "partial_end"))):
            face = up[pl.ds(x, 1), :] + gathered_row(up, 2 * rows, lane, lanes) * take("front", 1, k)
            beyond = take("coef_a", 1, k) * down[pl.ds(x, 1), :]
            partial_x.append(take(name) + jnp.where(at_a == 0, face, 0.0) - jnp.where(at_a == last, beyond, 0.0))
        second = take("end_fixed") + take("low_end") * partial_x[1]

        lane = lax.broadcasted_iota(jnp.int32, (1, lanes), 1)
        weight = ((lane // dirs).astype(F32) + 0.5) / radial
        raw = (take("ends") + second) * weight
        film = raw[:, 0:128]
        for k in range(1, lanes // 128):
            film = film + raw[:, 128 * k:128 * k + 128]
        shift = 64
        while shift >= dirs:
            film = film + pltpu.roll(film, shift, 1)
            shift //= 2
        film_msg[...] = jnp.zeros(film_msg.shape, F32)
        film_msg[pl.ds(0, cells), :] = film

        def finish(up_msg, down_msg):
            for msg in (up_msg, down_msg):
                msg[1, pl.ds(2, 2), :] = jnp.zeros((2, lanes), F32)
                for a in range(cells):
                    msg[1, pl.ds(3, 1), pl.ds(128 * a, 128)] = film[a:a + 1]
            up_msg[0] = take("ends")
            up_msg[1, pl.ds(0, 1), :] = gathered_row(up, 2 * rows, AT_ROW_A, lanes)
            up_msg[1, pl.ds(1, 1), :] = gathered_row(down, 2 * rows, AT_ROW_A, lanes)
            up_msg[1, pl.ds(2, 1), :] = take("coefs", 1)
            up_msg[1, pl.ds(2, 1), pl.ds(128 * 4, radial)] = up[pl.ds(2 * rows, 1), pl.ds(AT_COEF, radial)]
            up_msg[1, pl.ds(2, 1), pl.ds(128 * 5, radial)] = down[pl.ds(2 * rows, 1), pl.ds(AT_COEF, radial)]
            up_msg[2] = second
            down_msg[0] = take("first")
            down_msg[1, pl.ds(0, 1), :] = gathered_row(up, 2 * rows, AT_ROW_B, lanes)
            down_msg[1, pl.ds(1, 1), :] = down[pl.ds(0, 1), :]
            down_msg[2] = partial_x[0]

        even_x = lax.rem(lax.axis_index("ax"), 2) == 0

        @pl.when(even_x)
        def _():
            finish(out_up, out_down)

        @pl.when(jnp.logical_not(even_x))
        def _():
            finish(out_down, out_up)

    @pl.when(even)
    def _():
        work(in_o, in_e, msg_e, msg_o)

    @pl.when(jnp.logical_not(even))
    def _():
        work(in_e, in_o, msg_e, msg_o)


def last_kernel(
    coef_2, partial, fixed, edges, in_e, in_o, x_o, x_e,
    out,
    packed, spread, up, down, below, above, now, edge, result, mixed, sems,
):
    cells, rows, lanes = partial.shape
    radial = packed.shape[1] // 2
    dirs = lanes // radial
    n = cells * rows
    last, end = cells - 1, rows - 1
    even = even_az()
    place = lax.axis_index("ax")
    even_x = lax.rem(place, 2) == 0
    final = lax.axis_size("ax") - 1
    layer = 6 * rows
    loads = [
        pltpu.make_async_copy(coef_2.at[pl.ds(a * layer, layer)], mixed.at[pl.ds(a * layer, layer)], sems.at[cells + a])
        for a in range(cells)
    ]
    for copy in loads:
        copy.start()

    @pl.when(even)
    def _():
        up[...] = in_o[...]
        down[...] = in_e[...]

    @pl.when(jnp.logical_not(even))
    def _():
        up[...] = in_e[...]
        down[...] = in_o[...]

    @pl.when(even_x)
    def _():
        below[...] = jnp.where(place == 0, 0.0, x_o[...])
        above[...] = x_e[...]

    @pl.when(jnp.logical_not(even_x))
    def _():
        below[...] = x_e[...]
        above[...] = jnp.where(place == final, 0.0, x_o[...])

    face_a, coef_a = edges[pl.ds(0, rows), :], edges[pl.ds(rows, rows), :]
    ends, first, coef_x = (edges[pl.ds(2 * rows + 4 * k, cells), :] for k in range(3))

    def joined(msg, lane):
        return jnp.concatenate([msg[pl.ds(2 * rows, 8), pl.ds(lane + 128 * k, radial)] for k in range(rows // 8)], axis=0)

    for k, lane in enumerate((AT_C1, AT_B2, AT_C2)):
        packed[pl.ds(k * rows, rows), :] = two_terms(joined(up, lane))
    singles = [below[1, pl.ds(2, 1), pl.ds(128 * k, radial)] for k in range(14)]
    singles += [msg[pl.ds(2 * rows, 1), pl.ds(AT_COEF, radial)] for msg in (up, down)]
    packed[pl.ds(3 * rows, 16), :] = two_terms(jnp.concatenate(singles, axis=0))
    spread_all(packed, [spread], radial, dirs)
    in_c1, in_b2, in_c2 = (spread[pl.ds(k * rows, rows), :] for k in range(3))
    below_c = spread[pl.ds(3 * rows, 6), :]
    below_b2, below_c2 = spread[pl.ds(3 * rows + 6, 4), :], spread[pl.ds(3 * rows + 10, 4), :]
    own_c = jnp.concatenate([coef_x, spread[pl.ds(3 * rows + 14, 2), :]], axis=0)

    starts = jnp.concatenate([first, gathered_row(up, 2 * rows, AT_ROW_B, lanes), down[pl.ds(0, 1), :]], axis=0)
    enter = jnp.concatenate([below[0], below[1, pl.ds(0, 2), :]], axis=0) + below_c * starts
    leave = own_c * jnp.concatenate([above[0], above[1, pl.ds(0, 2), :]], axis=0)
    crossing = in_c1 * edges[pl.ds(2 * rows + 16, rows), :]
    beyond = coef_a * down[pl.ds(0, rows), :]
    at_x = lax.broadcasted_iota(jnp.int32, (rows, 1), 0)

    def with_edges(block, k):
        return block + jnp.where(at_x == 0, enter[k:k + 1], 0.0) - jnp.where(at_x == end, leave[k:k + 1], 0.0)

    for a in range(cells):
        f = partial[a]
        if a == 0:
            f = f + up[pl.ds(0, rows), :] + crossing
        if a == last:
            f = f - beyond
        now[a] = with_edges(f, a)
    now[cells] = with_edges(down[pl.ds(rows, rows), :] + face_a + beyond, 5)
    lower = up[pl.ds(rows, rows), :] + in_b2 * (
        jnp.where(at_x == 0, enter[4:5], 0.0) - jnp.where(at_x == end, leave[4:5], 0.0) - crossing
    )
    before = lower + in_c2 * now[0]

    first_now = jnp.concatenate([now[a, pl.ds(0, 1), :] for a in range(cells)], axis=0)
    enter_2 = below[2] - below_b2 * (below_c[0:4] * first) + below_c2 * first_now
    inside = jnp.where(place == final, 0.0, 1.0)
    edge[...] = inside * (above[2] + ends + leave[0:4])

    def low(c, a):
        return mixed[pl.ds((a * 6 + c) * rows, rows), :]

    def high(c, a):
        return mixed[pl.ds((a * 6 + 3 + c) * rows, rows), :]

    copies = []
    for a in range(cells):
        loads[a].wait()
        f = now[a]
        face = low(0, a) * f + high(0, a) * now[a + 1]
        change = fixed[a] + (face - before)
        before = face
        face = low(1, a) * f + high(1, a) * ahead_x(f, edge[pl.ds(a, 1), :])
        change = change + (face - behind_x(face, enter_2[a:a + 1]))
        face = low(2, a) * f + high(2, a) * ahead_r(f, dirs)
        change = change + (face - behind_r(face, dirs))
        result[a] = f - change
        copies.append(pltpu.make_async_copy(result.at[a], out.at[a], sems.at[a]))
        copies[a].start()

    for copy in copies:
        copy.wait()


def film_kernel(done, row_film, film_own, film_1, x_o, x_e, totals, film_out):
    del done
    cells, share = film_out.shape
    place = lax.axis_index("ax")
    mean = jnp.sum(totals[:, 0:1, :], axis=0) / (cells * totals.shape[0])
    factor = mean / row_film[...]
    for k, source in enumerate((x_o, film_1, x_e, film_own)):

        @pl.when(place == k)
        def _():
            if len(source.shape) == 2:
                film = source[pl.ds(0, cells), :]
            else:
                film = jnp.concatenate([source[1, pl.ds(3, 1), pl.ds(128 * a, 128)] for a in range(cells)], axis=0)
            film_out[...] = (film * factor)[:, k * share:(k + 1) * share]


def swap(value, axis, pairing):
    count = lax.axis_size(axis)
    if axis == "ax":
        other = [i ^ pairing for i in range(count)]
    elif pairing == 0:
        other = [i ^ 1 for i in range(count)]
    else:
        other = [(i - 1 if i % 2 == 0 else i + 1) % count for i in range(count)]
    return lax.ppermute(value, axis, list(enumerate(other)))


def pinned(value, space):
    return pltpu.with_memory_space_constraint(value, space)


def placed(space, shape, dtype):
    return space(shape, dtype)


def call(kernel, args, outs, scratch, in_hbm=0, out_hbm=0, free=0, sems=0, cost=None):
    vmem, hbm = pl.BlockSpec(memory_space=pltpu.VMEM), pl.BlockSpec(memory_space=pl.ANY)
    shapes = [pltpu.VMEM(shape, dtype) for shape, dtype in scratch]
    pinned_outs = len(outs) - free
    shapes_out = [placed(pltpu.HBM if i < out_hbm else pltpu.VMEM, *out) for i, out in enumerate(outs[:pinned_outs])]
    shapes_out += [jax.ShapeDtypeStruct(*out) for out in outs[pinned_outs:]]
    args = [pinned(arg, pltpu.HBM if i < in_hbm else pltpu.VMEM) for i, arg in enumerate(args)]
    if sems:
        shapes.append(pltpu.SemaphoreType.DMA((sems,)))
    return pl.pallas_call(
        kernel,
        out_shape=shapes_out,
        in_specs=[hbm] * in_hbm + [vmem] * (len(args) - in_hbm),
        out_specs=[hbm] * out_hbm + [vmem] * (len(outs) - out_hbm),
        scratch_shapes=shapes,
        compiler_params=pltpu.CompilerParams(vmem_limit_bytes=32 * 2**20),
        cost_estimate=cost,
        name=kernel.__name__,
    )(*args)


def local(tangent, velocity, face_frac, branch, basis, design, exit_film):
    cells, rows, lanes = tangent.shape
    radial = velocity.shape[-1]
    dirs = design.shape[1]
    n = cells * rows
    devices = lax.axis_size("az")
    layer, cell_layer = (rows, lanes), (rows, radial)
    z_msg, x_msg, line = (2 * rows + 8, lanes), (3, cells, lanes), (cells, lanes)
    inputs = (tangent, velocity, face_frac, branch, basis, design, exit_film)
    count = (3 * len(EDGE) + 2) * rows
    kept = [(value.shape, value.dtype) for value in inputs]
    kept[5] = ((CHUNK, CHUNK), BF16)
    z_e, z_o, sums, field, vel, share, kind, left, weights, film_in = call(
        edge_kernel,
        inputs,
        [(z_msg, F32), (z_msg, F32), ((devices, 2, 128), F32)] + kept,
        [
            (design.shape, BF16), ((len(EDGE) * rows, lanes), BF16), ((count, 2 * radial), BF16), ((count, lanes), F32), (layer, F32),
            ((2, lanes), F32), ((2, *layer), F32), ((2, *layer), F32), (layer, F32),
        ],
        in_hbm=7,
        sems=7,
    )
    in_e, in_o = swap(z_e, "az", 0), swap(z_o, "az", 1)
    totals = lax.all_to_all(sums, "az", 0, 0)
    velocity_tangent, middle, partial, edges, row_film = call(
        local_kernel,
        (field, vel, share, kind, left, weights, film_in),
        [
            (basis.shape, BF16), ((32, lanes), F32), (tangent.shape, F32), ((3 * rows + 16, lanes), F32),
            ((cells, 128), F32),
        ],
        [(basis.shape, BF16), ((9 * n + 16, 2 * radial), BF16), ((9 * n + 16, lanes), F32)],
        out_hbm=1,
        sems=1,
        cost=pl.CostEstimate(flops=10**9, bytes_accessed=10 * 10**6, transcendentals=0),
    )
    x_e, x_o, film = call(
        middle_kernel, (middle, in_e, in_o), [(x_msg, F32), (x_msg, F32), ((8, 128), F32)], []
    )
    from_o, from_e, film_1 = swap(x_o, "ax", 3), swap(x_e, "ax", 1), swap(film, "ax", 2)
    coef_2, fixed = call(
        step_kernel,
        (velocity_tangent, vel, share, kind, film),
        [((6 * n, lanes), F32), (tangent.shape, F32)],
        [(basis.shape, BF16), ((9 * n, 2 * radial), BF16), ((3 * n, lanes), F32), ((6 * n, lanes), F32)],
        in_hbm=1,
        out_hbm=1,
        sems=1 + lanes // CHUNK,
        cost=pl.CostEstimate(flops=10**9, bytes_accessed=10 * 10**6, transcendentals=0),
    )
    count = 3 * rows + 16
    (out,) = call(
        last_kernel,
        (coef_2, partial, fixed, edges, in_e, in_o, from_o, from_e),
        [(tangent.shape, F32)],
        [
            ((count, 2 * radial), BF16), ((count, lanes), F32), (z_msg, F32), (z_msg, F32), (x_msg, F32), (x_msg, F32),
            ((cells + 1, *layer), F32), (line, F32), (tangent.shape, F32), ((6 * n, lanes), F32),
        ],
        in_hbm=1,
        out_hbm=1,
        sems=2 * cells,
    )
    (film_out,) = call(
        film_kernel,
        (out, row_film, film, film_1, from_o, from_e, totals),
        [((cells, dirs // lax.axis_size("ax")), F32)],
        [],
        in_hbm=1,
        free=1,
    )
    return out, velocity_tangent, film_out


def solution(mesh):
    in_specs = (
        P("az", "ax", None),
        P(None, "az", "ax", None),
        P(None, None, "az", "ax", None),
        P(None, None, "az", "ax", None),
        P(None, "az", "ax", None),
        P(),
        P("az", None),
    )
    out_specs = (P("az", "ax", None), P(None, "az", "ax", None), P("az", "ax"))
    return jax.shard_map(local, mesh=mesh, in_specs=in_specs, out_specs=out_specs, check_vma=False)
```

```python
import jax
import jax.numpy as jnp
from jax import lax
from jax.experimental import pallas as pl
from jax.experimental.pallas import tpu as pltpu
from jax.sharding import PartitionSpec as P

F32, BF16 = jnp.float32, jnp.bfloat16
CHUNK = 256
RADIAL = 64
CELLS = 4
UNROLL = 8
AT_C1, AT_B2, AT_C2, AT_ROW_A, AT_ROW_B, AT_COEF, AT_FIRST, AT_END = 0, 256, 512, 768, 1024, 1280, 1408, 1664


def mix(speed, branch):
    part = speed * (0.25 * branch.astype(F32))
    rest = speed - part
    ahead = speed > 0
    return jnp.where(ahead, rest, part), jnp.where(ahead, part, rest)


def two_terms(values):
    high = values.astype(BF16)
    low = (values - high.astype(F32)).astype(BF16)
    return jnp.concatenate([high, low], axis=-1)


def spreader(offset, lanes, radial, dirs):
    row = lax.broadcasted_iota(jnp.int32, (2 * radial, lanes), 0)
    lane = lax.broadcasted_iota(jnp.int32, (2 * radial, lanes), 1) + offset
    shift = dirs.bit_length() - 1
    return jnp.where((row & (radial - 1)) == (lane >> shift), 1.0, 0.0).astype(BF16)


def spread_all(packed, outs, radial, dirs):
    lanes = outs[0].shape[1]

    @pl.loop(0, lanes // CHUNK, unroll=UNROLL)
    def _(k):
        at = pl.multiple_of(k * CHUNK, CHUNK)
        ones = spreader(at, CHUNK, radial, dirs)
        row = 0
        for out in outs:
            count = out.shape[0]
            left = packed[pl.ds(row, count), :]
            out[:, pl.ds(at, CHUNK)] = jnp.dot(left, ones, preferred_element_type=F32)
            row += count


def blocks_of(design):
    dirs = design.shape[1]
    row = lax.broadcasted_iota(jnp.int32, (CHUNK, dirs), 0)
    col = lax.broadcasted_iota(jnp.int32, (CHUNK, dirs), 1)
    pick = jnp.where((row & (dirs - 1)) == col, 1.0, 0.0).astype(BF16)
    tiled = jnp.dot(pick, design, preferred_element_type=F32).astype(BF16)
    tiled = lax.dot_general(tiled, pick, (((1,), (1,)), ((), ())), preferred_element_type=F32)
    row = lax.broadcasted_iota(jnp.int32, (CHUNK, CHUNK), 0)
    col = lax.broadcasted_iota(jnp.int32, (CHUNK, CHUNK), 1)
    shift = dirs.bit_length() - 1
    return jnp.where((row >> shift) == (col >> shift), tiled, 0.0).astype(BF16)


def wall(radial):
    lane = lax.broadcasted_iota(jnp.int32, (1, radial), 1)
    return jnp.where(lane < radial - 1, 1.0, 0.0)


def ahead_x(rows, last):
    n = rows.shape[0]
    at = lax.broadcasted_iota(jnp.int32, rows.shape, 0)
    return jnp.where(at == n - 1, last, pltpu.roll(rows, n - 1, 0))


def behind_x(rows, first):
    at = lax.broadcasted_iota(jnp.int32, rows.shape, 0)
    return jnp.where(at == 0, first, pltpu.roll(rows, 1, 0))


def ahead_r(rows, dirs):
    return pltpu.roll(rows, rows.shape[1] - dirs, 1)


def behind_r(rows, dirs):
    return pltpu.roll(rows, dirs, 1)


def even_az():
    return lax.rem(lax.axis_index("az"), 2) == 0


def radial_weights(radial):
    return (lax.broadcasted_iota(jnp.int32, (1, radial), 1).astype(F32) + 0.5) / radial


EDGE = ((0, 0), (0, 2), (0, 3), (1, 0), (1, 3), (2, 0), (2, 3))


def edge_kernel(
    tangent, velocity, frac, branch, basis, design, exit_film,
    msg_e, msg_o, sums, field, vel, share, kind, left, weights, film,
    mat, vel_tan, packed, spread, work, ends, edge, faces, face_a, sems,
):
    cells, rows, lanes = field.shape
    radial = vel.shape[-1]
    dirs = lanes // radial
    last, end = cells - 1, rows - 1
    inner = wall(radial)
    blocks = [(c, a) for c in range(3) for a in range(cells)]
    later = [block for block in blocks if block not in EDGE]
    pairs = [(exit_film, film), (design, mat), (velocity, vel)]
    pairs += [(src.at[at], dst.at[at]) for src, dst in ((branch, kind), (frac, share)) for at in (0, (1, 0))]
    pairs += [(tangent, field)] + [(basis.at[at], left.at[at]) for at in EDGE]
    needed = len(pairs)
    pairs += [(src.at[1, c], dst.at[1, c]) for src, dst in ((branch, kind), (frac, share)) for c in (1, 2)]
    pairs += [(basis.at[at], left.at[at]) for at in later]
    copies = [pltpu.make_async_copy(src, dst, sems.at[i]) for i, (src, dst) in enumerate(pairs)]
    for copy in copies:
        copy.start()
    copies[0].wait()
    sums[...] = jnp.full(sums.shape, jnp.sum(film[...] * radial_weights(radial)), F32)
    copies[1].wait()
    weights[...] = blocks_of(mat[...])
    for copy in copies[2:7]:
        copy.wait()

    at = {}
    row = 0
    for c, a in EDGE:
        low, high = mix(vel[c, a], kind[0, c, a])
        if (c, a) == (0, last):
            high_a = high
        if c == 1:
            at["high", a] = high
        for name, part in zip("plh", (share[0, c, a], low, high), strict=True):
            packed[pl.ds(row, rows), :] = two_terms(part * inner if c == 2 else part)
            at[name, c, a] = row
            row += rows
    low_2, high_2 = mix(vel[0, last], kind[1, 0, last])
    for name, part in zip("pl", (share[1, 0, last], low_2), strict=True):
        packed[pl.ds(row, rows), :] = two_terms(part)
        at[name] = row
        row += rows
    spread_all(packed, [spread], radial, dirs)

    for copy in copies[7:needed]:
        copy.wait()

    @pl.loop(0, lanes // CHUNK, unroll=UNROLL)
    def _(k):
        lane = pl.ds(pl.multiple_of(k * CHUNK, CHUNK), CHUNK)
        part = jnp.concatenate([left[c, a, :, lane] for c, a in EDGE], axis=0)
        vel_tan[:, lane] = jnp.dot(part, weights[...], preferred_element_type=F32).astype(BF16)

    def sp(*key):
        return spread[pl.ds(at[key], rows), :]

    def speed(c, a):
        return vel_tan[pl.ds(EDGE.index((c, a)) * rows, rows), :].astype(F32)

    def along_az(a):
        f = field[a]
        face = speed(0, a) * sp("p", 0, a) + sp("l", 0, a) * f
        return face if a == last else face + sp("h", 0, a) * field[a + 1]

    faces[0] = along_az(0)
    faces[1] = along_az(last - 1)
    face_a[...] = along_az(last)
    for i, a in enumerate((0, last)):
        f = field[a]
        change = faces[0] if a == 0 else face_a[...] - faces[1]
        face = speed(1, a) * sp("p", 1, a) + sp("l", 1, a) * f + sp("h", 1, a) * ahead_x(f, 0.0)
        ends[pl.ds(i, 1), :] = face[end:, :]
        change = change + (face - behind_x(face, 0.0))
        face = speed(2, a) * sp("p", 2, a) + sp("l", 2, a) * f + sp("h", 2, a) * ahead_r(f, dirs)
        change = change + (face - behind_r(face, dirs))
        edge[i] = f - change
    work[...] = speed(0, last) * spread[pl.ds(at["p"], rows), :] + spread[pl.ds(at["l"], rows), :] * edge[1]

    def small_rows(msg, lane, block):
        for k in range(lanes // CHUNK):
            msg[pl.ds(2 * rows + k, 1), pl.ds(lane, CHUNK)] = block[:, k * CHUNK:(k + 1) * CHUNK]

    def halves(msg, lane, block):
        for k in range(rows // 8):
            msg[pl.ds(2 * rows, 8), pl.ds(lane + 128 * k, radial)] = block[8 * k:8 * k + 8]

    def fill(up_msg, down_msg):
        for msg in (up_msg, down_msg):
            msg[pl.ds(2 * rows, 8), :] = jnp.zeros((8, lanes), F32)
        up_msg[pl.ds(0, rows), :] = face_a[...]
        up_msg[pl.ds(rows, rows), :] = work[...]
        halves(up_msg, AT_C1, high_a)
        halves(up_msg, AT_B2, low_2)
        halves(up_msg, AT_C2, high_2)
        small_rows(up_msg, AT_ROW_A, ends[pl.ds(1, 1), :])
        small_rows(up_msg, AT_ROW_B, field[last, pl.ds(0, 1), :])
        small_rows(up_msg, AT_FIRST, sp("h", 0, last)[0:1])
        small_rows(up_msg, AT_END, sp("h", 0, last)[end:])
        up_msg[pl.ds(2 * rows, 1), pl.ds(AT_COEF, radial)] = at["high", last][end:, :]
        down_msg[pl.ds(0, rows), :] = field[0]
        down_msg[pl.ds(rows, rows), :] = edge[0]
        small_rows(down_msg, AT_ROW_A, ends[pl.ds(0, 1), :])
        down_msg[pl.ds(2 * rows, 1), pl.ds(AT_COEF, radial)] = at["high", 0][end:, :]

    even = even_az()

    @pl.when(even)
    def _():
        fill(msg_e, msg_o)

    @pl.when(jnp.logical_not(even))
    def _():
        fill(msg_o, msg_e)

    for copy in copies[needed:]:
        copy.wait()


MIDDLE = dict(
    ends=0, end_fixed=4, low_end=8, first=12, partial_first=16, partial_end=20, front=24, coef_a=26, coefs=28
)


def local_kernel(
    field, vel, share, kind, left, weights, film,
    vel_tan, middle, partial, edges, row_film,
    product, packed, spread, sems,
):
    cells, rows, lanes = field.shape
    radial = vel.shape[-1]
    dirs = lanes // radial
    n = cells * rows
    last, end = cells - 1, rows - 1
    inner = wall(radial)
    for c in range(3):
        low, high = mix(vel[c], kind[0, c])
        for k, part in enumerate((share[0, c], low, high)):
            part = part.reshape(n, radial)
            packed[pl.ds((k * 3 + c) * n, n), :] = two_terms(part * inner if c == 2 else part)
        if c == 1:
            high_1 = high
    low_2, high_2 = mix(vel[1], kind[1, 1])
    tail = [share[1, 1, :, end, :], low_2[:, end, :], jnp.zeros((8, radial), F32)]
    packed[pl.ds(9 * n, 16), :] = two_terms(jnp.concatenate(tail, axis=0))
    middle[pl.ds(MIDDLE["coefs"], 1), :] = jnp.zeros((1, lanes), F32)
    for start, part in ((0, high_1), (6, low_2), (10, high_2)):
        for a in range(cells):
            middle[pl.ds(MIDDLE["coefs"], 1), pl.ds(128 * (start + a), radial)] = part[a, end:, :]
    spread_all(packed, [spread], radial, dirs)

    @pl.loop(0, lanes // CHUNK, unroll=UNROLL)
    def _(k):
        lane = pl.ds(pl.multiple_of(k * CHUNK, CHUNK), CHUNK)
        block = jnp.dot(left[:, :, :, lane].reshape(3 * n, CHUNK), weights[...], preferred_element_type=F32)
        product[:, :, :, lane] = block.astype(BF16).reshape(3, cells, rows, CHUNK)

    output = pltpu.make_async_copy(product, vel_tan, sems.at[0])
    output.start()

    def sp(k, c, a):
        return spread[pl.ds((k * 3 + c) * n + a * rows, rows), :]

    def speed(c, a):
        return product[c, a].astype(F32)

    def put(name, a, block):
        middle[pl.ds(MIDDLE[name] + a, block.shape[0]), :] = block

    before = None
    for a in range(cells):
        f = field[a]
        here = speed(0, a) * sp(0, 0, a) + sp(1, 0, a) * f
        if a < last:
            here = here + sp(2, 0, a) * field[a + 1]
        change = here if before is None else here - before
        before = here
        speed_x = speed(1, a)
        face = speed_x * sp(0, 1, a) + sp(1, 1, a) * f + sp(2, 1, a) * ahead_x(f, 0.0)
        put("ends", a, face[end:])
        edges[pl.ds(2 * rows + a, 1), :] = face[end:]
        change = change + (face - behind_x(face, 0.0))
        face = speed(2, a) * sp(0, 2, a) + sp(1, 2, a) * f + sp(2, 2, a) * ahead_r(f, dirs)
        change = change + (face - behind_r(face, dirs))
        block = f - change
        partial[a] = block
        put("first", a, f[0:1])
        edges[pl.ds(2 * rows + 4 + a, 1), :] = f[0:1]
        put("partial_first", a, block[0:1])
        put("partial_end", a, block[end:])
        put("low_end", a, spread[pl.ds(9 * n + cells + a, 1), :])
        put("end_fixed", a, speed_x[end:] * spread[pl.ds(9 * n + a, 1), :])
        edges[pl.ds(2 * rows + 8 + a, 1), :] = sp(2, 1, a)[end:]
    edges[pl.ds(0, rows), :] = before
    edges[pl.ds(2 * rows + 12, 4), :] = jnp.zeros((4, lanes), F32)
    edges[pl.ds(2 * rows + 16, rows), :] = field[0]
    edges[pl.ds(rows, rows), :] = sp(2, 0, last)
    for k, x in enumerate((0, end)):
        put("front", k, field[0, pl.ds(x, 1), :])
        put("coef_a", k, sp(2, 0, last)[x:x + 1])
    total = jnp.sum(film[...] * radial_weights(radial), axis=1, keepdims=True)
    row_film[...] = jnp.broadcast_to(total, row_film.shape)
    output.wait()


def step_kernel(
    vel_tan, vel, share, kind, after,
    mixed, fixed,
    product, packed, spread, sems,
):
    del after
    _, cells, rows, lanes = product.shape
    radial = vel.shape[-1]
    dirs = lanes // radial
    n = cells * rows
    inner = wall(radial)
    fetch = pltpu.make_async_copy(vel_tan, product, sems.at[0])
    fetch.start()
    for c in range(3):
        for k, part in enumerate((share[1, c], *mix(vel[c], kind[1, c]))):
            part = part.reshape(n, radial)
            part = two_terms(part * inner if c == 2 else part)
            if k == 0:
                packed[pl.ds(c * n, n), :] = part
                continue
            for a in range(cells):
                row = 3 * n + ((a * 2 + k - 1) * 3 + c) * rows
                packed[pl.ds(row, rows), :] = part[a * rows:(a + 1) * rows]
    for k in range(lanes // CHUNK):
        lane = pl.ds(k * CHUNK, CHUNK)
        ones = spreader(k * CHUNK, CHUNK, radial, dirs)
        mixed[:, lane] = jnp.dot(packed[pl.ds(3 * n, 6 * n), :], ones, preferred_element_type=F32)
        spread[:, lane] = jnp.dot(packed[pl.ds(0, 3 * n), :], ones, preferred_element_type=F32)
    fetch.wait()
    before = None
    for a in range(cells):
        faces = [product[c, a].astype(F32) * spread[pl.ds(c * n + a * rows, rows), :] for c in range(3)]
        change = faces[0] if before is None else faces[0] - before
        before = faces[0]
        change = change + (faces[1] - behind_x(faces[1], 0.0))
        fixed[a] = change + (faces[2] - behind_r(faces[2], dirs))


def gathered_row(msg, row, lane, lanes):
    return jnp.concatenate([msg[pl.ds(row + k, 1), pl.ds(lane, CHUNK)] for k in range(lanes // CHUNK)], axis=1)


def middle_kernel(
    middle, in_e, in_o,
    msg_e, msg_o, film_msg,
):
    cells, rows, lanes = CELLS, (in_e.shape[0] - 8) // 2, in_e.shape[1]
    radial, dirs = RADIAL, lanes // RADIAL
    last, end = cells - 1, rows - 1

    def take(name, count=CELLS, at=0):
        return middle[pl.ds(MIDDLE[name] + at, count), :]

    even = even_az()

    def work(up, down, out_up, out_down):
        at_a = lax.broadcasted_iota(jnp.int32, (cells, 1), 0)
        partial_x = []
        for k, (x, lane, name) in enumerate(((0, AT_FIRST, "partial_first"), (end, AT_END, "partial_end"))):
            face = up[pl.ds(x, 1), :] + gathered_row(up, 2 * rows, lane, lanes) * take("front", 1, k)
            beyond = take("coef_a", 1, k) * down[pl.ds(x, 1), :]
            partial_x.append(take(name) + jnp.where(at_a == 0, face, 0.0) - jnp.where(at_a == last, beyond, 0.0))
        second = take("end_fixed") + take("low_end") * partial_x[1]

        lane = lax.broadcasted_iota(jnp.int32, (1, lanes), 1)
        weight = ((lane // dirs).astype(F32) + 0.5) / radial
        raw = (take("ends") + second) * weight
        film = raw[:, 0:128]
        for k in range(1, lanes // 128):
            film = film + raw[:, 128 * k:128 * k + 128]
        shift = 64
        while shift >= dirs:
            film = film + pltpu.roll(film, shift, 1)
            shift //= 2
        film_msg[...] = jnp.zeros(film_msg.shape, F32)
        film_msg[pl.ds(0, cells), :] = film

        def finish(up_msg, down_msg):
            for msg in (up_msg, down_msg):
                msg[1, pl.ds(2, 2), :] = jnp.zeros((2, lanes), F32)
                for a in range(cells):
                    msg[1, pl.ds(3, 1), pl.ds(128 * a, 128)] = film[a:a + 1]
            up_msg[0] = take("ends")
            up_msg[1, pl.ds(0, 1), :] = gathered_row(up, 2 * rows, AT_ROW_A, lanes)
            up_msg[1, pl.ds(1, 1), :] = gathered_row(down, 2 * rows, AT_ROW_A, lanes)
            up_msg[1, pl.ds(2, 1), :] = take("coefs", 1)
            up_msg[1, pl.ds(2, 1), pl.ds(128 * 4, radial)] = up[pl.ds(2 * rows, 1), pl.ds(AT_COEF, radial)]
            up_msg[1, pl.ds(2, 1), pl.ds(128 * 5, radial)] = down[pl.ds(2 * rows, 1), pl.ds(AT_COEF, radial)]
            up_msg[2] = second
            down_msg[0] = take("first")
            down_msg[1, pl.ds(0, 1), :] = gathered_row(up, 2 * rows, AT_ROW_B, lanes)
            down_msg[1, pl.ds(1, 1), :] = down[pl.ds(0, 1), :]
            down_msg[2] = partial_x[0]

        even_x = lax.rem(lax.axis_index("ax"), 2) == 0

        @pl.when(even_x)
        def _():
            finish(out_up, out_down)

        @pl.when(jnp.logical_not(even_x))
        def _():
            finish(out_down, out_up)

    @pl.when(even)
    def _():
        work(in_o, in_e, msg_e, msg_o)

    @pl.when(jnp.logical_not(even))
    def _():
        work(in_e, in_o, msg_e, msg_o)


def last_kernel(
    mixed, partial, fixed, edges, in_e, in_o, x_o, x_e,
    out,
    packed, spread, up, down, below, above, now, edge, result, sems,
):
    cells, rows, lanes = partial.shape
    radial = packed.shape[1] // 2
    dirs = lanes // radial
    n = cells * rows
    last, end = cells - 1, rows - 1
    even = even_az()
    place = lax.axis_index("ax")
    even_x = lax.rem(place, 2) == 0
    final = lax.axis_size("ax") - 1

    @pl.when(even)
    def _():
        up[...] = in_o[...]
        down[...] = in_e[...]

    @pl.when(jnp.logical_not(even))
    def _():
        up[...] = in_e[...]
        down[...] = in_o[...]

    @pl.when(even_x)
    def _():
        below[...] = jnp.where(place == 0, 0.0, x_o[...])
        above[...] = x_e[...]

    @pl.when(jnp.logical_not(even_x))
    def _():
        below[...] = x_e[...]
        above[...] = jnp.where(place == final, 0.0, x_o[...])

    face_a, coef_a = edges[pl.ds(0, rows), :], edges[pl.ds(rows, rows), :]
    ends, first, coef_x = (edges[pl.ds(2 * rows + 4 * k, cells), :] for k in range(3))

    def joined(msg, lane):
        return jnp.concatenate([msg[pl.ds(2 * rows, 8), pl.ds(lane + 128 * k, radial)] for k in range(rows // 8)], axis=0)

    for k, lane in enumerate((AT_C1, AT_B2, AT_C2)):
        packed[pl.ds(k * rows, rows), :] = two_terms(joined(up, lane))
    singles = [below[1, pl.ds(2, 1), pl.ds(128 * k, radial)] for k in range(14)]
    singles += [msg[pl.ds(2 * rows, 1), pl.ds(AT_COEF, radial)] for msg in (up, down)]
    packed[pl.ds(3 * rows, 16), :] = two_terms(jnp.concatenate(singles, axis=0))
    spread_all(packed, [spread], radial, dirs)
    in_c1, in_b2, in_c2 = (spread[pl.ds(k * rows, rows), :] for k in range(3))
    below_c = spread[pl.ds(3 * rows, 6), :]
    below_b2, below_c2 = spread[pl.ds(3 * rows + 6, 4), :], spread[pl.ds(3 * rows + 10, 4), :]
    own_c = jnp.concatenate([coef_x, spread[pl.ds(3 * rows + 14, 2), :]], axis=0)

    starts = jnp.concatenate([first, gathered_row(up, 2 * rows, AT_ROW_B, lanes), down[pl.ds(0, 1), :]], axis=0)
    enter = jnp.concatenate([below[0], below[1, pl.ds(0, 2), :]], axis=0) + below_c * starts
    leave = own_c * jnp.concatenate([above[0], above[1, pl.ds(0, 2), :]], axis=0)
    crossing = in_c1 * edges[pl.ds(2 * rows + 16, rows), :]
    beyond = coef_a * down[pl.ds(0, rows), :]
    at_x = lax.broadcasted_iota(jnp.int32, (rows, 1), 0)

    def with_edges(block, k):
        return block + jnp.where(at_x == 0, enter[k:k + 1], 0.0) - jnp.where(at_x == end, leave[k:k + 1], 0.0)

    for a in range(cells):
        f = partial[a]
        if a == 0:
            f = f + up[pl.ds(0, rows), :] + crossing
        if a == last:
            f = f - beyond
        now[a] = with_edges(f, a)
    now[cells] = with_edges(down[pl.ds(rows, rows), :] + face_a + beyond, 5)
    lower = up[pl.ds(rows, rows), :] + in_b2 * (
        jnp.where(at_x == 0, enter[4:5], 0.0) - jnp.where(at_x == end, leave[4:5], 0.0) - crossing
    )
    before = lower + in_c2 * now[0]

    first_now = jnp.concatenate([now[a, pl.ds(0, 1), :] for a in range(cells)], axis=0)
    enter_2 = below[2] - below_b2 * (below_c[0:4] * first) + below_c2 * first_now
    inside = jnp.where(place == final, 0.0, 1.0)
    edge[...] = inside * (above[2] + ends + leave[0:4])

    def low(c, a):
        return mixed[pl.ds((a * 6 + c) * rows, rows), :]

    def high(c, a):
        return mixed[pl.ds((a * 6 + 3 + c) * rows, rows), :]

    copies = []
    for a in range(cells):
        f = now[a]
        face = low(0, a) * f + high(0, a) * now[a + 1]
        change = fixed[a] + (face - before)
        before = face
        face = low(1, a) * f + high(1, a) * ahead_x(f, edge[pl.ds(a, 1), :])
        change = change + (face - behind_x(face, enter_2[a:a + 1]))
        face = low(2, a) * f + high(2, a) * ahead_r(f, dirs)
        change = change + (face - behind_r(face, dirs))
        result[a] = f - change
        copies.append(pltpu.make_async_copy(result.at[a], out.at[a], sems.at[a]))
        copies[a].start()

    for copy in copies:
        copy.wait()


def film_kernel(done, row_film, film_own, film_1, x_o, x_e, totals, film_out):
    del done
    cells, share = film_out.shape
    place = lax.axis_index("ax")
    mean = jnp.sum(totals[:, 0:1, :], axis=0) / (cells * totals.shape[0])
    factor = mean / row_film[...]
    for k, source in enumerate((x_o, film_1, x_e, film_own)):

        @pl.when(place == k)
        def _():
            if len(source.shape) == 2:
                film = source[pl.ds(0, cells), :]
            else:
                film = jnp.concatenate([source[1, pl.ds(3, 1), pl.ds(128 * a, 128)] for a in range(cells)], axis=0)
            film_out[...] = (film * factor)[:, k * share:(k + 1) * share]


def swap(value, axis, pairing):
    count = lax.axis_size(axis)
    if axis == "ax":
        other = [i ^ pairing for i in range(count)]
    elif pairing == 0:
        other = [i ^ 1 for i in range(count)]
    else:
        other = [(i - 1 if i % 2 == 0 else i + 1) % count for i in range(count)]
    return lax.ppermute(value, axis, list(enumerate(other)))


def pinned(value, space):
    return pltpu.with_memory_space_constraint(value, space)


def placed(space, shape, dtype):
    return space(shape, dtype)


def call(kernel, args, outs, scratch, in_hbm=0, out_hbm=0, free=0, sems=0, cost=None):
    vmem, hbm = pl.BlockSpec(memory_space=pltpu.VMEM), pl.BlockSpec(memory_space=pl.ANY)
    shapes = [pltpu.VMEM(shape, dtype) for shape, dtype in scratch]
    pinned_outs = len(outs) - free
    shapes_out = [placed(pltpu.HBM if i < out_hbm else pltpu.VMEM, *out) for i, out in enumerate(outs[:pinned_outs])]
    shapes_out += [jax.ShapeDtypeStruct(*out) for out in outs[pinned_outs:]]
    args = [pinned(arg, pltpu.HBM if i < in_hbm else pltpu.VMEM) for i, arg in enumerate(args)]
    if sems:
        shapes.append(pltpu.SemaphoreType.DMA((sems,)))
    return pl.pallas_call(
        kernel,
        out_shape=shapes_out,
        in_specs=[hbm] * in_hbm + [vmem] * (len(args) - in_hbm),
        out_specs=[hbm] * out_hbm + [vmem] * (len(outs) - out_hbm),
        scratch_shapes=shapes,
        compiler_params=pltpu.CompilerParams(vmem_limit_bytes=32 * 2**20),
        cost_estimate=cost,
        name=kernel.__name__,
    )(*args)


def local(tangent, velocity, face_frac, branch, basis, design, exit_film):
    cells, rows, lanes = tangent.shape
    radial = velocity.shape[-1]
    dirs = design.shape[1]
    n = cells * rows
    devices = lax.axis_size("az")
    layer, cell_layer = (rows, lanes), (rows, radial)
    z_msg, x_msg, line = (2 * rows + 8, lanes), (3, cells, lanes), (cells, lanes)
    inputs = (tangent, velocity, face_frac, branch, basis, design, exit_film)
    count = (3 * len(EDGE) + 2) * rows
    kept = [(value.shape, value.dtype) for value in inputs]
    kept[5] = ((CHUNK, CHUNK), BF16)
    z_e, z_o, sums, field, vel, share, kind, left, weights, film_in = call(
        edge_kernel,
        inputs,
        [(z_msg, F32), (z_msg, F32), ((devices, 2, 128), F32)] + kept,
        [
            (design.shape, BF16), ((len(EDGE) * rows, lanes), BF16), ((count, 2 * radial), BF16), ((count, lanes), F32), (layer, F32),
            ((2, lanes), F32), ((2, *layer), F32), ((2, *layer), F32), (layer, F32),
        ],
        in_hbm=7,
        sems=24,
    )
    in_e, in_o = swap(z_e, "az", 0), swap(z_o, "az", 1)
    totals = lax.all_to_all(sums, "az", 0, 0)
    velocity_tangent, middle, partial, edges, row_film = call(
        local_kernel,
        (field, vel, share, kind, left, weights, film_in),
        [
            (basis.shape, BF16), ((32, lanes), F32), (tangent.shape, F32), ((3 * rows + 16, lanes), F32),
            ((cells, 128), F32),
        ],
        [(basis.shape, BF16), ((9 * n + 16, 2 * radial), BF16), ((9 * n + 16, lanes), F32)],
        out_hbm=1,
        sems=1,
        cost=pl.CostEstimate(flops=10**9, bytes_accessed=10 * 10**6, transcendentals=0),
    )
    x_e, x_o, film = call(
        middle_kernel, (middle, in_e, in_o), [(x_msg, F32), (x_msg, F32), ((8, 128), F32)], []
    )
    from_o, from_e, film_1 = swap(x_o, "ax", 3), swap(x_e, "ax", 1), swap(film, "ax", 2)
    coef_2, fixed = call(
        step_kernel,
        (velocity_tangent, vel, share, kind, film),
        [((6 * n, lanes), F32), (tangent.shape, F32)],
        [(basis.shape, BF16), ((9 * n, 2 * radial), BF16), ((3 * n, lanes), F32)],
        in_hbm=1,
        sems=1,
        cost=pl.CostEstimate(flops=10**9, bytes_accessed=10 * 10**6, transcendentals=0),
    )
    count = 3 * rows + 16
    (out,) = call(
        last_kernel,
        (coef_2, partial, fixed, edges, in_e, in_o, from_o, from_e),
        [(tangent.shape, F32)],
        [
            ((count, 2 * radial), BF16), ((count, lanes), F32), (z_msg, F32), (z_msg, F32), (x_msg, F32), (x_msg, F32),
            ((cells + 1, *layer), F32), (line, F32), (tangent.shape, F32),
        ],
        out_hbm=1,
        sems=cells,
    )
    (film_out,) = call(
        film_kernel,
        (out, row_film, film, film_1, from_o, from_e, totals),
        [((cells, dirs // lax.axis_size("ax")), F32)],
        [],
        in_hbm=1,
        free=1,
    )
    return out, velocity_tangent, film_out


def solution(mesh):
    in_specs = (
        P("az", "ax", None),
        P(None, "az", "ax", None),
        P(None, None, "az", "ax", None),
        P(None, None, "az", "ax", None),
        P(None, "az", "ax", None),
        P(),
        P("az", None),
    )
    out_specs = (P("az", "ax", None), P(None, "az", "ax", None), P("az", "ax"))
    return jax.shard_map(local, mesh=mesh, in_specs=in_specs, out_specs=out_specs, check_vma=False)
```

```python
import jax
import jax.numpy as jnp
from jax import lax
from jax.experimental import pallas as pl
from jax.experimental.pallas import tpu as pltpu
from jax.sharding import PartitionSpec as P

F32, BF16 = jnp.float32, jnp.bfloat16
CHUNK = 256
RADIAL = 64
CELLS = 4
UNROLL = 8
AT_C1, AT_B2, AT_C2, AT_ROW_A, AT_ROW_B, AT_COEF, AT_FIRST, AT_END = 0, 256, 512, 768, 1024, 1280, 1408, 1664


def mix(speed, branch):
    part = speed * (0.25 * branch.astype(F32))
    rest = speed - part
    ahead = speed > 0
    return jnp.where(ahead, rest, part), jnp.where(ahead, part, rest)


def two_terms(values):
    high = values.astype(BF16)
    low = (values - high.astype(F32)).astype(BF16)
    return jnp.concatenate([high, low], axis=-1)


def spreader(offset, lanes, radial, dirs):
    row = lax.broadcasted_iota(jnp.int32, (2 * radial, lanes), 0)
    lane = lax.broadcasted_iota(jnp.int32, (2 * radial, lanes), 1) + offset
    shift = dirs.bit_length() - 1
    return jnp.where((row & (radial - 1)) == (lane >> shift), 1.0, 0.0).astype(BF16)


def spread_all(packed, outs, radial, dirs):
    lanes = outs[0].shape[1]

    @pl.loop(0, lanes // CHUNK, unroll=UNROLL)
    def _(k):
        at = pl.multiple_of(k * CHUNK, CHUNK)
        ones = spreader(at, CHUNK, radial, dirs)
        row = 0
        for out in outs:
            count = out.shape[0]
            left = packed[pl.ds(row, count), :]
            out[:, pl.ds(at, CHUNK)] = jnp.dot(left, ones, preferred_element_type=F32)
            row += count


def blocks_of(design):
    dirs = design.shape[1]
    row = lax.broadcasted_iota(jnp.int32, (CHUNK, dirs), 0)
    col = lax.broadcasted_iota(jnp.int32, (CHUNK, dirs), 1)
    pick = jnp.where((row & (dirs - 1)) == col, 1.0, 0.0).astype(BF16)
    tiled = jnp.dot(pick, design, preferred_element_type=F32).astype(BF16)
    tiled = lax.dot_general(tiled, pick, (((1,), (1,)), ((), ())), preferred_element_type=F32)
    row = lax.broadcasted_iota(jnp.int32, (CHUNK, CHUNK), 0)
    col = lax.broadcasted_iota(jnp.int32, (CHUNK, CHUNK), 1)
    shift = dirs.bit_length() - 1
    return jnp.where((row >> shift) == (col >> shift), tiled, 0.0).astype(BF16)


def wall(radial):
    lane = lax.broadcasted_iota(jnp.int32, (1, radial), 1)
    return jnp.where(lane < radial - 1, 1.0, 0.0)


def ahead_x(rows, last):
    n = rows.shape[0]
    at = lax.broadcasted_iota(jnp.int32, rows.shape, 0)
    return jnp.where(at == n - 1, last, pltpu.roll(rows, n - 1, 0))


def behind_x(rows, first):
    at = lax.broadcasted_iota(jnp.int32, rows.shape, 0)
    return jnp.where(at == 0, first, pltpu.roll(rows, 1, 0))


def ahead_r(rows, dirs):
    return pltpu.roll(rows, rows.shape[1] - dirs, 1)


def behind_r(rows, dirs):
    return pltpu.roll(rows, dirs, 1)


def even_az():
    return lax.rem(lax.axis_index("az"), 2) == 0


def radial_weights(radial):
    return (lax.broadcasted_iota(jnp.int32, (1, radial), 1).astype(F32) + 0.5) / radial


EDGE = ((0, 0), (0, 2), (0, 3), (1, 0), (1, 3), (2, 0), (2, 3))


def edge_kernel(
    tangent, velocity, frac, branch, basis, design, exit_film,
    msg_e, msg_o, sums, field, vel, share, kind, left, weights, film,
    mat, vel_tan, packed, spread, work, ends, edge, faces, face_a, sems,
):
    cells, rows, lanes = field.shape
    radial = vel.shape[-1]
    dirs = lanes // radial
    last, end = cells - 1, rows - 1
    inner = wall(radial)
    pairs = [
        (exit_film, film), (design, mat), (velocity, vel), (branch, kind), (frac, share), (basis, left), (tangent, field),
    ]
    copies = [pltpu.make_async_copy(src, dst, sems.at[i]) for i, (src, dst) in enumerate(pairs)]
    for copy in copies:
        copy.start()
    copies[0].wait()
    sums[...] = jnp.full(sums.shape, jnp.sum(film[...] * radial_weights(radial)), F32)
    copies[1].wait()
    weights[...] = blocks_of(mat[...])
    for copy in copies[2:5]:
        copy.wait()

    at = {}
    row = 0
    for c, a in EDGE:
        low, high = mix(vel[c, a], kind[0, c, a])
        if (c, a) == (0, last):
            high_a = high
        if c == 1:
            at["high", a] = high
        for name, part in zip("plh", (share[0, c, a], low, high), strict=True):
            packed[pl.ds(row, rows), :] = two_terms(part * inner if c == 2 else part)
            at[name, c, a] = row
            row += rows
    low_2, high_2 = mix(vel[0, last], kind[1, 0, last])
    for name, part in zip("pl", (share[1, 0, last], low_2), strict=True):
        packed[pl.ds(row, rows), :] = two_terms(part)
        at[name] = row
        row += rows
    spread_all(packed, [spread], radial, dirs)

    for copy in copies[5:]:
        copy.wait()

    @pl.loop(0, lanes // CHUNK, unroll=UNROLL)
    def _(k):
        lane = pl.ds(pl.multiple_of(k * CHUNK, CHUNK), CHUNK)
        part = jnp.concatenate([left[c, a, :, lane] for c, a in EDGE], axis=0)
        vel_tan[:, lane] = jnp.dot(part, weights[...], preferred_element_type=F32).astype(BF16)

    def sp(*key):
        return spread[pl.ds(at[key], rows), :]

    def speed(c, a):
        return vel_tan[pl.ds(EDGE.index((c, a)) * rows, rows), :].astype(F32)

    def along_az(a):
        f = field[a]
        face = speed(0, a) * sp("p", 0, a) + sp("l", 0, a) * f
        return face if a == last else face + sp("h", 0, a) * field[a + 1]

    faces[0] = along_az(0)
    faces[1] = along_az(last - 1)
    face_a[...] = along_az(last)
    for i, a in enumerate((0, last)):
        f = field[a]
        change = faces[0] if a == 0 else face_a[...] - faces[1]
        face = speed(1, a) * sp("p", 1, a) + sp("l", 1, a) * f + sp("h", 1, a) * ahead_x(f, 0.0)
        ends[pl.ds(i, 1), :] = face[end:, :]
        change = change + (face - behind_x(face, 0.0))
        face = speed(2, a) * sp("p", 2, a) + sp("l", 2, a) * f + sp("h", 2, a) * ahead_r(f, dirs)
        change = change + (face - behind_r(face, dirs))
        edge[i] = f - change
    work[...] = speed(0, last) * spread[pl.ds(at["p"], rows), :] + spread[pl.ds(at["l"], rows), :] * edge[1]

    def small_rows(msg, lane, block):
        for k in range(lanes // CHUNK):
            msg[pl.ds(2 * rows + k, 1), pl.ds(lane, CHUNK)] = block[:, k * CHUNK:(k + 1) * CHUNK]

    def halves(msg, lane, block):
        for k in range(rows // 8):
            msg[pl.ds(2 * rows, 8), pl.ds(lane + 128 * k, radial)] = block[8 * k:8 * k + 8]

    def fill(up_msg, down_msg):
        for msg in (up_msg, down_msg):
            msg[pl.ds(2 * rows, 8), :] = jnp.zeros((8, lanes), F32)
        up_msg[pl.ds(0, rows), :] = face_a[...]
        up_msg[pl.ds(rows, rows), :] = work[...]
        halves(up_msg, AT_C1, high_a)
        halves(up_msg, AT_B2, low_2)
        halves(up_msg, AT_C2, high_2)
        small_rows(up_msg, AT_ROW_A, ends[pl.ds(1, 1), :])
        small_rows(up_msg, AT_ROW_B, field[last, pl.ds(0, 1), :])
        small_rows(up_msg, AT_FIRST, sp("h", 0, last)[0:1])
        small_rows(up_msg, AT_END, sp("h", 0, last)[end:])
        up_msg[pl.ds(2 * rows, 1), pl.ds(AT_COEF, radial)] = at["high", last][end:, :]
        down_msg[pl.ds(0, rows), :] = field[0]
        down_msg[pl.ds(rows, rows), :] = edge[0]
        small_rows(down_msg, AT_ROW_A, ends[pl.ds(0, 1), :])
        down_msg[pl.ds(2 * rows, 1), pl.ds(AT_COEF, radial)] = at["high", 0][end:, :]

    even = even_az()

    @pl.when(even)
    def _():
        fill(msg_e, msg_o)

    @pl.when(jnp.logical_not(even))
    def _():
        fill(msg_o, msg_e)


MIDDLE = dict(
    ends=0, end_fixed=4, low_end=8, first=12, partial_first=16, partial_end=20, front=24, coef_a=26, coefs=28
)


def local_kernel(
    field, vel, share, kind, left, weights, film,
    vel_tan, middle, partial, edges, row_film,
    product, packed, spread, sems,
):
    cells, rows, lanes = field.shape
    radial = vel.shape[-1]
    dirs = lanes // radial
    n = cells * rows
    last, end = cells - 1, rows - 1
    inner = wall(radial)
    for c in range(3):
        low, high = mix(vel[c], kind[0, c])
        for k, part in enumerate((share[0, c], low, high)):
            part = part.reshape(n, radial)
            packed[pl.ds((k * 3 + c) * n, n), :] = two_terms(part * inner if c == 2 else part)
        if c == 1:
            high_1 = high
    low_2, high_2 = mix(vel[1], kind[1, 1])
    tail = [share[1, 1, :, end, :], low_2[:, end, :], jnp.zeros((8, radial), F32)]
    packed[pl.ds(9 * n, 16), :] = two_terms(jnp.concatenate(tail, axis=0))
    middle[pl.ds(MIDDLE["coefs"], 1), :] = jnp.zeros((1, lanes), F32)
    for start, part in ((0, high_1), (6, low_2), (10, high_2)):
        for a in range(cells):
            middle[pl.ds(MIDDLE["coefs"], 1), pl.ds(128 * (start + a), radial)] = part[a, end:, :]
    spread_all(packed, [spread], radial, dirs)

    @pl.loop(0, lanes // CHUNK, unroll=UNROLL)
    def _(k):
        lane = pl.ds(pl.multiple_of(k * CHUNK, CHUNK), CHUNK)
        block = jnp.dot(left[:, :, :, lane].reshape(3 * n, CHUNK), weights[...], preferred_element_type=F32)
        product[:, :, :, lane] = block.astype(BF16).reshape(3, cells, rows, CHUNK)

    output = pltpu.make_async_copy(product, vel_tan, sems.at[0])
    output.start()

    def sp(k, c, a):
        return spread[pl.ds((k * 3 + c) * n + a * rows, rows), :]

    def speed(c, a):
        return product[c, a].astype(F32)

    def put(name, a, block):
        middle[pl.ds(MIDDLE[name] + a, block.shape[0]), :] = block

    before = None
    for a in range(cells):
        f = field[a]
        here = speed(0, a) * sp(0, 0, a) + sp(1, 0, a) * f
        if a < last:
            here = here + sp(2, 0, a) * field[a + 1]
        change = here if before is None else here - before
        before = here
        speed_x = speed(1, a)
        face = speed_x * sp(0, 1, a) + sp(1, 1, a) * f + sp(2, 1, a) * ahead_x(f, 0.0)
        put("ends", a, face[end:])
        edges[pl.ds(2 * rows + a, 1), :] = face[end:]
        change = change + (face - behind_x(face, 0.0))
        face = speed(2, a) * sp(0, 2, a) + sp(1, 2, a) * f + sp(2, 2, a) * ahead_r(f, dirs)
        change = change + (face - behind_r(face, dirs))
        block = f - change
        partial[a] = block
        put("first", a, f[0:1])
        edges[pl.ds(2 * rows + 4 + a, 1), :] = f[0:1]
        put("partial_first", a, block[0:1])
        put("partial_end", a, block[end:])
        put("low_end", a, spread[pl.ds(9 * n + cells + a, 1), :])
        put("end_fixed", a, speed_x[end:] * spread[pl.ds(9 * n + a, 1), :])
        edges[pl.ds(2 * rows + 8 + a, 1), :] = sp(2, 1, a)[end:]
    edges[pl.ds(0, rows), :] = before
    edges[pl.ds(2 * rows + 12, 4), :] = jnp.zeros((4, lanes), F32)
    edges[pl.ds(2 * rows + 16, rows), :] = field[0]
    edges[pl.ds(rows, rows), :] = sp(2, 0, last)
    for k, x in enumerate((0, end)):
        put("front", k, field[0, pl.ds(x, 1), :])
        put("coef_a", k, sp(2, 0, last)[x:x + 1])
    total = jnp.sum(film[...] * radial_weights(radial), axis=1, keepdims=True)
    row_film[...] = jnp.broadcast_to(total, row_film.shape)
    output.wait()


def step_kernel(
    vel_tan, vel, share, kind, after,
    mixed, fixed,
    product, packed, spread, sems,
):
    del after
    _, cells, rows, lanes = product.shape
    radial = vel.shape[-1]
    dirs = lanes // radial
    n = cells * rows
    inner = wall(radial)
    fetch = pltpu.make_async_copy(vel_tan, product, sems.at[0])
    fetch.start()
    for c in range(3):
        for k, part in enumerate((share[1, c], *mix(vel[c], kind[1, c]))):
            part = part.reshape(n, radial)
            part = two_terms(part * inner if c == 2 else part)
            if k == 0:
                packed[pl.ds(c * n, n), :] = part
                continue
            for a in range(cells):
                row = 3 * n + ((a * 2 + k - 1) * 3 + c) * rows
                packed[pl.ds(row, rows), :] = part[a * rows:(a + 1) * rows]
    for k in range(lanes // CHUNK):
        lane = pl.ds(k * CHUNK, CHUNK)
        ones = spreader(k * CHUNK, CHUNK, radial, dirs)
        mixed[:, lane] = jnp.dot(packed[pl.ds(3 * n, 6 * n), :], ones, preferred_element_type=F32)
        spread[:, lane] = jnp.dot(packed[pl.ds(0, 3 * n), :], ones, preferred_element_type=F32)
    fetch.wait()
    before = None
    for a in range(cells):
        faces = [product[c, a].astype(F32) * spread[pl.ds(c * n + a * rows, rows), :] for c in range(3)]
        change = faces[0] if before is None else faces[0] - before
        before = faces[0]
        change = change + (faces[1] - behind_x(faces[1], 0.0))
        fixed[a] = change + (faces[2] - behind_r(faces[2], dirs))


def gathered_row(msg, row, lane, lanes):
    return jnp.concatenate([msg[pl.ds(row + k, 1), pl.ds(lane, CHUNK)] for k in range(lanes // CHUNK)], axis=1)


def middle_kernel(
    middle, in_e, in_o,
    msg_e, msg_o, film_msg,
):
    cells, rows, lanes = CELLS, (in_e.shape[0] - 8) // 2, in_e.shape[1]
    radial, dirs = RADIAL, lanes // RADIAL
    last, end = cells - 1, rows - 1

    def take(name, count=CELLS, at=0):
        return middle[pl.ds(MIDDLE[name] + at, count), :]

    even = even_az()

    def work(up, down, out_up, out_down):
        at_a = lax.broadcasted_iota(jnp.int32, (cells, 1), 0)
        partial_x = []
        for k, (x, lane, name) in enumerate(((0, AT_FIRST, "partial_first"), (end, AT_END, "partial_end"))):
            face = up[pl.ds(x, 1), :] + gathered_row(up, 2 * rows, lane, lanes) * take("front", 1, k)
            beyond = take("coef_a", 1, k) * down[pl.ds(x, 1), :]
            partial_x.append(take(name) + jnp.where(at_a == 0, face, 0.0) - jnp.where(at_a == last, beyond, 0.0))
        second = take("end_fixed") + take("low_end") * partial_x[1]

        lane = lax.broadcasted_iota(jnp.int32, (1, lanes), 1)
        weight = ((lane // dirs).astype(F32) + 0.5) / radial
        raw = (take("ends") + second) * weight
        film = raw[:, 0:128]
        for k in range(1, lanes // 128):
            film = film + raw[:, 128 * k:128 * k + 128]
        shift = 64
        while shift >= dirs:
            film = film + pltpu.roll(film, shift, 1)
            shift //= 2
        film_msg[...] = jnp.zeros(film_msg.shape, F32)
        film_msg[pl.ds(0, cells), :] = film

        def finish(up_msg, down_msg):
            for msg in (up_msg, down_msg):
                msg[1, pl.ds(2, 2), :] = jnp.zeros((2, lanes), F32)
                for a in range(cells):
                    msg[1, pl.ds(3, 1), pl.ds(128 * a, 128)] = film[a:a + 1]
            up_msg[0] = take("ends")
            up_msg[1, pl.ds(0, 1), :] = gathered_row(up, 2 * rows, AT_ROW_A, lanes)
            up_msg[1, pl.ds(1, 1), :] = gathered_row(down, 2 * rows, AT_ROW_A, lanes)
            up_msg[1, pl.ds(2, 1), :] = take("coefs", 1)
            up_msg[1, pl.ds(2, 1), pl.ds(128 * 4, radial)] = up[pl.ds(2 * rows, 1), pl.ds(AT_COEF, radial)]
            up_msg[1, pl.ds(2, 1), pl.ds(128 * 5, radial)] = down[pl.ds(2 * rows, 1), pl.ds(AT_COEF, radial)]
            up_msg[2] = second
            down_msg[0] = take("first")
            down_msg[1, pl.ds(0, 1), :] = gathered_row(up, 2 * rows, AT_ROW_B, lanes)
            down_msg[1, pl.ds(1, 1), :] = down[pl.ds(0, 1), :]
            down_msg[2] = partial_x[0]

        even_x = lax.rem(lax.axis_index("ax"), 2) == 0

        @pl.when(even_x)
        def _():
            finish(out_up, out_down)

        @pl.when(jnp.logical_not(even_x))
        def _():
            finish(out_down, out_up)

    @pl.when(even)
    def _():
        work(in_o, in_e, msg_e, msg_o)

    @pl.when(jnp.logical_not(even))
    def _():
        work(in_e, in_o, msg_e, msg_o)


def last_kernel(
    mixed, partial, fixed, edges, in_e, in_o, x_o, x_e,
    out,
    packed, spread, up, down, below, above, now, edge, result, sems,
):
    cells, rows, lanes = partial.shape
    radial = packed.shape[1] // 2
    dirs = lanes // radial
    n = cells * rows
    last, end = cells - 1, rows - 1
    even = even_az()
    place = lax.axis_index("ax")
    even_x = lax.rem(place, 2) == 0
    final = lax.axis_size("ax") - 1

    @pl.when(even)
    def _():
        up[...] = in_o[...]
        down[...] = in_e[...]

    @pl.when(jnp.logical_not(even))
    def _():
        up[...] = in_e[...]
        down[...] = in_o[...]

    @pl.when(even_x)
    def _():
        below[...] = jnp.where(place == 0, 0.0, x_o[...])
        above[...] = x_e[...]

    @pl.when(jnp.logical_not(even_x))
    def _():
        below[...] = x_e[...]
        above[...] = jnp.where(place == final, 0.0, x_o[...])

    face_a, coef_a = edges[pl.ds(0, rows), :], edges[pl.ds(rows, rows), :]
    ends, first, coef_x = (edges[pl.ds(2 * rows + 4 * k, cells), :] for k in range(3))

    def joined(msg, lane):
        return jnp.concatenate([msg[pl.ds(2 * rows, 8), pl.ds(lane + 128 * k, radial)] for k in range(rows // 8)], axis=0)

    for k, lane in enumerate((AT_C1, AT_B2, AT_C2)):
        packed[pl.ds(k * rows, rows), :] = two_terms(joined(up, lane))
    singles = [below[1, pl.ds(2, 1), pl.ds(128 * k, radial)] for k in range(14)]
    singles += [msg[pl.ds(2 * rows, 1), pl.ds(AT_COEF, radial)] for msg in (up, down)]
    packed[pl.ds(3 * rows, 16), :] = two_terms(jnp.concatenate(singles, axis=0))
    spread_all(packed, [spread], radial, dirs)
    in_c1, in_b2, in_c2 = (spread[pl.ds(k * rows, rows), :] for k in range(3))
    below_c = spread[pl.ds(3 * rows, 6), :]
    below_b2, below_c2 = spread[pl.ds(3 * rows + 6, 4), :], spread[pl.ds(3 * rows + 10, 4), :]
    own_c = jnp.concatenate([coef_x, spread[pl.ds(3 * rows + 14, 2), :]], axis=0)

    starts = jnp.concatenate([first, gathered_row(up, 2 * rows, AT_ROW_B, lanes), down[pl.ds(0, 1), :]], axis=0)
    enter = jnp.concatenate([below[0], below[1, pl.ds(0, 2), :]], axis=0) + below_c * starts
    leave = own_c * jnp.concatenate([above[0], above[1, pl.ds(0, 2), :]], axis=0)
    crossing = in_c1 * edges[pl.ds(2 * rows + 16, rows), :]
    beyond = coef_a * down[pl.ds(0, rows), :]
    at_x = lax.broadcasted_iota(jnp.int32, (rows, 1), 0)

    def with_edges(block, k):
        return block + jnp.where(at_x == 0, enter[k:k + 1], 0.0) - jnp.where(at_x == end, leave[k:k + 1], 0.0)

    for a in range(cells):
        f = partial[a]
        if a == 0:
            f = f + up[pl.ds(0, rows), :] + crossing
        if a == last:
            f = f - beyond
        now[a] = with_edges(f, a)
    now[cells] = with_edges(down[pl.ds(rows, rows), :] + face_a + beyond, 5)
    lower = up[pl.ds(rows, rows), :] + in_b2 * (
        jnp.where(at_x == 0, enter[4:5], 0.0) - jnp.where(at_x == end, leave[4:5], 0.0) - crossing
    )
    before = lower + in_c2 * now[0]

    first_now = jnp.concatenate([now[a, pl.ds(0, 1), :] for a in range(cells)], axis=0)
    enter_2 = below[2] - below_b2 * (below_c[0:4] * first) + below_c2 * first_now
    inside = jnp.where(place == final, 0.0, 1.0)
    edge[...] = inside * (above[2] + ends + leave[0:4])

    def low(c, a):
        return mixed[pl.ds((a * 6 + c) * rows, rows), :]

    def high(c, a):
        return mixed[pl.ds((a * 6 + 3 + c) * rows, rows), :]

    copies = []
    for a in range(cells):
        f = now[a]
        face = low(0, a) * f + high(0, a) * now[a + 1]
        change = fixed[a] + (face - before)
        before = face
        face = low(1, a) * f + high(1, a) * ahead_x(f, edge[pl.ds(a, 1), :])
        change = change + (face - behind_x(face, enter_2[a:a + 1]))
        face = low(2, a) * f + high(2, a) * ahead_r(f, dirs)
        change = change + (face - behind_r(face, dirs))
        result[a] = f - change
        copies.append(pltpu.make_async_copy(result.at[a], out.at[a], sems.at[a]))
        copies[a].start()

    for copy in copies:
        copy.wait()


def film_kernel(done, row_film, film_own, film_1, x_o, x_e, totals, film_out):
    del done
    cells, share = film_out.shape
    place = lax.axis_index("ax")
    mean = jnp.sum(totals[:, 0:1, :], axis=0) / (cells * totals.shape[0])
    factor = mean / row_film[...]
    for k, source in enumerate((x_o, film_1, x_e, film_own)):

        @pl.when(place == k)
        def _():
            if len(source.shape) == 2:
                film = source[pl.ds(0, cells), :]
            else:
                film = jnp.concatenate([source[1, pl.ds(3, 1), pl.ds(128 * a, 128)] for a in range(cells)], axis=0)
            film_out[...] = (film * factor)[:, k * share:(k + 1) * share]


def swap(value, axis, pairing):
    count = lax.axis_size(axis)
    if axis == "ax":
        other = [i ^ pairing for i in range(count)]
    elif pairing == 0:
        other = [i ^ 1 for i in range(count)]
    else:
        other = [(i - 1 if i % 2 == 0 else i + 1) % count for i in range(count)]
    return lax.ppermute(value, axis, list(enumerate(other)))


def pinned(value, space):
    return pltpu.with_memory_space_constraint(value, space)


def placed(space, shape, dtype):
    return space(shape, dtype)


def call(kernel, args, outs, scratch, in_hbm=0, out_hbm=0, free=0, sems=0, cost=None):
    vmem, hbm = pl.BlockSpec(memory_space=pltpu.VMEM), pl.BlockSpec(memory_space=pl.ANY)
    shapes = [pltpu.VMEM(shape, dtype) for shape, dtype in scratch]
    pinned_outs = len(outs) - free
    shapes_out = [placed(pltpu.HBM if i < out_hbm else pltpu.VMEM, *out) for i, out in enumerate(outs[:pinned_outs])]
    shapes_out += [jax.ShapeDtypeStruct(*out) for out in outs[pinned_outs:]]
    args = [pinned(arg, pltpu.HBM if i < in_hbm else pltpu.VMEM) for i, arg in enumerate(args)]
    if sems:
        shapes.append(pltpu.SemaphoreType.DMA((sems,)))
    return pl.pallas_call(
        kernel,
        out_shape=shapes_out,
        in_specs=[hbm] * in_hbm + [vmem] * (len(args) - in_hbm),
        out_specs=[hbm] * out_hbm + [vmem] * (len(outs) - out_hbm),
        scratch_shapes=shapes,
        compiler_params=pltpu.CompilerParams(vmem_limit_bytes=32 * 2**20),
        cost_estimate=cost,
        name=kernel.__name__,
    )(*args)


def local(tangent, velocity, face_frac, branch, basis, design, exit_film):
    cells, rows, lanes = tangent.shape
    radial = velocity.shape[-1]
    dirs = design.shape[1]
    n = cells * rows
    devices = lax.axis_size("az")
    layer, cell_layer = (rows, lanes), (rows, radial)
    z_msg, x_msg, line = (2 * rows + 8, lanes), (3, cells, lanes), (cells, lanes)
    inputs = (tangent, velocity, face_frac, branch, basis, design, exit_film)
    count = (3 * len(EDGE) + 2) * rows
    kept = [(value.shape, value.dtype) for value in inputs]
    kept[5] = ((CHUNK, CHUNK), BF16)
    z_e, z_o, sums, field, vel, share, kind, left, weights, film_in = call(
        edge_kernel,
        inputs,
        [(z_msg, F32), (z_msg, F32), ((devices, 2, 128), F32)] + kept,
        [
            (design.shape, BF16), ((len(EDGE) * rows, lanes), BF16), ((count, 2 * radial), BF16), ((count, lanes), F32), (layer, F32),
            ((2, lanes), F32), ((2, *layer), F32), ((2, *layer), F32), (layer, F32),
        ],
        in_hbm=7,
        sems=7,
    )
    in_e, in_o = swap(z_e, "az", 0), swap(z_o, "az", 1)
    totals = lax.all_to_all(sums, "az", 0, 0)
    velocity_tangent, middle, partial, edges, row_film = call(
        local_kernel,
        (field, vel, share, kind, left, weights, film_in),
        [
            (basis.shape, BF16), ((32, lanes), F32), (tangent.shape, F32), ((3 * rows + 16, lanes), F32),
            ((cells, 128), F32),
        ],
        [(basis.shape, BF16), ((9 * n + 16, 2 * radial), BF16), ((9 * n + 16, lanes), F32)],
        out_hbm=1,
        sems=1,
        cost=pl.CostEstimate(flops=10**9, bytes_accessed=10 * 10**6, transcendentals=0),
    )
    x_e, x_o, film = call(
        middle_kernel, (middle, in_e, in_o), [(x_msg, F32), (x_msg, F32), ((8, 128), F32)], []
    )
    from_o, from_e, film_1 = swap(x_o, "ax", 3), swap(x_e, "ax", 1), swap(film, "ax", 2)
    coef_2, fixed = call(
        step_kernel,
        (velocity_tangent, vel, share, kind, film),
        [((6 * n, lanes), F32), (tangent.shape, F32)],
        [(basis.shape, BF16), ((9 * n, 2 * radial), BF16), ((3 * n, lanes), F32)],
        in_hbm=1,
        sems=1,
        cost=pl.CostEstimate(flops=10**9, bytes_accessed=10 * 10**6, transcendentals=0),
    )
    count = 3 * rows + 16
    (out,) = call(
        last_kernel,
        (coef_2, partial, fixed, edges, in_e, in_o, from_o, from_e),
        [(tangent.shape, F32)],
        [
            ((count, 2 * radial), BF16), ((count, lanes), F32), (z_msg, F32), (z_msg, F32), (x_msg, F32), (x_msg, F32),
            ((cells + 1, *layer), F32), (line, F32), (tangent.shape, F32),
        ],
        out_hbm=1,
        sems=cells,
    )
    (film_out,) = call(
        film_kernel,
        (out, row_film, film, film_1, from_o, from_e, totals),
        [((cells, dirs // lax.axis_size("ax")), F32)],
        [],
        in_hbm=1,
        free=1,
    )
    return out, velocity_tangent, film_out


def solution(mesh):
    in_specs = (
        P("az", "ax", None),
        P(None, "az", "ax", None),
        P(None, None, "az", "ax", None),
        P(None, None, "az", "ax", None),
        P(None, "az", "ax", None),
        P(),
        P("az", None),
    )
    out_specs = (P("az", "ax", None), P(None, "az", "ax", None), P("az", "ax"))
    return jax.shard_map(local, mesh=mesh, in_specs=in_specs, out_specs=out_specs, check_vma=False)
```
